32 devices in a mesh: grp: 4 (over z), tp: 8 (over y, x, core).
Axes of the slice: x: 2, y: 2, z: 4, core: 2. Of those that a mesh axis runs over, the one named last changes fastest.
Arguments:
- inputs: bfloat16 [15360, 8192], P('grp', 'tp'), may hold values from -6 to 6
- cotangent: bfloat16 [15360, 8192], P('grp', 'tp'), may hold values from -0.059814453 to 0.059814453
- factor_a: bfloat16 [16, 8192, 128], P('grp', 'tp'), may hold values from -0.0625 to 0.0625
- factor_b: bfloat16 [16, 128, 8192], P('grp', None, 'tp'), may hold values from -0.5 to 0.5
- adapter_slot: int32 [16], replicated, may hold values from 0 to 15, as said below
- seg_adapter: int32 [4, 30], replicated, may hold values from 0 to 15, as said below
Outputs:
- factor_a_grad: bfloat16 [16, 8192, 128], P('grp', 'tp')
- factor_b_grad: bfloat16 [16, 128, 8192], P('grp', None, 'tp')
The draws below stay inside these ranges and needn't reach their ends.
Inputs may be any that keep to these rules, and one draw needn't show every extreme that they name: `adapter_slot`: A permutation: slot s lies on index s // 4 of grp. `seg_adapter`: within one micro-batch, all segments whose adapters' slots lie on the same index of grp use the same adapter.
All inputs are finite; a program needn't handle non-finite values.
Results may differ from the reference program's by a relative error of at most 0.0057.
Values may be sent and summed in bfloat16 or wider, within the bound.
No kernel may reach another device: no remote copies, remote signals or barrier semaphores. Data moves between devices by JAX's collectives and lax.ppermute only.
A program may use at most 64 MiB of HBM per device.

```python
import jax
import jax.numpy as jnp
from jax import lax

D = 8192
R = 128
SEGLEN = 128
SEG = 30
OWN = 4
NA = 16
TOKENS = 15360
N_GRP = 4


def layout_draw(key):
    base = jax.random.fold_in(key, 31)
    keys = jax.random.split(base, 6)
    storage = jax.random.permutation(keys[0], NA)
    inverse = jnp.argsort(storage)
    local_pick = jax.random.randint(keys[1], (N_GRP, N_GRP), 0, OWN)
    order = jax.random.permutation(keys[2], N_GRP)
    first_draw = jax.random.randint(keys[3], (N_GRP, SEG), 0, N_GRP)
    second_draw = jax.random.randint(keys[4], (N_GRP, SEG), 0, N_GRP)
    owners = order[jnp.minimum(first_draw, second_draw)]
    spots = jax.random.randint(keys[5], (N_GRP, 1), 0, SEG)
    positions = jnp.arange(SEG)[None, :]
    owners = jnp.where(positions == spots, order[N_GRP - 1], owners)
    full_group = jax.random.randint(jax.random.fold_in(base, 5), (), 0, N_GRP)
    cover = order[positions % N_GRP]
    owners = jnp.where(jnp.arange(N_GRP)[:, None] == full_group, cover, owners)
    chosen = jnp.take_along_axis(local_pick, owners, axis=1)
    slots = owners * OWN + chosen
    adapters = inverse[slots]
    return (storage.astype(jnp.int32), adapters.astype(jnp.int32))


def draw_adapter_slot(key, part):
    return layout_draw(key)[0]


def draw_seg_adapter(key, part):
    return layout_draw(key)[1]


def block_levels(own_key, dims, pieces, least, high):
    gain, own = 1.0, jax.random.fold_in(own_key, 6)
    for axis_at, parts in pieces:
        draws = jnp.exp(jax.random.uniform(jax.random.fold_in(own, axis_at), (parts,), jnp.float32, least / len(pieces), high / len(pieces)))
        gain = gain * jnp.repeat(draws, dims[axis_at] // parts).reshape([-1 if axis == axis_at else 1 for axis in range(len(dims))])
    return gain


def bell_draw(own_key, dims, scale, limit, shards=(), dtype=jnp.bfloat16):
    array = scale * jax.random.normal(own_key, dims, jnp.float32)
    if shards:
        array = array * block_levels(own_key, dims, shards, -0.22, 0.18)
    return jnp.clip(array, -limit, limit).astype(dtype)


def setup_inputs(seed: int = 0) -> dict:
    key_list = jax.random.split(jax.random.key(seed), 7)
    inputs = bell_draw(key_list[0], (TOKENS, D), 1.0, 6.0, ((0, 4), (1, 8)))
    cotangent = bell_draw(key_list[1], (TOKENS, D), 0.01, 0.059814453, ((0, 4), (1, 8)))
    factor_a = bell_draw(key_list[2], (NA, D, R), D ** -0.5, 0.0625, ((0, 4), (1, 8)))
    factor_b = bell_draw(key_list[3], (NA, R, D), R ** -0.5, 0.5, ((0, 4), (2, 8)))
    adapter_slot = draw_adapter_slot(jax.random.fold_in(key_list[6], 71), 0)
    seg_adapter = draw_seg_adapter(jax.random.fold_in(key_list[6], 71), 0)
    return dict(inputs=inputs, cotangent=cotangent, factor_a=factor_a, factor_b=factor_b, adapter_slot=adapter_slot, seg_adapter=seg_adapter)


def reference(inputs, cotangent, factor_a, factor_b, adapter_slot, seg_adapter):
    slot_table = adapter_slot[seg_adapter].astype(jnp.int32)
    tok_blocks = inputs.reshape(N_GRP, SEG, SEGLEN, D)
    cot_blocks = cotangent.reshape(N_GRP, SEG, SEGLEN, D)

    def one_group(totals, item):
        tok_group, cot_group, slot_row = item
        seg_a = factor_a[slot_row].astype(jnp.float32)
        seg_b = factor_b[slot_row].astype(jnp.float32)
        tok_float = tok_group.astype(jnp.float32)
        cot_float = cot_group.astype(jnp.float32)
        low_input = jnp.einsum("std,sdr->str", tok_float, seg_a).astype(jnp.bfloat16)
        low_grad = jnp.einsum("std,srd->str", cot_float, seg_b).astype(jnp.bfloat16)
        grad_seg_a = jnp.einsum("std,str->sdr", tok_float, low_grad.astype(jnp.float32))
        grad_seg_b = jnp.einsum("str,std->srd", low_input.astype(jnp.float32), cot_float)
        part_a = jax.ops.segment_sum(grad_seg_a, slot_row, num_segments=NA)
        part_b = jax.ops.segment_sum(grad_seg_b, slot_row, num_segments=NA)
        part_a = lax.optimization_barrier(part_a.astype(jnp.bfloat16)).astype(jnp.float32)
        part_b = lax.optimization_barrier(part_b.astype(jnp.bfloat16)).astype(jnp.float32)
        return (totals[0] + part_a, totals[1] + part_b), None

    start = (jnp.zeros((NA, D, R), jnp.float32), jnp.zeros((NA, R, D), jnp.float32))
    totals, unused = lax.scan(one_group, start, (tok_blocks, cot_blocks, slot_table))
    return totals[0].astype(jnp.bfloat16), totals[1].astype(jnp.bfloat16)
```

```python
import functools

import jax
import jax.numpy as jnp
from jax import lax
from jax.experimental import pallas as pl
from jax.experimental.pallas import tpu as pltpu
from jax.sharding import PartitionSpec as P

VMEM_LIMIT = 40 * 1024 * 1024
ANY = pl.BlockSpec(memory_space=pl.ANY)


def peers(groups):
    if groups & (groups - 1) == 0:
        return (lambda i, d: i ^ d), (lambda i, d: i ^ d)
    return (lambda i, d: (i + d) % groups), (lambda i, d: (i + groups - d) % groups)


def step_segments(seg_count):
    return max(n for n in range(1, 7) if seg_count % n == 0)


def pick_kernel(count, slots_ref, factor_ref, *rest):
    outs, sems = rest[:count], rest[count]
    copies = [
        pltpu.make_async_copy(factor_ref.at[slots_ref[d + 1]], outs[d], sems.at[d])
        for d in range(count)
    ]
    for copy in copies:
        copy.start()
    for copy in copies:
        copy.wait()


def pick_factors(slots, factor, groups):
    block = jax.ShapeDtypeStruct(factor.shape[1:], factor.dtype)
    return pl.pallas_call(
        functools.partial(pick_kernel, groups - 1),
        grid_spec=pltpu.PrefetchScalarGridSpec(
            num_scalar_prefetch=1,
            grid=(1,),
            in_specs=[ANY],
            out_specs=[ANY] * (groups - 1),
            scratch_shapes=[pltpu.SemaphoreType.DMA((groups - 1,))],
        ),
        out_shape=[block] * (groups - 1),
        cost_estimate=pl.CostEstimate(
            flops=0, bytes_accessed=2 * (groups - 1) * 2 * block.size, transcendentals=0
        ),
        name="pick_factors",
    )(slots, factor)


def low_kernel(groups, seg_rows, segs, flip, rel_ref, slots_ref, rows_ref, store_ref, *rest):
    others, out_ref, raw, sems = rest[: groups - 1], rest[groups - 1], rest[groups], rest[-1]
    held = rest[groups + 1] if flip else raw
    step = pl.program_id(0)

    @pl.when(step == 0)
    def fetch():
        sources = [store_ref.at[slots_ref[0]], *others]
        copies = [
            pltpu.make_async_copy(source, raw.at[d], sems.at[d])
            for d, source in enumerate(sources)
        ]
        for copy in copies:
            copy.start()
        for d, copy in enumerate(copies):
            copy.wait()
            if flip:
                held[d] = raw[d].T

    for k in range(segs):
        rows = pl.ds(k * seg_rows, seg_rows)
        out_ref[rows, :] = jnp.dot(
            rows_ref[rows, :],
            held[rel_ref[step * segs + k]],
            preferred_element_type=jnp.float32,
        ).astype(out_ref.dtype)


def low_rank_rows(rel, slots, rows, store, others, flip):
    groups = len(others) + 1
    seg_count = rel.shape[0]
    seg_rows = rows.shape[0] // seg_count
    segs = step_segments(seg_count)
    features = rows.shape[1]
    rank = store.shape[1] if flip else store.shape[2]
    scratch = [pltpu.VMEM((groups, *store.shape[1:]), store.dtype)]
    if flip:
        scratch.append(pltpu.VMEM((groups, features, rank), store.dtype))
    return pl.pallas_call(
        functools.partial(low_kernel, groups, seg_rows, segs, flip),
        grid_spec=pltpu.PrefetchScalarGridSpec(
            num_scalar_prefetch=2,
            grid=(seg_count // segs,),
            in_specs=[pl.BlockSpec((segs * seg_rows, features), lambda i, *_: (i, 0))]
            + [ANY] * groups,
            out_specs=pl.BlockSpec((segs * seg_rows, rank), lambda i, *_: (i, 0)),
            scratch_shapes=scratch + [pltpu.SemaphoreType.DMA((groups,))],
        ),
        out_shape=jax.ShapeDtypeStruct((rows.shape[0], rank), jnp.bfloat16),
        compiler_params=pltpu.CompilerParams(vmem_limit_bytes=VMEM_LIMIT),
        cost_estimate=pl.CostEstimate(
            flops=2 * rows.size * rank, bytes_accessed=2 * rows.size, transcendentals=0
        ),
        name="low_rank_rows",
    )(rel, slots, rows, store, *others)


def grad_kernel(groups, seg_rows, segs, flip, rel_ref, low_ref, rows_ref, *rest):
    outs, acc = rest[:groups], rest[groups]
    step = pl.program_id(0)

    @pl.when(step == 0)
    def clear():
        acc[...] = jnp.zeros_like(acc)

    for k in range(segs):
        rows = pl.ds(k * seg_rows, seg_rows)
        where = rel_ref[step * segs + k]
        acc[where] += lax.dot_general(
            low_ref[rows, :],
            rows_ref[rows, :],
            (((0,), (0,)), ((), ())),
            preferred_element_type=jnp.float32,
        )

    @pl.when(step == pl.num_programs(0) - 1)
    def finish():
        for d in range(groups):
            total = acc[d].astype(jnp.bfloat16)
            outs[d][...] = total.T if flip else total


def group_grads(rel, low, rows, groups, flip):
    seg_count = rel.shape[0]
    seg_rows = rows.shape[0] // seg_count
    segs = step_segments(seg_count)
    features, rank = rows.shape[1], low.shape[1]
    shape = (features, rank) if flip else (rank, features)
    return pl.pallas_call(
        functools.partial(grad_kernel, groups, seg_rows, segs, flip),
        grid_spec=pltpu.PrefetchScalarGridSpec(
            num_scalar_prefetch=1,
            grid=(seg_count // segs,),
            in_specs=[
                pl.BlockSpec((segs * seg_rows, rank), lambda i, *_: (i, 0)),
                pl.BlockSpec((segs * seg_rows, features), lambda i, *_: (i, 0)),
            ],
            out_specs=[pl.BlockSpec(shape, lambda i, *_: (0, 0))] * groups,
            scratch_shapes=[pltpu.VMEM((groups, rank, features), jnp.float32)],
        ),
        out_shape=[jax.ShapeDtypeStruct(shape, jnp.bfloat16)] * groups,
        compiler_params=pltpu.CompilerParams(vmem_limit_bytes=VMEM_LIMIT),
        cost_estimate=pl.CostEstimate(
            flops=2 * rows.size * rank, bytes_accessed=2 * rows.size, transcendentals=0
        ),
        name="group_grads",
    )(rel, low, rows)


def total_kernel(groups, slots_ref, *rest):
    blocks, out_ref, acc = rest[:groups], rest[groups], rest[groups + 1]
    acc[...] = jnp.zeros_like(acc)
    for d in range(groups):
        acc[slots_ref[d]] += blocks[d][...].astype(jnp.float32)
    out_ref[...] = acc[...].astype(out_ref.dtype)


def slot_totals(slots, blocks, owned):
    groups = len(blocks)
    shape = blocks[0].shape
    return pl.pallas_call(
        functools.partial(total_kernel, groups),
        grid_spec=pltpu.PrefetchScalarGridSpec(
            num_scalar_prefetch=1,
            grid=(1,),
            in_specs=[pl.BlockSpec(shape, lambda i, *_: (0, 0))] * groups,
            out_specs=pl.BlockSpec((owned, *shape), lambda i, *_: (0, 0, 0)),
            scratch_shapes=[pltpu.VMEM((owned, *shape), jnp.float32)],
        ),
        out_shape=jax.ShapeDtypeStruct((owned, *shape), jnp.bfloat16),
        compiler_params=pltpu.CompilerParams(vmem_limit_bytes=VMEM_LIMIT),
        cost_estimate=pl.CostEstimate(
            flops=groups * blocks[0].size,
            bytes_accessed=2 * (groups + owned) * blocks[0].size,
            transcendentals=0,
        ),
        name="slot_totals",
    )(slots, *blocks)


def tp_sum(part, parts):
    split = part.reshape(parts, part.shape[0] // parts, part.shape[1])
    shares = lax.all_to_all(split, "tp", split_axis=0, concat_axis=0, tiled=True)
    mine = jnp.sum(shares.astype(jnp.float32), axis=0).astype(jnp.bfloat16)
    return lax.all_gather(mine, "tp", axis=0, tiled=True)


def body(groups, parts, inputs, cotangent, factor_a, factor_b, adapter_slot, seg_adapter):
    owned = factor_a.shape[0]
    to, back = peers(groups)
    me = lax.axis_index("grp")
    matches = seg_adapter[:, :, None] == jnp.arange(adapter_slot.shape[0], dtype=jnp.int32)
    slot_all = jnp.sum(jnp.where(matches, adapter_slot, 0), axis=2)
    owner_all, local_all = slot_all // owned, slot_all % owned
    my_slots = jnp.max(jnp.where(owner_all == me, local_all, 0), axis=1)
    order = jnp.arange(groups, dtype=jnp.int32)
    slots = jnp.sum(
        jnp.where(to(me, order)[:, None] == order[None, :], my_slots[None, :], 0), axis=1
    )
    my_owners = lax.dynamic_index_in_dim(owner_all, me, 0, keepdims=False)
    rel = jnp.sum(
        jnp.where(my_owners[:, None] == back(me, order)[None, :], order[None, :], 0), axis=1
    )

    def send(blocks, where):
        return [
            lax.ppermute(block, "grp", [(i, where(i, d + 1)) for i in range(groups)])
            for d, block in enumerate(blocks)
        ]

    got_b = send(pick_factors(slots, factor_b, groups), to)
    picked_a = pick_factors(slots, factor_a, groups)
    picked_a, got_b = lax.optimization_barrier((picked_a, got_b))
    got_a = send(picked_a, to)
    part_grad = low_rank_rows(rel, slots, cotangent, factor_b, got_b, True)
    low_grad = tp_sum(part_grad, parts)
    own_a, *grads_a = group_grads(rel, low_grad, inputs, groups, True)
    grads_a, got_a = lax.optimization_barrier((grads_a, got_a))
    back_a = send(grads_a, back)
    part_input = low_rank_rows(rel, slots, inputs, factor_a, got_a, False)
    low_input = tp_sum(part_input, parts)
    own_b, *grads_b = group_grads(rel, low_input, cotangent, groups, False)
    grads_b, back_a = lax.optimization_barrier((grads_b, back_a))
    back_b = send(grads_b, back)
    grad_a = slot_totals(slots, [own_a, *back_a], owned)
    grad_b = slot_totals(slots, [own_b, *back_b], owned)
    return grad_a, grad_b


def solution(mesh):
    return jax.shard_map(
        functools.partial(body, mesh.shape["grp"], mesh.shape["tp"]),
        mesh=mesh,
        in_specs=(
            P("grp", "tp"),
            P("grp", "tp"),
            P("grp", "tp", None),
            P("grp", None, "tp"),
            P(),
            P(),
        ),
        out_specs=(P("grp", "tp", None), P("grp", None, "tp")),
        check_vma=False,
    )
```

```python
import functools

import jax
import jax.numpy as jnp
from jax import lax
from jax.experimental import pallas as pl
from jax.experimental.pallas import tpu as pltpu
from jax.sharding import PartitionSpec as P

VMEM_LIMIT = 57 * 1024 * 1024
SMALL = pl.CostEstimate(flops=0, bytes_accessed=1024, transcendentals=0)
ANY = pl.BlockSpec(memory_space=pl.ANY)


def peers(groups):
    if groups & (groups - 1) == 0:
        return (lambda i, d: i ^ d), (lambda i, d: i ^ d)
    return (lambda i, d: (i + d) % groups), (lambda i, d: (i + groups - d) % groups)


def step_segments(seg_count):
    return max(n for n in range(1, 7) if seg_count % n == 0)


def pick_kernel(count, slots_ref, *rest):
    for source, out in zip(rest[:count], rest[count:]):
        out[...] = source[0]


def pick_factors(slots, factor, groups):
    block = factor.shape[1:]
    count = groups - 1
    return pl.pallas_call(
        functools.partial(pick_kernel, count),
        grid_spec=pltpu.PrefetchScalarGridSpec(
            num_scalar_prefetch=1,
            grid=(1,),
            in_specs=[
                pl.BlockSpec((1, *block), lambda i, slots, d=d: (slots[d], 0, 0))
                for d in range(1, groups)
            ],
            out_specs=[pl.BlockSpec(block, lambda i, *_: (0, 0))] * count,
        ),
        out_shape=[jax.ShapeDtypeStruct(block, factor.dtype)] * count,
        compiler_params=pltpu.CompilerParams(vmem_limit_bytes=VMEM_LIMIT),
        cost_estimate=SMALL,
        name="pick_factors",
    )(slots, *[factor] * count)


def low_kernel(groups, seg_rows, segs, flip, rel_ref, slots_ref, rows_ref, store_ref, *rest):
    others, out_ref, raw, sems = rest[: groups - 1], rest[groups - 1], rest[groups], rest[-1]
    held = rest[groups + 1] if flip else raw
    step = pl.program_id(0)

    @pl.when(step == 0)
    def fetch():
        sources = [store_ref.at[slots_ref[0]], *others]
        copies = [
            pltpu.make_async_copy(source, raw.at[d], sems.at[d])
            for d, source in enumerate(sources)
        ]
        for copy in copies:
            copy.start()
        for d, copy in enumerate(copies):
            copy.wait()
            if flip:
                held[d] = raw[d].T

    for k in range(segs):
        rows = pl.ds(k * seg_rows, seg_rows)
        out_ref[rows, :] = jnp.dot(
            rows_ref[rows, :],
            held[rel_ref[step * segs + k]],
            preferred_element_type=jnp.float32,
        ).astype(out_ref.dtype)


def low_rank_rows(rel, slots, rows, store, others, flip):
    groups = len(others) + 1
    seg_count = rel.shape[0]
    seg_rows = rows.shape[0] // seg_count
    segs = step_segments(seg_count)
    features = rows.shape[1]
    rank = store.shape[1] if flip else store.shape[2]
    scratch = [pltpu.VMEM((groups, *store.shape[1:]), store.dtype)]
    if flip:
        scratch.append(pltpu.VMEM((groups, features, rank), store.dtype))
    return pl.pallas_call(
        functools.partial(low_kernel, groups, seg_rows, segs, flip),
        grid_spec=pltpu.PrefetchScalarGridSpec(
            num_scalar_prefetch=2,
            grid=(seg_count // segs,),
            in_specs=[pl.BlockSpec((segs * seg_rows, features), lambda i, *_: (i, 0))]
            + [ANY] * groups,
            out_specs=pl.BlockSpec((segs * seg_rows, rank), lambda i, *_: (i, 0)),
            scratch_shapes=scratch + [pltpu.SemaphoreType.DMA((groups,))],
        ),
        out_shape=jax.ShapeDtypeStruct((rows.shape[0], rank), jnp.bfloat16),
        compiler_params=pltpu.CompilerParams(vmem_limit_bytes=VMEM_LIMIT),
        cost_estimate=SMALL,
        name="low_rank_rows",
    )(rel, slots, rows, store, *others)


def grad_kernel(groups, seg_rows, segs, flip, rel_ref, low_ref, rows_ref, *rest):
    outs, acc = rest[:groups], rest[groups]
    step = pl.program_id(0)

    @pl.when(step == 0)
    def clear():
        acc[...] = jnp.zeros_like(acc)

    for k in range(segs):
        rows = pl.ds(k * seg_rows, seg_rows)
        where = rel_ref[step * segs + k]
        acc[where] += lax.dot_general(
            low_ref[rows, :],
            rows_ref[rows, :],
            (((0,), (0,)), ((), ())),
            preferred_element_type=jnp.float32,
        )

    @pl.when(step == pl.num_programs(0) - 1)
    def finish():
        for d in range(groups):
            total = acc[d].astype(jnp.bfloat16)
            outs[d][...] = total.T if flip else total


def group_grads(rel, low, rows, groups, flip):
    seg_count = rel.shape[0]
    seg_rows = rows.shape[0] // seg_count
    segs = step_segments(seg_count)
    features, rank = rows.shape[1], low.shape[1]
    shape = (features, rank) if flip else (rank, features)
    return pl.pallas_call(
        functools.partial(grad_kernel, groups, seg_rows, segs, flip),
        grid_spec=pltpu.PrefetchScalarGridSpec(
            num_scalar_prefetch=1,
            grid=(seg_count // segs,),
            in_specs=[
                pl.BlockSpec((segs * seg_rows, rank), lambda i, *_: (i, 0)),
                pl.BlockSpec((segs * seg_rows, features), lambda i, *_: (i, 0)),
            ],
            out_specs=[pl.BlockSpec(shape, lambda i, *_: (0, 0))] * groups,
            scratch_shapes=[pltpu.VMEM((groups, rank, features), jnp.float32)],
        ),
        out_shape=[jax.ShapeDtypeStruct(shape, jnp.bfloat16)] * groups,
        compiler_params=pltpu.CompilerParams(vmem_limit_bytes=VMEM_LIMIT),
        cost_estimate=SMALL,
        name="group_grads",
    )(rel, low, rows)


def total_kernel(groups, slots_ref, *rest):
    blocks, out_ref, acc = rest[:groups], rest[groups], rest[groups + 1]
    acc[...] = jnp.zeros_like(acc)
    for d in range(groups):
        acc[slots_ref[d]] += blocks[d][...].astype(jnp.float32)
    out_ref[...] = acc[...].astype(out_ref.dtype)


def slot_totals(slots, blocks, owned):
    groups = len(blocks)
    shape = blocks[0].shape
    return pl.pallas_call(
        functools.partial(total_kernel, groups),
        grid_spec=pltpu.PrefetchScalarGridSpec(
            num_scalar_prefetch=1,
            grid=(1,),
            in_specs=[pl.BlockSpec(shape, lambda i, *_: (0, 0))] * groups,
            out_specs=pl.BlockSpec((owned, *shape), lambda i, *_: (0, 0, 0)),
            scratch_shapes=[pltpu.VMEM((owned, *shape), jnp.float32)],
        ),
        out_shape=jax.ShapeDtypeStruct((owned, *shape), jnp.bfloat16),
        compiler_params=pltpu.CompilerParams(vmem_limit_bytes=VMEM_LIMIT),
        cost_estimate=SMALL,
        name="slot_totals",
    )(slots, *blocks)


def tp_sum(part, parts):
    split = part.reshape(parts, part.shape[0] // parts, part.shape[1])
    shares = lax.all_to_all(split, "tp", split_axis=0, concat_axis=0, tiled=True)
    mine = jnp.sum(shares.astype(jnp.float32), axis=0).astype(jnp.bfloat16)
    return lax.all_gather(mine, "tp", axis=0, tiled=True)


def apart(valid, work, *args):
    out = jax.eval_shape(work, *args)
    return lax.cond(valid, work, lambda *_: jnp.zeros(out.shape, out.dtype), *args)


def body(groups, parts, inputs, cotangent, factor_a, factor_b, adapter_slot, seg_adapter):
    owned = factor_a.shape[0]
    to, back = peers(groups)
    me = lax.axis_index("grp")
    matches = seg_adapter[:, :, None] == jnp.arange(adapter_slot.shape[0], dtype=jnp.int32)
    slot_all = jnp.sum(jnp.where(matches, adapter_slot, 0), axis=2)
    owner_all, local_all = slot_all // owned, slot_all % owned
    my_slots = jnp.max(jnp.where(owner_all == me, local_all, 0), axis=1)
    order = jnp.arange(groups, dtype=jnp.int32)
    slots = jnp.sum(
        jnp.where(to(me, order)[:, None] == order[None, :], my_slots[None, :], 0), axis=1
    )
    my_owners = lax.dynamic_index_in_dim(owner_all, me, 0, keepdims=False)
    rel = jnp.sum(
        jnp.where(my_owners[:, None] == back(me, order)[None, :], order[None, :], 0), axis=1
    )

    valid = seg_adapter[0, 0] >= 0

    def send(blocks, where):
        return [
            lax.ppermute(block, "grp", [(i, where(i, d + 1)) for i in range(groups)])
            for d, block in enumerate(blocks)
        ]

    got_b = send(pick_factors(slots, factor_b, groups), to)
    picked_a = pick_factors(slots, factor_a, groups)
    picked_a, got_b = lax.optimization_barrier((picked_a, got_b))
    got_a = send(picked_a, to)
    low_grad = apart(
        valid, lambda *args: tp_sum(low_rank_rows(*args, True), parts), rel, slots, cotangent, factor_b, got_b,
    )
    own_a, *grads_a = group_grads(rel, low_grad, inputs, groups, True)
    grads_a, got_a = lax.optimization_barrier((grads_a, got_a))
    back_a = send(grads_a, back)
    low_input = apart(
        valid, lambda *args: tp_sum(low_rank_rows(*args, False), parts), rel, slots, inputs, factor_a, got_a
    )
    own_b, *grads_b = group_grads(rel, low_input, cotangent, groups, False)
    grads_b, back_a = lax.optimization_barrier((grads_b, back_a))
    back_b = send(grads_b, back)
    grad_a = slot_totals(slots, [own_a, *back_a], owned)
    grad_b = slot_totals(slots, [own_b, *back_b], owned)
    return grad_a, grad_b


def solution(mesh):
    return jax.shard_map(
        functools.partial(body, mesh.shape["grp"], mesh.shape["tp"]),
        mesh=mesh,
        in_specs=(
            P("grp", "tp"),
            P("grp", "tp"),
            P("grp", "tp", None),
            P("grp", None, "tp"),
            P(),
            P(),
        ),
        out_specs=(P("grp", "tp", None), P("grp", None, "tp")),
        check_vma=False,
    )
```

```python
import functools

import jax
import jax.numpy as jnp
from jax import lax
from jax.experimental import pallas as pl
from jax.experimental.pallas import tpu as pltpu
from jax.sharding import PartitionSpec as P

VMEM_LIMIT = 57 * 1024 * 1024
SMALL = pl.CostEstimate(flops=0, bytes_accessed=1024, transcendentals=0)
ANY = pl.BlockSpec(memory_space=pl.ANY)


def peers(groups):
    if groups & (groups - 1) == 0:
        return (lambda i, d: i ^ d), (lambda i, d: i ^ d)
    return (lambda i, d: (i + d) % groups), (lambda i, d: (i + groups - d) % groups)


def step_segments(seg_count):
    return max(n for n in range(1, 7) if seg_count % n == 0)


def segment_specs(segs, seg_rows, features):
    return [
        pl.BlockSpec((seg_rows, features), lambda i, *_, k=k: (i * segs + k, 0))
        for k in range(segs)
    ]


def pick_kernel(count, slots_ref, *rest):
    for source, out in zip(rest[:count], rest[count:]):
        out[...] = source[0]


def pick_factors(slots, factor, groups):
    block = factor.shape[1:]
    count = groups - 1
    return pl.pallas_call(
        functools.partial(pick_kernel, count),
        grid_spec=pltpu.PrefetchScalarGridSpec(
            num_scalar_prefetch=1,
            grid=(1,),
            in_specs=[
                pl.BlockSpec((1, *block), lambda i, slots, d=d: (slots[d], 0, 0))
                for d in range(1, groups)
            ],
            out_specs=[pl.BlockSpec(block, lambda i, *_: (0, 0))] * count,
        ),
        out_shape=[jax.ShapeDtypeStruct(block, factor.dtype)] * count,
        compiler_params=pltpu.CompilerParams(vmem_limit_bytes=VMEM_LIMIT),
        cost_estimate=SMALL,
        name="pick_factors",
    )(slots, *[factor] * count)


def low_kernel(groups, seg_rows, segs, flip, rel_ref, slots_ref, *rest):
    rows_refs, store_ref, rest = rest[:segs], rest[segs], rest[segs + 1 :]
    others, out_ref, raw, sems = rest[: groups - 1], rest[groups - 1], rest[groups], rest[-1]
    held = rest[groups + 1] if flip else raw
    step = pl.program_id(0)

    @pl.when(step == 0)
    def fetch():
        sources = [store_ref.at[slots_ref[0]], *others]
        copies = [
            pltpu.make_async_copy(source, raw.at[d], sems.at[d])
            for d, source in enumerate(sources)
        ]
        for copy in copies:
            copy.start()
        for d, copy in enumerate(copies):
            copy.wait()
            if flip:
                held[d] = raw[d].T

    for k in range(segs):
        out_ref[pl.ds(k * seg_rows, seg_rows), :] = jnp.dot(
            rows_refs[k][...],
            held[rel_ref[step * segs + k]],
            preferred_element_type=jnp.float32,
        ).astype(out_ref.dtype)


def low_rank_rows(rel, slots, rows, store, others, flip):
    groups = len(others) + 1
    seg_count = rel.shape[0]
    seg_rows = rows.shape[0] // seg_count
    segs = step_segments(seg_count)
    features = rows.shape[1]
    rank = store.shape[1] if flip else store.shape[2]
    scratch = [pltpu.VMEM((groups, *store.shape[1:]), store.dtype)]
    if flip:
        scratch.append(pltpu.VMEM((groups, features, rank), store.dtype))
    return pl.pallas_call(
        functools.partial(low_kernel, groups, seg_rows, segs, flip),
        grid_spec=pltpu.PrefetchScalarGridSpec(
            num_scalar_prefetch=2,
            grid=(seg_count // segs,),
            in_specs=segment_specs(segs, seg_rows, features) + [ANY] * groups,
            out_specs=pl.BlockSpec((segs * seg_rows, rank), lambda i, *_: (i, 0)),
            scratch_shapes=scratch + [pltpu.SemaphoreType.DMA((groups,))],
        ),
        out_shape=jax.ShapeDtypeStruct((rows.shape[0], rank), jnp.bfloat16),
        compiler_params=pltpu.CompilerParams(vmem_limit_bytes=VMEM_LIMIT),
        cost_estimate=SMALL,
        name="low_rank_rows",
    )(rel, slots, *[rows] * segs, store, *others)


def grad_kernel(groups, seg_rows, segs, flip, rel_ref, low_ref, *rest):
    rows_refs, rest = rest[:segs], rest[segs:]
    outs, acc = rest[:groups], rest[groups]
    step = pl.program_id(0)

    @pl.when(step == 0)
    def clear():
        acc[...] = jnp.zeros_like(acc)

    for k in range(segs):
        where = rel_ref[step * segs + k]
        acc[where] += lax.dot_general(
            low_ref[pl.ds(k * seg_rows, seg_rows), :],
            rows_refs[k][...],
            (((0,), (0,)), ((), ())),
            preferred_element_type=jnp.float32,
        )

    @pl.when(step == pl.num_programs(0) - 1)
    def finish():
        for d in range(groups):
            total = acc[d].astype(jnp.bfloat16)
            outs[d][...] = total.T if flip else total


def group_grads(rel, low, rows, groups, flip):
    seg_count = rel.shape[0]
    seg_rows = rows.shape[0] // seg_count
    segs = step_segments(seg_count)
    features, rank = rows.shape[1], low.shape[1]
    shape = (features, rank) if flip else (rank, features)
    return pl.pallas_call(
        functools.partial(grad_kernel, groups, seg_rows, segs, flip),
        grid_spec=pltpu.PrefetchScalarGridSpec(
            num_scalar_prefetch=1,
            grid=(seg_count // segs,),
            in_specs=[pl.BlockSpec((segs * seg_rows, rank), lambda i, *_: (i, 0))]
            + segment_specs(segs, seg_rows, features),
            out_specs=[pl.BlockSpec(shape, lambda i, *_: (0, 0))] * groups,
            scratch_shapes=[pltpu.VMEM((groups, rank, features), jnp.float32)],
        ),
        out_shape=[jax.ShapeDtypeStruct(shape, jnp.bfloat16)] * groups,
        compiler_params=pltpu.CompilerParams(vmem_limit_bytes=VMEM_LIMIT),
        cost_estimate=SMALL,
        name="group_grads",
    )(rel, low, *[rows] * segs)


def total_kernel(groups, slots_ref, *rest):
    blocks, out_ref, acc = rest[:groups], rest[groups], rest[groups + 1]
    acc[...] = jnp.zeros_like(acc)
    for d in range(groups):
        acc[slots_ref[d]] += blocks[d][...].astype(jnp.float32)
    out_ref[...] = acc[...].astype(out_ref.dtype)


def slot_totals(slots, blocks, owned):
    groups = len(blocks)
    shape = blocks[0].shape
    return pl.pallas_call(
        functools.partial(total_kernel, groups),
        grid_spec=pltpu.PrefetchScalarGridSpec(
            num_scalar_prefetch=1,
            grid=(1,),
            in_specs=[pl.BlockSpec(shape, lambda i, *_: (0, 0))] * groups,
            out_specs=pl.BlockSpec((owned, *shape), lambda i, *_: (0, 0, 0)),
            scratch_shapes=[pltpu.VMEM((owned, *shape), jnp.float32)],
        ),
        out_shape=jax.ShapeDtypeStruct((owned, *shape), jnp.bfloat16),
        compiler_params=pltpu.CompilerParams(vmem_limit_bytes=VMEM_LIMIT),
        cost_estimate=SMALL,
        name="slot_totals",
    )(slots, *blocks)


def tp_sum(part, parts):
    mine = lax.psum_scatter(part, "tp", scatter_dimension=0, tiled=True).astype(jnp.bfloat16)
    return lax.all_gather(mine, "tp", axis=0, tiled=True)


def apart(valid, work, *args):
    out = jax.eval_shape(work, *args)
    return lax.cond(valid, work, lambda *_: jnp.zeros(out.shape, out.dtype), *args)


def body(groups, parts, inputs, cotangent, factor_a, factor_b, adapter_slot, seg_adapter):
    owned = factor_a.shape[0]
    to, back = peers(groups)
    me = lax.axis_index("grp")
    matches = seg_adapter[:, :, None] == jnp.arange(adapter_slot.shape[0], dtype=jnp.int32)
    slot_all = jnp.sum(jnp.where(matches, adapter_slot, 0), axis=2)
    owner_all, local_all = slot_all // owned, slot_all % owned
    my_slots = jnp.max(jnp.where(owner_all == me, local_all, 0), axis=1)
    order = jnp.arange(groups, dtype=jnp.int32)
    slots = jnp.sum(
        jnp.where(to(me, order)[:, None] == order[None, :], my_slots[None, :], 0), axis=1
    )
    my_owners = lax.dynamic_index_in_dim(owner_all, me, 0, keepdims=False)
    rel = jnp.sum(
        jnp.where(my_owners[:, None] == back(me, order)[None, :], order[None, :], 0), axis=1
    )

    valid = seg_adapter[0, 0] >= 0

    def send(blocks, where):
        return [
            lax.ppermute(block, "grp", [(i, where(i, d + 1)) for i in range(groups)])
            for d, block in enumerate(blocks)
        ]

    got_b = send(pick_factors(slots, factor_b, groups), to)
    picked_a = pick_factors(slots, factor_a, groups)
    picked_a, got_b = lax.optimization_barrier((picked_a, got_b))
    got_a = send(picked_a, to)
    low_grad = apart(
        valid, lambda *args: tp_sum(low_rank_rows(*args, True), parts), rel, slots, cotangent, factor_b, got_b,
    )
    own_a, *grads_a = group_grads(rel, low_grad, inputs, groups, True)
    grads_a, got_a = lax.optimization_barrier((grads_a, got_a))
    back_a = send(grads_a, back)
    low_input = apart(
        valid, lambda *args: tp_sum(low_rank_rows(*args, False), parts), rel, slots, inputs, factor_a, got_a
    )
    own_b, *grads_b = group_grads(rel, low_input, cotangent, groups, False)
    grads_b, back_a = lax.optimization_barrier((grads_b, back_a))
    back_b = send(grads_b, back)
    grad_a = slot_totals(slots, [own_a, *back_a], owned)
    grad_b = slot_totals(slots, [own_b, *back_b], owned)
    return grad_a, grad_b


def solution(mesh):
    return jax.shard_map(
        functools.partial(body, mesh.shape["grp"], mesh.shape["tp"]),
        mesh=mesh,
        in_specs=(
            P("grp", "tp"),
            P("grp", "tp"),
            P("grp", "tp", None),
            P("grp", None, "tp"),
            P(),
            P(),
        ),
        out_specs=(P("grp", "tp", None), P("grp", None, "tp")),
        check_vma=False,
    )
```

```python
import functools

import jax
import jax.numpy as jnp
from jax import lax
from jax.experimental import pallas as pl
from jax.experimental.pallas import tpu as pltpu
from jax.sharding import PartitionSpec as P

VMEM_LIMIT = 24 * 1024 * 1024
ANY = pl.BlockSpec(memory_space=pl.ANY)
PARAMS = pltpu.CompilerParams(vmem_limit_bytes=VMEM_LIMIT)


def cost(flops, moved):
    return pl.CostEstimate(flops=flops, bytes_accessed=moved, transcendentals=0)


def peers(groups):
    if groups & (groups - 1) == 0:
        across = lambda i, d: i ^ ((groups - d) % groups)
        return across, across
    return (lambda i, d: (i + d) % groups), (lambda i, d: (i + groups - d) % groups)


def step_segments(seg_count, most):
    return max(n for n in range(1, most + 1) if seg_count % n == 0)


def whole(shape):
    return pl.BlockSpec(shape, lambda i, *_: (0,) * len(shape))


def pick_kernel(groups, slots_ref, *rest):
    for source, out in zip(rest[:groups], rest[groups:]):
        out[...] = source[0]


def pick_factors(slots, factor, groups):
    block = factor.shape[1:]
    return pl.pallas_call(
        functools.partial(pick_kernel, groups),
        grid_spec=pltpu.PrefetchScalarGridSpec(
            num_scalar_prefetch=1,
            grid=(1,),
            in_specs=[
                pl.BlockSpec((1, *block), lambda i, slots, d=d: (slots[d], 0, 0))
                for d in range(groups)
            ],
            out_specs=[whole(block)] * groups,
        ),
        out_shape=[jax.ShapeDtypeStruct(block, factor.dtype)] * groups,
        compiler_params=PARAMS,
        cost_estimate=cost(0, 4 * groups * block[0] * block[1]),
        name="pick_factors",
    )(slots, *[pltpu.with_memory_space_constraint(factor, pltpu.HBM)] * groups)


def low_kernel(seg_rows, pieces, flip, rel_ref, half_ref, rows_ref, *rest):
    groups = len(rest) - 4 - flip
    blocks, out_ref, rest = rest[:groups], rest[groups], rest[groups + 1 :]
    raw, rows, sems = rest[0], rest[-2], rest[-1]
    held = rest[1] if flip else raw
    piece = rows.shape[0] // pieces
    base = half_ref[0] * rows.shape[0]
    fetches = [pltpu.make_async_copy(blocks[d], raw.at[d], sems.at[d]) for d in range(groups)]
    arrivals = [
        pltpu.make_async_copy(
            rows_ref.at[pl.ds(pl.multiple_of(base + k * piece, seg_rows), piece)],
            rows.at[pl.ds(k * piece, piece)],
            sems.at[groups + k],
        )
        for k in range(pieces)
    ]
    for copy in fetches + arrivals:
        copy.start()
    for d, copy in enumerate(fetches):
        copy.wait()
        if flip:
            held[d] = raw[d].T
    segs = piece // seg_rows
    first = half_ref[0] * segs * pieces
    for k, copy in enumerate(arrivals):
        copy.wait()
        for n in range(k * segs, (k + 1) * segs):
            at = pl.ds(n * seg_rows, seg_rows)
            out_ref[at, :] = jnp.dot(
                rows[at, :], held[rel_ref[first + n]], preferred_element_type=jnp.float32
            ).astype(out_ref.dtype)


def low_rank_rows(rel, half, rows, blocks, flip, dtype):
    groups = len(blocks)
    seg_count = rel.shape[0]
    seg_rows = rows.shape[0] // seg_count
    pieces = seg_count // 2 // step_segments(seg_count // 2, 3)
    count, features = rows.shape[0] // 2, rows.shape[1]
    rank = blocks[0].shape[0 if flip else 1]
    scratch = [pltpu.VMEM((groups, *blocks[0].shape), rows.dtype)]
    if flip:
        scratch.append(pltpu.VMEM((groups, features, rank), rows.dtype))
    return pl.pallas_call(
        functools.partial(low_kernel, seg_rows, pieces, flip),
        grid_spec=pltpu.PrefetchScalarGridSpec(
            num_scalar_prefetch=2,
            grid=(1,),
            in_specs=[ANY] * (groups + 1),
            out_specs=whole((count, rank)),
            scratch_shapes=[
                *scratch,
                pltpu.VMEM((count, features), rows.dtype),
                pltpu.SemaphoreType.DMA((groups + pieces,)),
            ],
        ),
        out_shape=jax.ShapeDtypeStruct((count, rank), dtype),
        compiler_params=PARAMS,
        cost_estimate=cost(rows.size * rank, rows.size),
        name="low_rank_rows",
    )(rel, half, pltpu.with_memory_space_constraint(rows, pltpu.HBM), *blocks)


def share_kernel(chips, chip_ref, kept_ref, got_ref, *rest):
    outs, total = rest[:chips], rest[chips]
    total[...] = kept_ref[...] + got_ref[...].astype(jnp.float32)
    count = total.shape[0] // chips
    for q in range(chips):
        start = pl.multiple_of(chip_ref[q] * count, 8)
        outs[q][...] = total[pl.ds(start, count), :].astype(outs[q].dtype)


def chip_shares(chip_order, kept, got):
    chips = chip_order.shape[0]
    block = (kept.shape[0] // chips, kept.shape[1])
    return pl.pallas_call(
        functools.partial(share_kernel, chips),
        grid_spec=pltpu.PrefetchScalarGridSpec(
            num_scalar_prefetch=1,
            grid=(1,),
            in_specs=[whole(kept.shape), whole(got.shape)],
            out_specs=[whole(block)] * chips,
            scratch_shapes=[pltpu.VMEM(kept.shape, jnp.float32)],
        ),
        out_shape=[
            jax.ShapeDtypeStruct(block, jnp.bfloat16 if q else jnp.float32) for q in range(chips)
        ],
        compiler_params=PARAMS,
        cost_estimate=cost(kept.size, 8 * kept.size),
        name="chip_shares",
    )(chip_order, kept, got)


def sum_kernel(own_ref, *rest):
    total = own_ref[...]
    for ref in rest[:-1]:
        total += ref[...].astype(jnp.float32)
    rest[-1][...] = total.astype(rest[-1].dtype)


def sum_shares(own, others):
    return pl.pallas_call(
        sum_kernel,
        out_shape=jax.ShapeDtypeStruct(own.shape, jnp.bfloat16),
        cost_estimate=cost(own.size, 8 * own.size),
        compiler_params=PARAMS,
        name="sum_shares",
    )(own, *others)


def low_rows(parts, rel, rows, *blocks, flip):
    chips = parts // 2
    to, _ = peers(chips)
    index = lax.axis_index("tp")
    core, chip = index % 2, index // 2
    give = low_rank_rows(rel, (1 - core)[None], rows, blocks, flip, jnp.bfloat16)
    got = lax.ppermute(give, "tp", [(i, i ^ 1) for i in range(parts)])
    kept = low_rank_rows(rel, core[None], rows, blocks, flip, jnp.float32)
    order = to(chip, jnp.arange(chips, dtype=jnp.int32)).astype(jnp.int32)
    own, *shares = chip_shares(order, kept, got)
    others = [
        lax.ppermute(share, "tp", [(i, to(i // 2, q + 1) * 2 + i % 2) for i in range(parts)])
        for q, share in enumerate(shares)
    ]
    mine = sum_shares(own, others)
    half = lax.all_gather(
        mine, "tp", axis=0, tiled=True,
        axis_index_groups=[[2 * c + k for c in range(chips)] for k in range(2)],
    )
    return lax.all_gather(
        half, "tp", axis=0, tiled=True,
        axis_index_groups=[[2 * c, 2 * c + 1] for c in range(chips)],
    )


def grad_kernel(groups, seg_rows, pieces, flip, rel_ref, low_ref, rows_ref, *rest):
    outs, (acc, low, rows, sems) = rest[:groups], rest[groups:]
    piece = rows.shape[0] // pieces
    segs = piece // seg_rows

    def arrival(k):
        at = pl.ds(pl.multiple_of(k * piece, seg_rows), piece)
        return pltpu.make_async_copy(rows_ref.at[at], rows.at[at], sems.at[k])

    lows = pltpu.make_async_copy(low_ref, low, sems.at[pieces])
    lows.start()
    for k in range(pieces):
        arrival(k).start()
    acc[...] = jnp.zeros_like(acc)
    lows.wait()

    def add_piece(k, carry):
        arrival(k).wait()
        for n in range(segs):
            at = pl.ds(pl.multiple_of(k * piece + n * seg_rows, seg_rows), seg_rows)
            acc[rel_ref[k * segs + n]] += lax.dot_general(
                low[at, :],
                rows[at, :],
                (((0,), (0,)), ((), ())),
                preferred_element_type=jnp.float32,
            )
        return carry

    lax.fori_loop(0, pieces, add_piece, 0)
    for d in range(groups):
        total = acc[d].astype(jnp.bfloat16)
        outs[d][...] = total.T if flip else total


def group_grads(rel, low, rows, groups, flip):
    seg_count = rel.shape[0]
    seg_rows = rows.shape[0] // seg_count
    pieces = seg_count // step_segments(seg_count, 5)
    features, rank = rows.shape[1], low.shape[1]
    shape = (features, rank) if flip else (rank, features)
    return pl.pallas_call(
        functools.partial(grad_kernel, groups, seg_rows, pieces, flip),
        grid_spec=pltpu.PrefetchScalarGridSpec(
            num_scalar_prefetch=1,
            grid=(1,),
            in_specs=[ANY, ANY],
            out_specs=[whole(shape)] * groups,
            scratch_shapes=[
                pltpu.VMEM((groups, rank, features), jnp.float32),
                pltpu.VMEM(low.shape, low.dtype),
                pltpu.VMEM(rows.shape, rows.dtype),
                pltpu.SemaphoreType.DMA((pieces + 1,)),
            ],
        ),
        out_shape=[jax.ShapeDtypeStruct(shape, jnp.bfloat16)] * groups,
        compiler_params=PARAMS,
        cost_estimate=cost(0, 1024),
        name="group_grads",
    )(rel, low, pltpu.with_memory_space_constraint(rows, pltpu.HBM))


def total_kernel(groups, slots_ref, *rest):
    blocks, out_ref, acc = rest[:groups], rest[groups], rest[groups + 1]
    acc[...] = jnp.zeros_like(acc)
    for d in range(groups):
        acc[slots_ref[d]] += blocks[d][...].astype(jnp.float32)
    out_ref[...] = acc[...].astype(out_ref.dtype)


def slot_totals(slots, blocks, owned):
    groups = len(blocks)
    shape = blocks[0].shape
    return pl.pallas_call(
        functools.partial(total_kernel, groups),
        grid_spec=pltpu.PrefetchScalarGridSpec(
            num_scalar_prefetch=1,
            grid=(1,),
            in_specs=[pl.BlockSpec(shape, lambda i, *_: (0, 0))] * groups,
            out_specs=pl.BlockSpec((owned, *shape), lambda i, *_: (0, 0, 0)),
            scratch_shapes=[pltpu.VMEM((owned, *shape), jnp.float32)],
        ),
        out_shape=jax.ShapeDtypeStruct((owned, *shape), jnp.bfloat16),
        compiler_params=PARAMS,
        cost_estimate=cost(groups * blocks[0].size, 2 * (groups + owned) * blocks[0].size),
        name="slot_totals",
    )(slots, *blocks)


def apart(valid, work, *args):
    out = jax.eval_shape(work, *args)
    return lax.cond(valid, work, lambda *_: jnp.zeros(out.shape, out.dtype), *args)


def body(groups, parts, inputs, cotangent, factor_a, factor_b, adapter_slot, seg_adapter):
    owned = factor_a.shape[0]
    to, back = peers(groups)
    me = lax.axis_index("grp")
    matches = seg_adapter[:, :, None] == jnp.arange(adapter_slot.shape[0], dtype=jnp.int32)
    slot_all = jnp.sum(jnp.where(matches, adapter_slot, 0), axis=2)
    owner_all, local_all = slot_all // owned, slot_all % owned
    my_slots = jnp.max(jnp.where(owner_all == me, local_all, 0), axis=1)
    order = jnp.arange(groups, dtype=jnp.int32)
    slots = jnp.sum(
        jnp.where(to(me, order)[:, None] == order[None, :], my_slots[None, :], 0), axis=1
    )
    my_owners = lax.dynamic_index_in_dim(owner_all, me, 0, keepdims=False)
    rel = jnp.sum(
        jnp.where(my_owners[:, None] == back(me, order)[None, :], order[None, :], 0), axis=1
    )

    valid = me >= 0

    def send(blocks, where):
        return [
            lax.ppermute(block, "grp", [(i, where(i, d)) for i in range(groups)])
            for d, block in enumerate(blocks, 1)
        ]

    low_of_a = functools.partial(low_rows, parts, flip=False)
    low_of_b = functools.partial(low_rows, parts, flip=True)
    own_factor_b, *picked_b = pick_factors(slots, factor_b, groups)
    got_b = send(picked_b, to)
    own_factor_a, *picked_a = pick_factors(slots, factor_a, groups)
    picked_a, got_b = lax.optimization_barrier((picked_a, got_b))
    got_a = send(picked_a, to)
    low_grad = apart(valid, low_of_b, rel, cotangent, own_factor_b, *got_b)
    own_a, *grads_a = group_grads(rel, low_grad, inputs, groups, True)
    grads_a, got_a = lax.optimization_barrier((grads_a, got_a))
    back_a = send(grads_a, back)
    low_input = apart(valid, low_of_a, rel, inputs, own_factor_a, *got_a)
    own_b, *grads_b = group_grads(rel, low_input, cotangent, groups, False)
    grads_b, back_a = lax.optimization_barrier((grads_b, back_a))
    back_b = send(grads_b, back)
    grad_a = slot_totals(slots, [own_a, *back_a], owned)
    grad_b = slot_totals(slots, [own_b, *back_b], owned)
    return grad_a, grad_b


def solution(mesh):
    return jax.shard_map(
        functools.partial(body, mesh.shape["grp"], mesh.shape["tp"]),
        mesh=mesh,
        in_specs=(
            P("grp", "tp"),
            P("grp", "tp"),
            P("grp", "tp", None),
            P("grp", None, "tp"),
            P(),
            P(),
        ),
        out_specs=(P("grp", "tp", None), P("grp", None, "tp")),
        check_vma=False,
    )
```

```python
import functools

import jax
import jax.numpy as jnp
from jax import lax
from jax.experimental import pallas as pl
from jax.experimental.pallas import tpu as pltpu
from jax.sharding import PartitionSpec as P

VMEM_LIMIT = 24 * 1024 * 1024
ANY = pl.BlockSpec(memory_space=pl.ANY)
HELD = pl.BlockSpec(memory_space=pltpu.VMEM)
PARAMS = pltpu.CompilerParams(vmem_limit_bytes=VMEM_LIMIT)


def cost(flops, moved):
    return pl.CostEstimate(flops=flops, bytes_accessed=moved, transcendentals=0)


def peers(groups):
    if groups & (groups - 1) == 0:
        across = lambda i, d: i ^ ((groups - d) % groups)
        return across, across
    return (lambda i, d: (i + d) % groups), (lambda i, d: (i + groups - d) % groups)


def step_segments(seg_count, most):
    return max(n for n in range(1, most + 1) if seg_count % n == 0)


def whole(shape):
    return pl.BlockSpec(shape, lambda i, *_: (0,) * len(shape))


def pick_kernel(groups, slots_ref, *rest):
    for source, out in zip(rest[:groups], rest[groups:]):
        out[...] = source[0]


def pick_factors(slots, factor, groups):
    block = factor.shape[1:]
    return pl.pallas_call(
        functools.partial(pick_kernel, groups),
        grid_spec=pltpu.PrefetchScalarGridSpec(
            num_scalar_prefetch=1,
            grid=(1,),
            in_specs=[
                pl.BlockSpec((1, *block), lambda i, slots, d=d: (slots[d], 0, 0))
                for d in range(groups)
            ],
            out_specs=[whole(block)] * groups,
        ),
        out_shape=[jax.ShapeDtypeStruct(block, factor.dtype)] * groups,
        compiler_params=PARAMS,
        cost_estimate=cost(0, 4 * groups * block[0] * block[1]),
        name="pick_factors",
    )(slots, *[pltpu.with_memory_space_constraint(factor, pltpu.HBM)] * groups)


def low_kernel(seg_rows, pieces, flip, keep, rel_ref, half_ref, rows_ref, *rest):
    groups = len(rest) - 4 - flip
    blocks, out_ref, rest = rest[:groups], rest[groups], rest[groups + 1 :]
    rows, rest = (rest[0], rest[1:]) if keep else (rest[-2], (*rest[:-2], rest[-1]))
    raw, sems = rest[0], rest[-1]
    held = rest[1] if flip else raw
    piece = rows.shape[0] // pieces
    base = half_ref[0] * rows.shape[0]
    fetches = [pltpu.make_async_copy(blocks[d], raw.at[d], sems.at[d]) for d in range(groups)]
    arrivals = [
        pltpu.make_async_copy(
            rows_ref.at[pl.ds(pl.multiple_of(base + k * piece, seg_rows), piece)],
            rows.at[pl.ds(k * piece, piece)],
            sems.at[groups + k],
        )
        for k in range(pieces)
    ]
    for copy in fetches + arrivals:
        copy.start()
    for d, copy in enumerate(fetches):
        copy.wait()
        if flip:
            held[d] = raw[d].T
    segs = piece // seg_rows
    first = half_ref[0] * segs * pieces
    for k, copy in enumerate(arrivals):
        copy.wait()
        for n in range(k * segs, (k + 1) * segs):
            at = pl.ds(n * seg_rows, seg_rows)
            out_ref[at, :] = jnp.dot(
                rows[at, :], held[rel_ref[first + n]], preferred_element_type=jnp.float32
            ).astype(out_ref.dtype)


def low_rank_rows(rel, half, rows, blocks, flip, dtype, keep):
    groups = len(blocks)
    seg_count = rel.shape[0]
    seg_rows = rows.shape[0] // seg_count
    pieces = seg_count // 2 // step_segments(seg_count // 2, 3)
    count, features = rows.shape[0] // 2, rows.shape[1]
    rank = blocks[0].shape[0 if flip else 1]
    scratch = [pltpu.VMEM((groups, *blocks[0].shape), rows.dtype)]
    if flip:
        scratch.append(pltpu.VMEM((groups, features, rank), rows.dtype))
    if not keep:
        scratch.append(pltpu.VMEM((count, features), rows.dtype))
    out = jax.ShapeDtypeStruct((count, rank), dtype)
    return pl.pallas_call(
        functools.partial(low_kernel, seg_rows, pieces, flip, keep),
        grid_spec=pltpu.PrefetchScalarGridSpec(
            num_scalar_prefetch=2,
            grid=(1,),
            in_specs=[ANY] * (groups + 1),
            out_specs=[whole((count, rank)), HELD] if keep else whole((count, rank)),
            scratch_shapes=[*scratch, pltpu.SemaphoreType.DMA((groups + pieces,))],
        ),
        out_shape=[out, pltpu.VMEM((count, features), rows.dtype)] if keep else out,
        compiler_params=PARAMS,
        cost_estimate=cost(rows.size * rank, rows.size),
        name="low_rank_rows",
    )(rel, half, pltpu.with_memory_space_constraint(rows, pltpu.HBM), *blocks)


def hold_kernel(halves_ref, rows_ref, *rest):
    outs, sems = rest[:-1], rest[-1]
    count = outs[0].shape[0]
    copies = [
        pltpu.make_async_copy(
            rows_ref.at[pl.ds(pl.multiple_of(halves_ref[k] * count, 16), count)], out, sems.at[k]
        )
        for k, out in enumerate(outs)
    ]
    for copy in copies:
        copy.start()
    for copy in copies:
        copy.wait()


def hold(halves, rows):
    shape = (rows.shape[0] // 2, rows.shape[1])
    return pl.pallas_call(
        hold_kernel,
        grid_spec=pltpu.PrefetchScalarGridSpec(
            num_scalar_prefetch=1,
            grid=(1,),
            in_specs=[ANY],
            out_specs=[HELD] * 2,
            scratch_shapes=[pltpu.SemaphoreType.DMA((2,))],
        ),
        out_shape=[pltpu.VMEM(shape, rows.dtype)] * 2,
        compiler_params=PARAMS,
        cost_estimate=cost(0, 4 * rows.size),
        name="hold_rows",
    )(halves, pltpu.with_memory_space_constraint(rows, pltpu.HBM))


def share_kernel(chips, chip_ref, kept_ref, got_ref, *rest):
    outs, total = rest[:chips], rest[chips]
    total[...] = kept_ref[...] + got_ref[...].astype(jnp.float32)
    count = total.shape[0] // chips
    for q in range(chips):
        start = pl.multiple_of(chip_ref[q] * count, 8)
        outs[q][...] = total[pl.ds(start, count), :].astype(outs[q].dtype)


def chip_shares(chip_order, kept, got):
    chips = chip_order.shape[0]
    block = (kept.shape[0] // chips, kept.shape[1])
    return pl.pallas_call(
        functools.partial(share_kernel, chips),
        grid_spec=pltpu.PrefetchScalarGridSpec(
            num_scalar_prefetch=1,
            grid=(1,),
            in_specs=[whole(kept.shape), whole(got.shape)],
            out_specs=[whole(block)] * chips,
            scratch_shapes=[pltpu.VMEM(kept.shape, jnp.float32)],
        ),
        out_shape=[
            jax.ShapeDtypeStruct(block, jnp.bfloat16 if q else jnp.float32) for q in range(chips)
        ],
        compiler_params=PARAMS,
        cost_estimate=cost(kept.size, 8 * kept.size),
        name="chip_shares",
    )(chip_order, kept, got)


def sum_kernel(own_ref, *rest):
    total = own_ref[...]
    for ref in rest[:-1]:
        total += ref[...].astype(jnp.float32)
    rest[-1][...] = total.astype(rest[-1].dtype)


def sum_shares(own, others):
    return pl.pallas_call(
        sum_kernel,
        out_shape=jax.ShapeDtypeStruct(own.shape, jnp.bfloat16),
        cost_estimate=cost(own.size, 8 * own.size),
        compiler_params=PARAMS,
        name="sum_shares",
    )(own, *others)


def from_other_core(parts, block):
    return lax.ppermute(block, "tp", [(i, i ^ 1) for i in range(parts)])


def chip_totals(parts, chip_order, kept, got):
    to, _ = peers(parts // 2)
    own, *shares = chip_shares(chip_order, kept, got)
    others = [
        lax.ppermute(share, "tp", [(i, to(i // 2, q + 1) * 2 + i % 2) for i in range(parts)])
        for q, share in enumerate(shares)
    ]
    return sum_shares(own, others)


def gather_chips(parts, mine):
    to, _ = peers(parts // 2)
    return [mine] + [
        lax.ppermute(mine, "tp", [(to(i // 2, q) * 2 + i % 2, i) for i in range(parts)])
        for q in range(1, parts // 2)
    ]


def gather_cores(parts, chip_order, blocks):
    if blocks[0].shape[0] % 16:
        stacked = jnp.take(jnp.stack(blocks), jnp.argsort(chip_order), axis=0)
        half, chip_order = stacked.reshape(-1, stacked.shape[2]), jnp.zeros((1,), jnp.int32)
    else:
        half = jnp.concatenate(blocks)
    return [from_other_core(parts, half), half], chip_order


def grad_kernel(groups, seg_rows, flip, rel_ref, halves_ref, chip_ref, *rest):
    lows, halves, rest = rest[:2], rest[2:4], rest[4:]
    outs, (acc, low, sems) = rest[:groups], rest[groups:]
    count, chips = halves[0].shape[0], chip_ref.shape[0]
    part = count // chips

    def arrival(k, q):
        to = pl.multiple_of(halves_ref[k] * count + chip_ref[q] * part, 16)
        return pltpu.make_async_copy(
            lows[k].at[pl.ds(q * part, part)], low.at[pl.ds(to, part)], sems.at[k * chips + q]
        )

    copies = [arrival(k, q) for k in range(2) for q in range(chips)]
    for copy in copies:
        copy.start()
    acc[...] = jnp.zeros_like(acc)
    for copy in copies:
        copy.wait()
    segs = count // seg_rows
    unroll = step_segments(segs, 5)
    for k in range(2):
        def add_segments(step, carry, k=k):
            for n in range(unroll):
                at = step * unroll + n
                seg = halves_ref[k] * segs + at
                acc[rel_ref[seg]] += lax.dot_general(
                    low[pl.ds(pl.multiple_of(seg * seg_rows, seg_rows), seg_rows), :],
                    halves[k][pl.ds(pl.multiple_of(at * seg_rows, seg_rows), seg_rows), :],
                    (((0,), (0,)), ((), ())),
                    preferred_element_type=jnp.float32,
                )
            return carry

        lax.fori_loop(0, segs // unroll, add_segments, 0)
    for d in range(groups):
        total = acc[d].astype(jnp.bfloat16)
        outs[d][...] = total.T if flip else total


def group_grads(rel, halves, chip_order, lows, rows, groups, flip):
    seg_count = rel.shape[0]
    count, features = rows[0].shape
    seg_rows = 2 * count // seg_count
    rank = lows[0].shape[1]
    shape = (features, rank) if flip else (rank, features)
    return pl.pallas_call(
        functools.partial(grad_kernel, groups, seg_rows, flip),
        grid_spec=pltpu.PrefetchScalarGridSpec(
            num_scalar_prefetch=3,
            grid=(1,),
            in_specs=[ANY, ANY, HELD, HELD],
            out_specs=[whole(shape)] * groups,
            scratch_shapes=[
                pltpu.VMEM((groups, rank, features), jnp.float32),
                pltpu.VMEM((2 * count, rank), jnp.bfloat16),
                pltpu.SemaphoreType.DMA((2 * chip_order.shape[0],)),
            ],
        ),
        out_shape=[jax.ShapeDtypeStruct(shape, jnp.bfloat16)] * groups,
        compiler_params=PARAMS,
        cost_estimate=cost(0, 1024),
        name="group_grads",
    )(rel, halves, chip_order, *lows, *rows)


def total_kernel(groups, slots_ref, *rest):
    blocks, out_ref, acc = rest[:groups], rest[groups], rest[groups + 1]
    acc[...] = jnp.zeros_like(acc)
    for d in range(groups):
        acc[slots_ref[d]] += blocks[d][...].astype(jnp.float32)
    out_ref[...] = acc[...].astype(out_ref.dtype)


def slot_totals(slots, blocks, owned):
    groups = len(blocks)
    shape = blocks[0].shape
    return pl.pallas_call(
        functools.partial(total_kernel, groups),
        grid_spec=pltpu.PrefetchScalarGridSpec(
            num_scalar_prefetch=1,
            grid=(1,),
            in_specs=[pl.BlockSpec(shape, lambda i, *_: (0, 0))] * groups,
            out_specs=pl.BlockSpec((owned, *shape), lambda i, *_: (0, 0, 0)),
            scratch_shapes=[pltpu.VMEM((owned, *shape), jnp.float32)],
        ),
        out_shape=jax.ShapeDtypeStruct((owned, *shape), jnp.bfloat16),
        compiler_params=PARAMS,
        cost_estimate=cost(groups * blocks[0].size, 2 * (groups + owned) * blocks[0].size),
        name="slot_totals",
    )(slots, *blocks)


def apart(valid, work, *args):
    out = jax.eval_shape(work, *args)
    zeros = lambda *_: jax.tree.map(lambda leaf: jnp.zeros(leaf.shape, leaf.dtype), out)
    return lax.cond(valid, work, zeros, *args)


def body(groups, parts, inputs, cotangent, factor_a, factor_b, adapter_slot, seg_adapter):
    owned = factor_a.shape[0]
    to, back = peers(groups)
    me = lax.axis_index("grp")
    matches = seg_adapter[:, :, None] == jnp.arange(adapter_slot.shape[0], dtype=jnp.int32)
    slot_all = jnp.sum(jnp.where(matches, adapter_slot, 0), axis=2)
    owner_all, local_all = slot_all // owned, slot_all % owned
    my_slots = jnp.max(jnp.where(owner_all == me, local_all, 0), axis=1)
    order = jnp.arange(groups, dtype=jnp.int32)
    slots = jnp.sum(
        jnp.where(to(me, order)[:, None] == order[None, :], my_slots[None, :], 0), axis=1
    )
    my_owners = lax.dynamic_index_in_dim(owner_all, me, 0, keepdims=False)
    rel = jnp.sum(
        jnp.where(my_owners[:, None] == back(me, order)[None, :], order[None, :], 0), axis=1
    )

    valid = me >= 0

    def send(block, d, where):
        return lax.ppermute(block, "grp", [(i, where(i, d)) for i in range(groups)])

    def send_all(blocks, where):
        return [send(block, d, where) for d, block in enumerate(blocks, 1)]

    chips = parts // 2
    index = lax.axis_index("tp")
    core, chip = index % 2, index // 2
    halves = jnp.stack([1 - core, core])
    chip_order = peers(chips)[0](chip, jnp.arange(chips, dtype=jnp.int32)).astype(jnp.int32)
    own_factor_b, *picked_b = pick_factors(slots, factor_b, groups)
    *far_b, near_b = send_all(picked_b, to)
    own_factor_a, *picked_a = pick_factors(slots, factor_a, groups)
    *picked_a, near_a = picked_a
    near_a, near_b = lax.optimization_barrier((near_a, near_b))
    near_a = send(near_a, groups - 1, to)
    picked_a, far_b, near_a, near_b = lax.optimization_barrier((picked_a, far_b, near_a, near_b))
    far_a = send_all(picked_a, to)
    def grad_totals(rel, halves, chip_order, cotangent, *blocks):
        give = low_rank_rows(rel, halves[:1], cotangent, blocks, True, jnp.bfloat16, False)
        got = from_other_core(parts, give)
        kept = low_rank_rows(rel, halves[1:], cotangent, blocks, True, jnp.float32, False)
        return chip_totals(parts, chip_order, kept, got)

    mine_grad = apart(
        valid, grad_totals, rel, halves, chip_order, cotangent, own_factor_b, *far_b, near_b
    )
    far_a, mine_grad = lax.optimization_barrier((far_a, mine_grad))
    grad_blocks = gather_chips(parts, mine_grad)
    blocks_a = own_factor_a, *far_a, near_a
    give, tok_give = low_rank_rows(rel, halves[:1], inputs, blocks_a, False, jnp.bfloat16, True)
    grad_blocks, give = lax.optimization_barrier((grad_blocks, give))
    got = from_other_core(parts, give)
    low_grad, order = gather_cores(parts, chip_order, grad_blocks)
    kept, tok_kept = low_rank_rows(rel, halves[1:], inputs, blocks_a, False, jnp.float32, True)
    low_grad, kept = lax.optimization_barrier((low_grad, kept))
    own_a, *grads_a = group_grads(
        rel, halves, order, low_grad, [tok_give, tok_kept], groups, True
    )
    back_a = send_all(grads_a, back)
    kept, own_a = lax.optimization_barrier((kept, own_a))

    def input_grads(rel, halves, chip_order, cotangent, kept, got):
        mine = chip_totals(parts, chip_order, kept, got)
        low_input, order = gather_cores(parts, chip_order, gather_chips(parts, mine))
        rows = hold(halves, cotangent)
        return group_grads(rel, halves, order, low_input, rows, groups, False)

    own_b, *grads_b = apart(valid, input_grads, rel, halves, chip_order, cotangent, kept, got)
    grads_b, back_a[:-1] = lax.optimization_barrier((grads_b, back_a[:-1]))
    back_b = send_all(grads_b, back)
    grad_a = slot_totals(slots, [own_a, *back_a], owned)
    grad_b = slot_totals(slots, [own_b, *back_b], owned)
    return grad_a, grad_b


def solution(mesh):
    return jax.shard_map(
        functools.partial(body, mesh.shape["grp"], mesh.shape["tp"]),
        mesh=mesh,
        in_specs=(
            P("grp", "tp"),
            P("grp", "tp"),
            P("grp", "tp", None),
            P("grp", None, "tp"),
            P(),
            P(),
        ),
        out_specs=(P("grp", "tp", None), P("grp", None, "tp")),
        check_vma=False,
    )
```

```python
import functools

import jax
import jax.numpy as jnp
from jax import lax
from jax.experimental import pallas as pl
from jax.experimental.pallas import tpu as pltpu
from jax.sharding import PartitionSpec as P

VMEM_LIMIT = 24 * 1024 * 1024
ANY = pl.BlockSpec(memory_space=pl.ANY)
HELD = pl.BlockSpec(memory_space=pltpu.VMEM)
PARAMS = pltpu.CompilerParams(vmem_limit_bytes=VMEM_LIMIT)


def cost(flops, moved):
    return pl.CostEstimate(flops=flops, bytes_accessed=moved, transcendentals=0)


def peers(groups):
    if groups & (groups - 1) == 0:
        across = lambda i, d: i ^ ((groups - d) % groups)
        return across, across
    return (lambda i, d: (i + d) % groups), (lambda i, d: (i + groups - d) % groups)


def step_segments(seg_count, most):
    return max(n for n in range(1, most + 1) if seg_count % n == 0)


def whole(shape):
    return pl.BlockSpec(shape, lambda i, *_: (0,) * len(shape))


def pick_kernel(groups, slots_ref, *rest):
    for source, out in zip(rest[:groups], rest[groups:]):
        out[...] = source[0]


def pick_factors(slots, factor, groups):
    block = factor.shape[1:]
    return pl.pallas_call(
        functools.partial(pick_kernel, groups),
        grid_spec=pltpu.PrefetchScalarGridSpec(
            num_scalar_prefetch=1,
            grid=(1,),
            in_specs=[
                pl.BlockSpec((1, *block), lambda i, slots, d=d: (slots[d], 0, 0))
                for d in range(groups)
            ],
            out_specs=[whole(block)] * groups,
        ),
        out_shape=[jax.ShapeDtypeStruct(block, factor.dtype)] * groups,
        compiler_params=PARAMS,
        cost_estimate=cost(0, 4 * groups * block[0] * block[1]),
        name="pick_factors",
    )(slots, *[pltpu.with_memory_space_constraint(factor, pltpu.HBM)] * groups)


def times_factors(seg_rows, base, spans, rel_ref, rows, held, out_ref):
    for arrived, segs in spans:
        arrived()
        for n in segs:
            at = pl.ds(n * seg_rows, seg_rows)
            out_ref[at, :] = jnp.dot(
                rows[at, :], held[rel_ref[base + n]], preferred_element_type=jnp.float32
            ).astype(out_ref.dtype)


def give_kernel(seg_rows, pieces, flip, rel_ref, halves_ref, rows_ref, *rest):
    groups = len(rest) - (6 if flip else 5)
    blocks, (out_ref, held, *halves), rest = rest[:groups], rest[groups : groups + 4], rest[groups + 4 :]
    raw, sems = rest[0] if flip else held, rest[-1]
    count = halves[0].shape[0]
    piece = count // pieces
    fetches = [pltpu.make_async_copy(blocks[d], raw.at[d], sems.at[d]) for d in range(groups)]
    arrivals = [
        pltpu.make_async_copy(
            rows_ref.at[pl.ds(pl.multiple_of(halves_ref[h] * count + k * piece, seg_rows), piece)],
            halves[h].at[pl.ds(k * piece, piece)],
            sems.at[groups + h * pieces + k],
        )
        for h in range(2)
        for k in range(pieces)
    ]
    for copy in fetches + arrivals:
        copy.start()
    for d, copy in enumerate(fetches):
        copy.wait()
        if flip:
            held[d] = raw[d].T
    segs = piece // seg_rows
    spans = [(arrivals[k].wait, range(k * segs, (k + 1) * segs)) for k in range(pieces)]
    times_factors(seg_rows, halves_ref[0] * segs * pieces, spans, rel_ref, halves[0], held, out_ref)
    for copy in arrivals[pieces:]:
        copy.wait()


def give_rows(rel, halves, rows, blocks, flip):
    groups = len(blocks)
    seg_count = rel.shape[0]
    seg_rows = rows.shape[0] // seg_count
    pieces = seg_count // 2 // step_segments(seg_count // 2, 3)
    count, features = rows.shape[0] // 2, rows.shape[1]
    rank = blocks[0].shape[0 if flip else 1]
    return pl.pallas_call(
        functools.partial(give_kernel, seg_rows, pieces, flip),
        grid_spec=pltpu.PrefetchScalarGridSpec(
            num_scalar_prefetch=2,
            grid=(1,),
            in_specs=[ANY] * (groups + 1),
            out_specs=[whole((count, rank)), HELD, HELD, HELD],
            scratch_shapes=[pltpu.VMEM((groups, *blocks[0].shape), rows.dtype)] * flip
            + [pltpu.SemaphoreType.DMA((groups + 2 * pieces,))],
        ),
        out_shape=[
            jax.ShapeDtypeStruct((count, rank), jnp.bfloat16),
            pltpu.VMEM((groups, features, rank), rows.dtype),
            pltpu.VMEM((count, features), rows.dtype),
            pltpu.VMEM((count, features), rows.dtype),
        ],
        compiler_params=PARAMS,
        cost_estimate=cost(rows.size * rank, 2 * rows.size),
        name="give_rows",
    )(rel, halves, pltpu.with_memory_space_constraint(rows, pltpu.HBM), *blocks)


def keep_kernel(seg_rows, rel_ref, halves_ref, rows, held, out_ref):
    segs = rows.shape[0] // seg_rows
    times_factors(
        seg_rows, halves_ref[1] * segs, [(lambda: None, range(segs))], rel_ref, rows, held, out_ref
    )


def keep_rows(rel, halves, rows, held):
    count, rank = rows.shape[0], held.shape[2]
    return pl.pallas_call(
        functools.partial(keep_kernel, 2 * count // rel.shape[0]),
        grid_spec=pltpu.PrefetchScalarGridSpec(
            num_scalar_prefetch=2,
            grid=(1,),
            in_specs=[HELD, HELD],
            out_specs=whole((count, rank)),
        ),
        out_shape=jax.ShapeDtypeStruct((count, rank), jnp.float32),
        compiler_params=PARAMS,
        cost_estimate=cost(2 * rows.size * rank, 2 * rows.size),
        name="keep_rows",
    )(rel, halves, rows, held)


def hold_kernel(halves_ref, rows_ref, *rest):
    outs, sems = rest[:-1], rest[-1]
    count = outs[0].shape[0]
    copies = [
        pltpu.make_async_copy(
            rows_ref.at[pl.ds(pl.multiple_of(halves_ref[k] * count, 16), count)], out, sems.at[k]
        )
        for k, out in enumerate(outs)
    ]
    for copy in copies:
        copy.start()
    for copy in copies:
        copy.wait()


def hold(halves, rows):
    shape = (rows.shape[0] // 2, rows.shape[1])
    return pl.pallas_call(
        hold_kernel,
        grid_spec=pltpu.PrefetchScalarGridSpec(
            num_scalar_prefetch=1,
            grid=(1,),
            in_specs=[ANY],
            out_specs=[HELD] * 2,
            scratch_shapes=[pltpu.SemaphoreType.DMA((2,))],
        ),
        out_shape=[pltpu.VMEM(shape, rows.dtype)] * 2,
        compiler_params=PARAMS,
        cost_estimate=cost(0, 4 * rows.size),
        name="hold_rows",
    )(halves, pltpu.with_memory_space_constraint(rows, pltpu.HBM))


def from_other_core(parts, block):
    return lax.ppermute(block, "tp", [(i, i ^ 1) for i in range(parts)])


def add_kernel(joined, first_refs, second_refs, out_refs):
    start = 0
    for first, second, out in zip(first_refs, second_refs, out_refs * (2 if joined else 1)):
        at = pl.ds(start, first.shape[0])
        start += first.shape[0] if joined else 0
        out[at, :] = (first[...].astype(jnp.float32) + second[...].astype(jnp.float32)).astype(out.dtype)


def add_rows(first, second, dtype, joined=False):
    def kernel(*refs):
        n = len(first)
        add_kernel(joined, refs[:n], refs[n : 2 * n], refs[2 * n :])

    outs = [jax.ShapeDtypeStruct(block.shape, dtype) for block in first]
    if joined:
        rows = sum(block.shape[0] for block in first)
        outs = [jax.ShapeDtypeStruct((rows, first[0].shape[1]), dtype)]
    return pl.pallas_call(
        kernel,
        out_shape=outs,
        compiler_params=PARAMS,
        cost_estimate=cost(0, 1024),
        name="add_rows",
    )(*first, *second)


def split_kernel(kept_ref, got_ref, *outs):
    start = 0
    for out in outs:
        at = pl.ds(start, out.shape[0])
        out[...] = (kept_ref[at, :] + got_ref[at, :].astype(jnp.float32)).astype(out.dtype)
        start += out.shape[0]


def chip_sums(kept, got, dtype):
    part = jax.ShapeDtypeStruct((kept.shape[0] // 2, kept.shape[1]), dtype)
    return pl.pallas_call(
        split_kernel,
        out_shape=[part, part],
        compiler_params=PARAMS,
        cost_estimate=cost(0, 1024),
        name="chip_sums",
    )(kept, got)


def chip_steps(parts):
    bits = (parts // 2).bit_length() - 1
    return [[(step + part * (bits // 2)) % bits for part in range(2)] for step in range(bits)]


def cross(parts, sums, step):
    return [
        lax.ppermute(block, "tp", [(i, i ^ (2 << bit)) for i in range(parts)])
        for block, bit in zip(sums, step)
    ]


def grad_kernel(groups, seg_rows, flip, rel_ref, halves_ref, *rest):
    lows, halves, rest = rest[:2], rest[2:4], rest[4:]
    outs, (acc, low, sems) = rest[:groups], rest[groups:]
    count = halves[0].shape[0]
    copies = [
        pltpu.make_async_copy(
            lows[k], low.at[pl.ds(pl.multiple_of(halves_ref[k] * count, seg_rows), count)], sems.at[k]
        )
        for k in range(2)
    ]
    for copy in copies:
        copy.start()
    acc[...] = jnp.zeros_like(acc)
    for copy in copies:
        copy.wait()
    segs = count // seg_rows
    unroll = step_segments(segs, 5)
    for k in range(2):
        def add_segments(step, carry, k=k):
            for n in range(unroll):
                at = step * unroll + n
                seg = halves_ref[k] * segs + at
                acc[rel_ref[seg]] += lax.dot_general(
                    low[pl.ds(pl.multiple_of(seg * seg_rows, seg_rows), seg_rows), :],
                    halves[k][pl.ds(pl.multiple_of(at * seg_rows, seg_rows), seg_rows), :],
                    (((0,), (0,)), ((), ())),
                    preferred_element_type=jnp.float32,
                )
            return carry

        lax.fori_loop(0, segs // unroll, add_segments, 0)
    for d in range(groups):
        total = acc[d].astype(jnp.bfloat16)
        outs[d][...] = total.T if flip else total


def group_grads(rel, halves, lows, rows, groups, flip):
    seg_count = rel.shape[0]
    count, features = rows[0].shape
    seg_rows = 2 * count // seg_count
    rank = lows[0].shape[1]
    shape = (features, rank) if flip else (rank, features)
    return pl.pallas_call(
        functools.partial(grad_kernel, groups, seg_rows, flip),
        grid_spec=pltpu.PrefetchScalarGridSpec(
            num_scalar_prefetch=2,
            grid=(1,),
            in_specs=[ANY, ANY, HELD, HELD],
            out_specs=[whole(shape)] * groups,
            scratch_shapes=[
                pltpu.VMEM((groups, rank, features), jnp.float32),
                pltpu.VMEM((2 * count, rank), jnp.bfloat16),
                pltpu.SemaphoreType.DMA((2,)),
            ],
        ),
        out_shape=[jax.ShapeDtypeStruct(shape, jnp.bfloat16)] * groups,
        compiler_params=PARAMS,
        cost_estimate=cost(0, 1024),
        name="group_grads",
    )(rel, halves, *lows, *rows)


def total_kernel(groups, slots_ref, *rest):
    blocks, out_ref, acc = rest[:groups], rest[groups], rest[groups + 1]
    acc[...] = jnp.zeros_like(acc)
    for d in range(groups):
        acc[slots_ref[d]] += blocks[d][...].astype(jnp.float32)
    out_ref[...] = acc[...].astype(out_ref.dtype)


def slot_totals(slots, blocks, owned):
    groups = len(blocks)
    shape = blocks[0].shape
    return pl.pallas_call(
        functools.partial(total_kernel, groups),
        grid_spec=pltpu.PrefetchScalarGridSpec(
            num_scalar_prefetch=1,
            grid=(1,),
            in_specs=[pl.BlockSpec(shape, lambda i, *_: (0, 0))] * groups,
            out_specs=pl.BlockSpec((owned, *shape), lambda i, *_: (0, 0, 0)),
            scratch_shapes=[pltpu.VMEM((owned, *shape), jnp.float32)],
        ),
        out_shape=jax.ShapeDtypeStruct((owned, *shape), jnp.bfloat16),
        compiler_params=PARAMS,
        cost_estimate=cost(groups * blocks[0].size, 2 * (groups + owned) * blocks[0].size),
        name="slot_totals",
    )(slots, *blocks)


def apart(valid, work, *args):
    out = jax.eval_shape(work, *args)
    zeros = lambda *_: jax.tree.map(lambda leaf: jnp.zeros(leaf.shape, leaf.dtype), out)
    return lax.cond(valid, work, zeros, *args)


def body(groups, parts, inputs, cotangent, factor_a, factor_b, adapter_slot, seg_adapter):
    owned = factor_a.shape[0]
    to, back = peers(groups)
    me = lax.axis_index("grp")
    matches = seg_adapter[:, :, None] == jnp.arange(adapter_slot.shape[0], dtype=jnp.int32)
    slot_all = jnp.sum(jnp.where(matches, adapter_slot, 0), axis=2)
    owner_all, local_all = slot_all // owned, slot_all % owned
    my_slots = jnp.max(jnp.where(owner_all == me, local_all, 0), axis=1)
    order = jnp.arange(groups, dtype=jnp.int32)
    slots = jnp.sum(
        jnp.where(to(me, order)[:, None] == order[None, :], my_slots[None, :], 0), axis=1
    )
    my_owners = lax.dynamic_index_in_dim(owner_all, me, 0, keepdims=False)
    rel = jnp.sum(
        jnp.where(my_owners[:, None] == back(me, order)[None, :], order[None, :], 0), axis=1
    )

    valid = me >= 0

    def send(block, d, where):
        return lax.ppermute(block, "grp", [(i, where(i, d)) for i in range(groups)])

    def send_all(blocks, where):
        return [send(block, d, where) for d, block in enumerate(blocks, 1)]

    core = lax.axis_index("tp") % 2
    halves = jnp.stack([1 - core, core])
    steps = chip_steps(parts)
    sent = jnp.bfloat16 if len(steps) <= 2 else jnp.float32
    own_factor_b, *picked_b = pick_factors(slots, factor_b, groups)
    got_b = send_all(picked_b, to)
    own_factor_a, *picked_a = pick_factors(slots, factor_a, groups)
    near_a = send(picked_a[-1], groups - 1, to)
    picked_a, got_b, near_a = lax.optimization_barrier((picked_a[:-1], got_b, near_a))
    far_a = send_all(picked_a, to)

    def first_grad_sums(rel, halves, cotangent, *blocks):
        give, held, _, rows = give_rows(rel, halves, cotangent, blocks, True)
        got = from_other_core(parts, give)
        sums = chip_sums(keep_rows(rel, halves, rows, held), got, sent)
        for step in steps[:-1]:
            sums = add_rows(sums, cross(parts, sums, step), sent)
        return sums

    sums = apart(valid, first_grad_sums, rel, halves, cotangent, own_factor_b, *got_b)
    far_a, sums = lax.optimization_barrier((far_a, sums))
    crossed = cross(parts, sums, steps[-1])
    give, held, *tok = give_rows(rel, halves, inputs, [own_factor_a, *far_a, near_a], False)
    crossed, give = lax.optimization_barrier((crossed, give))
    got = from_other_core(parts, give)
    (low,) = add_rows(sums, crossed, jnp.bfloat16, True)
    other_low = from_other_core(parts, low)
    kept = keep_rows(rel, halves, tok[1], held)
    low, other_low, kept = lax.optimization_barrier((low, other_low, kept))
    own_a, *grads_a = group_grads(rel, halves, [other_low, low], tok, groups, True)
    back_a = send_all(grads_a, back)
    kept, own_a = lax.optimization_barrier((kept, own_a))

    def input_grads(rel, halves, cotangent, kept, got):
        sums = chip_sums(kept, got, sent)
        crossed = cross(parts, sums, steps[0])
        crossed, rows = lax.optimization_barrier((crossed, hold(halves, cotangent)))
        for step in steps[1:]:
            sums = add_rows(sums, crossed, sent)
            crossed = cross(parts, sums, step)
        (low,) = add_rows(sums, crossed, jnp.bfloat16, True)
        return group_grads(rel, halves, [from_other_core(parts, low), low], rows, groups, False)

    own_b, *grads_b = apart(valid, input_grads, rel, halves, cotangent, kept, got)
    grads_b, back_a = lax.optimization_barrier((grads_b, back_a))
    back_b = send_all(grads_b, back)
    grad_a = slot_totals(slots, [own_a, *back_a], owned)
    grad_b = slot_totals(slots, [own_b, *back_b], owned)
    return grad_a, grad_b


def solution(mesh):
    return jax.shard_map(
        functools.partial(body, mesh.shape["grp"], mesh.shape["tp"]),
        mesh=mesh,
        in_specs=(
            P("grp", "tp"),
            P("grp", "tp"),
            P("grp", "tp", None),
            P("grp", None, "tp"),
            P(),
            P(),
        ),
        out_specs=(P("grp", "tp", None), P("grp", None, "tp")),
        check_vma=False,
    )
```

```python
import functools

import jax
import jax.numpy as jnp
from jax import lax
from jax.experimental import pallas as pl
from jax.experimental.pallas import tpu as pltpu
from jax.sharding import PartitionSpec as P

VMEM_LIMIT = 24 * 1024 * 1024
ANY = pl.BlockSpec(memory_space=pl.ANY)
HELD = pl.BlockSpec(memory_space=pltpu.VMEM)
PARAMS = pltpu.CompilerParams(vmem_limit_bytes=VMEM_LIMIT)


def cost(flops, moved):
    return pl.CostEstimate(flops=flops, bytes_accessed=moved, transcendentals=0)


def peers(groups):
    if groups & (groups - 1) == 0:
        across = lambda i, d: i ^ ((groups - d) % groups)
        return across, across
    return (lambda i, d: (i + d) % groups), (lambda i, d: (i + groups - d) % groups)


def step_segments(seg_count, most):
    return max(n for n in range(1, most + 1) if seg_count % n == 0)


def whole(shape):
    return pl.BlockSpec(shape, lambda i, *_: (0,) * len(shape))


def pick_kernel(groups, slots_ref, *rest):
    for source, out in zip(rest[:groups], rest[groups:]):
        out[...] = source[0]


def pick_factors(slots, factor, groups):
    block = factor.shape[1:]
    return pl.pallas_call(
        functools.partial(pick_kernel, groups),
        grid_spec=pltpu.PrefetchScalarGridSpec(
            num_scalar_prefetch=1,
            grid=(1,),
            in_specs=[
                pl.BlockSpec((1, *block), lambda i, slots, d=d: (slots[d], 0, 0))
                for d in range(groups)
            ],
            out_specs=[whole(block)] * groups,
        ),
        out_shape=[jax.ShapeDtypeStruct(block, factor.dtype)] * groups,
        compiler_params=PARAMS,
        cost_estimate=cost(0, 4 * groups * block[0] * block[1]),
        name="pick_factors",
    )(slots, *[pltpu.with_memory_space_constraint(factor, pltpu.HBM)] * groups)


def times_factors(seg_rows, flip, base, spans, rel_ref, rows, held, out_ref):
    contract = (((1,), (1 if flip else 0,)), ((), ()))
    for arrived, segs in spans:
        arrived()
        for n in segs:
            at = pl.ds(n * seg_rows, seg_rows)
            out_ref[at, :] = lax.dot_general(
                rows[at, :], held[rel_ref[base + n]], contract, preferred_element_type=jnp.float32
            ).astype(out_ref.dtype)


def give_kernel(seg_rows, pieces, flip, rel_ref, halves_ref, rows_ref, *rest):
    groups = len(rest) - 5
    blocks, (out_ref, held, *halves), sems = rest[:groups], rest[groups:-1], rest[-1]
    count = halves[0].shape[0]
    piece = count // pieces
    fetches = [pltpu.make_async_copy(blocks[d], held.at[d], sems.at[d]) for d in range(groups)]
    arrivals = [
        pltpu.make_async_copy(
            rows_ref.at[pl.ds(pl.multiple_of(halves_ref[h] * count + k * piece, seg_rows), piece)],
            halves[h].at[pl.ds(k * piece, piece)],
            sems.at[groups + h * pieces + k],
        )
        for h in range(2)
        for k in range(pieces)
    ]
    for copy in fetches + arrivals:
        copy.start()
    for copy in fetches:
        copy.wait()
    segs = piece // seg_rows
    spans = [(arrivals[k].wait, range(k * segs, (k + 1) * segs)) for k in range(pieces)]
    base = halves_ref[0] * segs * pieces
    times_factors(seg_rows, flip, base, spans, rel_ref, halves[0], held, out_ref)
    for copy in arrivals[pieces:]:
        copy.wait()


def give_rows(rel, halves, rows, blocks, flip):
    groups = len(blocks)
    seg_count = rel.shape[0]
    seg_rows = rows.shape[0] // seg_count
    pieces = seg_count // 2 // step_segments(seg_count // 2, 3)
    count, features = rows.shape[0] // 2, rows.shape[1]
    rank = blocks[0].shape[0 if flip else 1]
    return pl.pallas_call(
        functools.partial(give_kernel, seg_rows, pieces, flip),
        grid_spec=pltpu.PrefetchScalarGridSpec(
            num_scalar_prefetch=2,
            grid=(1,),
            in_specs=[ANY] * (groups + 1),
            out_specs=[whole((count, rank)), HELD, HELD, HELD],
            scratch_shapes=[pltpu.SemaphoreType.DMA((groups + 2 * pieces,))],
        ),
        out_shape=[
            jax.ShapeDtypeStruct((count, rank), jnp.bfloat16),
            pltpu.VMEM((groups, *blocks[0].shape), rows.dtype),
            pltpu.VMEM((count, features), rows.dtype),
            pltpu.VMEM((count, features), rows.dtype),
        ],
        compiler_params=PARAMS,
        cost_estimate=cost(rows.size * rank, 2 * rows.size),
        name="give_rows",
    )(rel, halves, pltpu.with_memory_space_constraint(rows, pltpu.HBM), *blocks)


def keep_kernel(seg_rows, flip, rel_ref, halves_ref, rows, held, out_ref):
    segs = rows.shape[0] // seg_rows
    spans = [(lambda: None, range(segs))]
    times_factors(seg_rows, flip, halves_ref[1] * segs, spans, rel_ref, rows, held, out_ref)


def keep_rows(rel, halves, rows, held, flip):
    count, rank = rows.shape[0], held.shape[1 if flip else 2]
    return pl.pallas_call(
        functools.partial(keep_kernel, 2 * count // rel.shape[0], flip),
        grid_spec=pltpu.PrefetchScalarGridSpec(
            num_scalar_prefetch=2,
            grid=(1,),
            in_specs=[HELD, HELD],
            out_specs=whole((count, rank)),
        ),
        out_shape=jax.ShapeDtypeStruct((count, rank), jnp.float32),
        compiler_params=PARAMS,
        cost_estimate=cost(2 * rows.size * rank, 2 * rows.size),
        name="keep_rows",
    )(rel, halves, rows, held)


def hold_kernel(halves_ref, rows_ref, *rest):
    outs, sems = rest[:-1], rest[-1]
    count = outs[0].shape[0]
    copies = [
        pltpu.make_async_copy(
            rows_ref.at[pl.ds(pl.multiple_of(halves_ref[k] * count, 16), count)], out, sems.at[k]
        )
        for k, out in enumerate(outs)
    ]
    for copy in copies:
        copy.start()
    for copy in copies:
        copy.wait()


def hold(halves, rows):
    shape = (rows.shape[0] // 2, rows.shape[1])
    return pl.pallas_call(
        hold_kernel,
        grid_spec=pltpu.PrefetchScalarGridSpec(
            num_scalar_prefetch=1,
            grid=(1,),
            in_specs=[ANY],
            out_specs=[HELD] * 2,
            scratch_shapes=[pltpu.SemaphoreType.DMA((2,))],
        ),
        out_shape=[pltpu.VMEM(shape, rows.dtype)] * 2,
        compiler_params=PARAMS,
        cost_estimate=cost(0, 4 * rows.size),
        name="hold_rows",
    )(halves, pltpu.with_memory_space_constraint(rows, pltpu.HBM))


def from_other_core(parts, block):
    return lax.ppermute(block, "tp", [(i, i ^ 1) for i in range(parts)])


def chip_kernel(sent, kept_ref, got_ref, *outs):
    start = 0
    for n in range(2):
        at = pl.ds(start, outs[n].shape[0])
        start += outs[n].shape[0]
        total = kept_ref[at, :] + got_ref[at, :].astype(jnp.float32)
        outs[n][...] = total
        outs[2 + n][...] = total.astype(sent)


def chip_sums(kept, got, sent):
    shape = (kept.shape[0] // 2, kept.shape[1])
    outs = pl.pallas_call(
        functools.partial(chip_kernel, sent),
        out_shape=[jax.ShapeDtypeStruct(shape, t) for t in (jnp.float32,) * 2 + (sent,) * 2],
        compiler_params=PARAMS,
        cost_estimate=cost(0, 1024),
        name="chip_sums",
    )(kept, got)
    return outs[:2], outs[2:]


def add_kernel(sent, *refs):
    for n in range(2):
        total = refs[n][...] + refs[2 + n][...].astype(jnp.float32)
        refs[4 + n][...] = total
        refs[6 + n][...] = total.astype(sent)


def add_parts(sums, crossed, sent):
    outs = pl.pallas_call(
        functools.partial(add_kernel, sent),
        out_shape=[jax.ShapeDtypeStruct(sums[0].shape, t) for t in (jnp.float32,) * 2 + (sent,) * 2],
        compiler_params=PARAMS,
        cost_estimate=cost(0, 1024),
        name="add_parts",
    )(*sums, *crossed)
    return outs[:2], outs[2:]


def join_kernel(*refs):
    rows = refs[0].shape[0]
    for n in range(2):
        total = refs[n][...] + refs[2 + n][...].astype(jnp.float32)
        refs[4][pl.ds(n * rows, rows), :] = total.astype(refs[4].dtype)


def join_parts(sums, crossed):
    rows, rank = sums[0].shape
    return pl.pallas_call(
        join_kernel,
        out_shape=jax.ShapeDtypeStruct((2 * rows, rank), jnp.bfloat16),
        compiler_params=PARAMS,
        cost_estimate=cost(0, 1024),
        name="join_parts",
    )(*sums, *crossed)


def chip_steps(parts):
    bits = (parts // 2).bit_length() - 1
    return [[(step + part * (bits // 2)) % bits for part in range(2)] for step in range(bits)]


def cross(parts, blocks, step):
    return [
        lax.ppermute(block, "tp", [(i, i ^ (2 << bit)) for i in range(parts)])
        for block, bit in zip(blocks, step)
    ]


def grad_kernel(order, resume, finish, seg_rows, flip, rel_ref, halves_ref, *refs):
    lows, rows, refs = refs[: len(order)], refs[len(order) : 2 * len(order)], refs[2 * len(order) :]
    if resume:
        so_far, refs = refs[0], refs[1:]
    outs, acc = (refs[:-1], refs[-1]) if finish else ((), refs[0])
    acc[...] = so_far[...] if resume else jnp.zeros_like(acc)
    segs = rows[0].shape[0] // seg_rows
    unroll = step_segments(segs, 5)
    for half, low, tokens in zip(order, lows, rows):

        def add_segments(step, carry, half=half, low=low, tokens=tokens):
            for n in range(unroll):
                seg = step * unroll + n
                at = pl.ds(pl.multiple_of(seg * seg_rows, seg_rows), seg_rows)
                acc[rel_ref[halves_ref[half] * segs + seg]] += lax.dot_general(
                    low[at, :],
                    tokens[at, :],
                    (((0,), (0,)), ((), ())),
                    preferred_element_type=jnp.float32,
                )
            return carry

        lax.fori_loop(0, segs // unroll, add_segments, 0)
    for d, out in enumerate(outs):
        total = acc[d].astype(jnp.bfloat16)
        out[...] = total.T if flip else total


def group_grads(rel, halves, order, lows, rows, groups, flip=False, so_far=None, finish=True):
    seg_count = rel.shape[0]
    count, features = rows[0].shape
    rank = lows[0].shape[1]
    shape = (features, rank) if flip else (rank, features)
    sums = pltpu.VMEM((groups, rank, features), jnp.float32)
    earlier = [] if so_far is None else [so_far]
    return pl.pallas_call(
        functools.partial(
            grad_kernel, order, bool(earlier), finish, 2 * count // seg_count, flip
        ),
        grid_spec=pltpu.PrefetchScalarGridSpec(
            num_scalar_prefetch=2,
            grid=(1,),
            in_specs=[HELD] * (2 * len(order) + len(earlier)),
            out_specs=[whole(shape)] * groups if finish else HELD,
            scratch_shapes=[sums] if finish else [],
        ),
        out_shape=[jax.ShapeDtypeStruct(shape, jnp.bfloat16)] * groups if finish else sums,
        compiler_params=PARAMS,
        cost_estimate=cost(0, 1024),
        name="group_grads",
    )(rel, halves, *lows, *rows, *earlier)


def total_kernel(groups, slots_ref, *rest):
    blocks, out_ref, acc = rest[:groups], rest[groups], rest[groups + 1]
    acc[...] = jnp.zeros_like(acc)
    for d in range(groups):
        acc[slots_ref[d]] += blocks[d][...].astype(jnp.float32)
    out_ref[...] = acc[...].astype(out_ref.dtype)


def slot_totals(slots, blocks, owned):
    groups = len(blocks)
    shape = blocks[0].shape
    return pl.pallas_call(
        functools.partial(total_kernel, groups),
        grid_spec=pltpu.PrefetchScalarGridSpec(
            num_scalar_prefetch=1,
            grid=(1,),
            in_specs=[pl.BlockSpec(shape, lambda i, *_: (0, 0))] * groups,
            out_specs=pl.BlockSpec((owned, *shape), lambda i, *_: (0, 0, 0)),
            scratch_shapes=[pltpu.VMEM((owned, *shape), jnp.float32)],
        ),
        out_shape=jax.ShapeDtypeStruct((owned, *shape), jnp.bfloat16),
        compiler_params=PARAMS,
        cost_estimate=cost(groups * blocks[0].size, 2 * (groups + owned) * blocks[0].size),
        name="slot_totals",
    )(slots, *blocks)


def apart(valid, work, *args):
    out = jax.eval_shape(work, *args)
    zeros = lambda *_: jax.tree.map(lambda leaf: jnp.zeros(leaf.shape, leaf.dtype), out)
    return lax.cond(valid, work, zeros, *args)


def body(groups, parts, inputs, cotangent, factor_a, factor_b, adapter_slot, seg_adapter):
    owned = factor_a.shape[0]
    to, back = peers(groups)
    me = lax.axis_index("grp")
    matches = seg_adapter[:, :, None] == jnp.arange(adapter_slot.shape[0], dtype=jnp.int32)
    slot_all = jnp.sum(jnp.where(matches, adapter_slot, 0), axis=2)
    owner_all, local_all = slot_all // owned, slot_all % owned
    my_slots = jnp.max(jnp.where(owner_all == me, local_all, 0), axis=1)
    order = jnp.arange(groups, dtype=jnp.int32)
    slots = jnp.sum(
        jnp.where(to(me, order)[:, None] == order[None, :], my_slots[None, :], 0), axis=1
    )
    my_owners = lax.dynamic_index_in_dim(owner_all, me, 0, keepdims=False)
    rel = jnp.sum(
        jnp.where(my_owners[:, None] == back(me, order)[None, :], order[None, :], 0), axis=1
    )

    valid = me >= 0

    def send(block, d, where):
        return lax.ppermute(block, "grp", [(i, where(i, d)) for i in range(groups)])

    def send_all(blocks, where):
        return [send(block, d, where) for d, block in enumerate(blocks, 1)]

    core = lax.axis_index("tp") % 2
    halves = jnp.stack([1 - core, core])
    steps = chip_steps(parts)
    sent = jnp.bfloat16 if len(steps) <= 2 else jnp.float32
    own_factor_b, *picked_b = pick_factors(slots, factor_b, groups)
    got_b = send_all(picked_b, to)
    own_factor_a, *picked_a = pick_factors(slots, factor_a, groups)
    near_a = send(picked_a[-1], groups - 1, to)
    picked_a, got_b = lax.optimization_barrier((picked_a[:-1], got_b))
    far_a = send_all(picked_a, to)

    def first_grad_sums(rel, halves, cotangent, *blocks):
        give, held, _, rows = give_rows(rel, halves, cotangent, blocks, True)
        got = from_other_core(parts, give)
        sums, out = chip_sums(keep_rows(rel, halves, rows, held, True), got, sent)
        for step in steps[:-1]:
            sums, out = add_parts(sums, cross(parts, out, step), sent)
        return sums, out

    sums, out = apart(valid, first_grad_sums, rel, halves, cotangent, own_factor_b, *got_b)
    crossed = cross(parts, out, steps[-1])
    give, held, *tok = give_rows(rel, halves, inputs, [own_factor_a, *far_a, near_a], False)
    crossed, give = lax.optimization_barrier((crossed, give))
    got = from_other_core(parts, give)
    low = join_parts(sums, crossed)
    other_low = from_other_core(parts, low)
    kept = keep_rows(rel, halves, tok[1], held, False)
    low, other_low, kept = lax.optimization_barrier((low, other_low, kept))
    own_a, *grads_a = group_grads(rel, halves, (1, 0), [low, other_low], tok[::-1], groups, True)
    back_a = send_all(grads_a, back)
    kept, own_a = lax.optimization_barrier((kept, own_a))

    def input_grads(rel, halves, cotangent, kept, got):
        sums, out = chip_sums(kept, got, sent)
        crossed = cross(parts, out, steps[0])
        crossed, rows = lax.optimization_barrier((crossed, hold(halves, cotangent)))
        for step in steps[1:]:
            sums, out = add_parts(sums, crossed, sent)
            crossed = cross(parts, out, step)
        low = join_parts(sums, crossed)
        other_low = from_other_core(parts, low)
        first = group_grads(rel, halves, (1,), [low], rows[1:], groups, finish=False)
        return group_grads(rel, halves, (0,), [other_low], rows[:1], groups, so_far=first)

    own_b, *grads_b = apart(valid, input_grads, rel, halves, cotangent, kept, got)
    grads_b, back_a = lax.optimization_barrier((grads_b, back_a))
    back_b = send_all(grads_b, back)
    grad_a = slot_totals(slots, [own_a, *back_a], owned)
    grad_b = slot_totals(slots, [own_b, *back_b], owned)
    return grad_a, grad_b


def solution(mesh):
    return jax.shard_map(
        functools.partial(body, mesh.shape["grp"], mesh.shape["tp"]),
        mesh=mesh,
        in_specs=(
            P("grp", "tp"),
            P("grp", "tp"),
            P("grp", "tp", None),
            P("grp", None, "tp"),
            P(),
            P(),
        ),
        out_specs=(P("grp", "tp", None), P("grp", None, "tp")),
        check_vma=False,
    )
```

```python
import functools

import jax
import jax.numpy as jnp
from jax import lax
from jax.experimental import pallas as pl
from jax.experimental.pallas import tpu as pltpu
from jax.sharding import PartitionSpec as P

VMEM_LIMIT = 24 * 1024 * 1024
ANY = pl.BlockSpec(memory_space=pl.ANY)
HELD = pl.BlockSpec(memory_space=pltpu.VMEM)
PARAMS = pltpu.CompilerParams(vmem_limit_bytes=VMEM_LIMIT)


def cost(flops, moved):
    return pl.CostEstimate(flops=flops, bytes_accessed=moved, transcendentals=0)


def peers(groups):
    if groups & (groups - 1) == 0:
        across = lambda i, d: i ^ ((groups - d) % groups)
        return across, across
    return (lambda i, d: (i + d) % groups), (lambda i, d: (i + groups - d) % groups)


def step_segments(seg_count, most):
    return max(n for n in range(1, most + 1) if seg_count % n == 0)


def whole(shape):
    return pl.BlockSpec(shape, lambda i, *_: (0,) * len(shape))


def pick_kernel(groups, slots_ref, *rest):
    for source, out in zip(rest[:groups], rest[groups:]):
        out[...] = source[0]


def pick_factors(slots, factor, groups):
    block = factor.shape[1:]
    return pl.pallas_call(
        functools.partial(pick_kernel, groups),
        grid_spec=pltpu.PrefetchScalarGridSpec(
            num_scalar_prefetch=1,
            grid=(1,),
            in_specs=[
                pl.BlockSpec((1, *block), lambda i, slots, d=d: (slots[d], 0, 0))
                for d in range(groups)
            ],
            out_specs=[whole(block)] * groups,
        ),
        out_shape=[jax.ShapeDtypeStruct(block, factor.dtype)] * groups,
        compiler_params=PARAMS,
        cost_estimate=cost(0, 4 * groups * block[0] * block[1]),
        name="pick_factors",
    )(slots, *[pltpu.with_memory_space_constraint(factor, pltpu.HBM)] * groups)


def times_factors(seg_rows, flip, base, spans, rel_ref, rows, held, out_ref):
    contract = (((1,), (1 if flip else 0,)), ((), ()))
    for arrived, segs in spans:
        arrived()
        for n in segs:
            at = pl.ds(n * seg_rows, seg_rows)
            out_ref[at, :] = lax.dot_general(
                rows[at, :], held[rel_ref[base + n]], contract, preferred_element_type=jnp.float32
            ).astype(out_ref.dtype)


def give_kernel(seg_rows, pieces, flip, rel_ref, halves_ref, rows_ref, *rest):
    groups = len(rest) - 5
    blocks, (out_ref, held, second, first, sems) = rest[:groups], rest[groups:]
    count = first.shape[0]
    piece = count // pieces
    fetches = [pltpu.make_async_copy(blocks[d], held.at[d], sems.at[d]) for d in range(groups)]
    arrivals = [
        pltpu.make_async_copy(
            rows_ref.at[pl.ds(pl.multiple_of(halves_ref[h] * count + k * piece, seg_rows), piece)],
            half.at[pl.ds(k * piece, piece)],
            sems.at[groups + h * pieces + k],
        )
        for h, half in enumerate((first, second))
        for k in range(pieces)
    ]
    for copy in fetches + arrivals:
        copy.start()
    for copy in fetches:
        copy.wait()
    segs = piece // seg_rows
    spans = [(arrivals[k].wait, range(k * segs, (k + 1) * segs)) for k in range(pieces)]
    base = halves_ref[0] * segs * pieces
    times_factors(seg_rows, flip, base, spans, rel_ref, first, held, out_ref)
    for copy in arrivals[pieces:]:
        copy.wait()


def give_rows(rel, halves, rows, blocks, flip):
    groups = len(blocks)
    seg_count = rel.shape[0]
    seg_rows = rows.shape[0] // seg_count
    pieces = seg_count // 2 // step_segments(seg_count // 2, 3)
    half = pltpu.VMEM((rows.shape[0] // 2, rows.shape[1]), rows.dtype)
    shape = (rows.shape[0] // 2, blocks[0].shape[0 if flip else 1])
    return pl.pallas_call(
        functools.partial(give_kernel, seg_rows, pieces, flip),
        grid_spec=pltpu.PrefetchScalarGridSpec(
            num_scalar_prefetch=2,
            grid=(1,),
            in_specs=[ANY] * (groups + 1),
            out_specs=[whole(shape), HELD, HELD],
            scratch_shapes=[half, pltpu.SemaphoreType.DMA((groups + 2 * pieces,))],
        ),
        out_shape=[
            jax.ShapeDtypeStruct(shape, jnp.bfloat16),
            pltpu.VMEM((groups, *blocks[0].shape), rows.dtype),
            half,
        ],
        compiler_params=PARAMS,
        cost_estimate=cost(rows.size * shape[1], 2 * rows.size),
        name="give_rows",
    )(rel, halves, pltpu.with_memory_space_constraint(rows, pltpu.HBM), *blocks)


def give_held_kernel(seg_rows, flip, rel_ref, halves_ref, rows, *rest):
    blocks, (out_ref, held, sems) = rest[:-3], rest[-3:]
    fetches = [pltpu.make_async_copy(block, held.at[d], sems.at[d]) for d, block in enumerate(blocks)]
    for copy in fetches:
        copy.start()
    for copy in fetches:
        copy.wait()
    segs = rows.shape[0] // seg_rows
    spans = [(lambda: None, range(segs))]
    times_factors(seg_rows, flip, halves_ref[0] * segs, spans, rel_ref, rows, held, out_ref)


def give_held_rows(rel, halves, rows, blocks, flip):
    groups = len(blocks)
    shape = (rows.shape[0], blocks[0].shape[0 if flip else 1])
    return pl.pallas_call(
        functools.partial(give_held_kernel, 2 * rows.shape[0] // rel.shape[0], flip),
        grid_spec=pltpu.PrefetchScalarGridSpec(
            num_scalar_prefetch=2,
            grid=(1,),
            in_specs=[HELD] + [ANY] * groups,
            out_specs=[whole(shape), HELD],
            scratch_shapes=[pltpu.SemaphoreType.DMA((groups,))],
        ),
        out_shape=[
            jax.ShapeDtypeStruct(shape, jnp.bfloat16),
            pltpu.VMEM((groups, *blocks[0].shape), rows.dtype),
        ],
        compiler_params=PARAMS,
        cost_estimate=cost(2 * rows.size * shape[1], 2 * rows.size),
        name="give_held_rows",
    )(rel, halves, rows, *blocks)


def keep_kernel(seg_rows, flip, rel_ref, halves_ref, rows, held, out_ref):
    segs = rows.shape[0] // seg_rows
    spans = [(lambda: None, range(segs))]
    times_factors(seg_rows, flip, halves_ref[1] * segs, spans, rel_ref, rows, held, out_ref)


def keep_rows(rel, halves, rows, held, flip):
    count, rank = rows.shape[0], held.shape[1 if flip else 2]
    return pl.pallas_call(
        functools.partial(keep_kernel, 2 * count // rel.shape[0], flip),
        grid_spec=pltpu.PrefetchScalarGridSpec(
            num_scalar_prefetch=2,
            grid=(1,),
            in_specs=[HELD, HELD],
            out_specs=whole((count, rank)),
        ),
        out_shape=jax.ShapeDtypeStruct((count, rank), jnp.float32),
        compiler_params=PARAMS,
        cost_estimate=cost(2 * rows.size * rank, 2 * rows.size),
        name="keep_rows",
    )(rel, halves, rows, held)


def hold_kernel(halves_ref, rows_ref, *rest):
    outs, sems = rest[:-1], rest[-1]
    count = outs[0].shape[0]
    copies = [
        pltpu.make_async_copy(
            rows_ref.at[pl.ds(pl.multiple_of(halves_ref[k] * count, 16), count)], out, sems.at[k]
        )
        for k, out in enumerate(outs)
    ]
    for copy in copies:
        copy.start()
    for copy in copies:
        copy.wait()


def hold(halves, rows):
    shape = (rows.shape[0] // 2, rows.shape[1])
    return pl.pallas_call(
        hold_kernel,
        grid_spec=pltpu.PrefetchScalarGridSpec(
            num_scalar_prefetch=1,
            grid=(1,),
            in_specs=[ANY],
            out_specs=[HELD] * 2,
            scratch_shapes=[pltpu.SemaphoreType.DMA((2,))],
        ),
        out_shape=[pltpu.VMEM(shape, rows.dtype)] * 2,
        compiler_params=PARAMS,
        cost_estimate=cost(0, 4 * rows.size),
        name="hold_rows",
    )(halves, pltpu.with_memory_space_constraint(rows, pltpu.HBM))


def from_other_core(parts, block):
    return lax.ppermute(block, "tp", [(i, i ^ 1) for i in range(parts)])


def chip_kernel(sent, kept_ref, got_ref, *outs):
    start = 0
    for n in range(2):
        at = pl.ds(start, outs[n].shape[0])
        start += outs[n].shape[0]
        total = kept_ref[at, :] + got_ref[at, :].astype(jnp.float32)
        outs[n][...] = total
        outs[2 + n][...] = total.astype(sent)


def chip_sums(kept, got, sent):
    shape = (kept.shape[0] // 2, kept.shape[1])
    outs = pl.pallas_call(
        functools.partial(chip_kernel, sent),
        out_shape=[jax.ShapeDtypeStruct(shape, t) for t in (jnp.float32,) * 2 + (sent,) * 2],
        compiler_params=PARAMS,
        cost_estimate=cost(0, 1024),
        name="chip_sums",
    )(kept, got)
    return outs[:2], outs[2:]


def add_kernel(sent, *refs):
    for n in range(2):
        total = refs[n][...] + refs[2 + n][...].astype(jnp.float32)
        refs[4 + n][...] = total
        refs[6 + n][...] = total.astype(sent)


def add_parts(sums, crossed, sent):
    outs = pl.pallas_call(
        functools.partial(add_kernel, sent),
        out_shape=[jax.ShapeDtypeStruct(sums[0].shape, t) for t in (jnp.float32,) * 2 + (sent,) * 2],
        compiler_params=PARAMS,
        cost_estimate=cost(0, 1024),
        name="add_parts",
    )(*sums, *crossed)
    return outs[:2], outs[2:]


def join_kernel(*refs):
    rows = refs[0].shape[0]
    for n in range(2):
        total = refs[n][...] + refs[2 + n][...].astype(jnp.float32)
        refs[4][pl.ds(n * rows, rows), :] = total.astype(refs[4].dtype)


def join_parts(sums, crossed):
    rows, rank = sums[0].shape
    return pl.pallas_call(
        join_kernel,
        out_shape=jax.ShapeDtypeStruct((2 * rows, rank), jnp.bfloat16),
        compiler_params=PARAMS,
        cost_estimate=cost(0, 1024),
        name="join_parts",
    )(*sums, *crossed)


def chip_steps(parts):
    bits = (parts // 2).bit_length() - 1
    return [[(step + part * (bits // 2)) % bits for part in range(2)] for step in range(bits)]


def cross(parts, blocks, step):
    return [
        lax.ppermute(block, "tp", [(i, i ^ (2 << bit)) for i in range(parts)])
        for block, bit in zip(blocks, step)
    ]


def grad_kernel(order, resume, finish, seg_rows, flip, rel_ref, halves_ref, *refs):
    lows, rows, refs = refs[: len(order)], refs[len(order) : 2 * len(order)], refs[2 * len(order) :]
    if resume:
        so_far, refs = refs[0], refs[1:]
    outs, acc = (refs[:-1], refs[-1]) if finish else ((), refs[0])
    acc[...] = so_far[...] if resume else jnp.zeros_like(acc)
    segs = rows[0].shape[0] // seg_rows
    unroll = step_segments(segs, 5)
    for half, low, tokens in zip(order, lows, rows):

        def add_segments(step, carry, half=half, low=low, tokens=tokens):
            for n in range(unroll):
                seg = step * unroll + n
                at = pl.ds(pl.multiple_of(seg * seg_rows, seg_rows), seg_rows)
                acc[rel_ref[halves_ref[half] * segs + seg]] += lax.dot_general(
                    low[at, :],
                    tokens[at, :],
                    (((0,), (0,)), ((), ())),
                    preferred_element_type=jnp.float32,
                )
            return carry

        lax.fori_loop(0, segs // unroll, add_segments, 0)
    for d, out in enumerate(outs):
        total = acc[d].astype(jnp.bfloat16)
        out[...] = total.T if flip else total


def group_grads(rel, halves, order, lows, rows, groups, flip=False, so_far=None, finish=True):
    seg_count = rel.shape[0]
    count, features = rows[0].shape
    rank = lows[0].shape[1]
    shape = (features, rank) if flip else (rank, features)
    sums = pltpu.VMEM((groups, rank, features), jnp.float32)
    earlier = [] if so_far is None else [so_far]
    return pl.pallas_call(
        functools.partial(
            grad_kernel, order, bool(earlier), finish, 2 * count // seg_count, flip
        ),
        grid_spec=pltpu.PrefetchScalarGridSpec(
            num_scalar_prefetch=2,
            grid=(1,),
            in_specs=[HELD] * (2 * len(order) + len(earlier)),
            out_specs=[whole(shape)] * groups if finish else HELD,
            scratch_shapes=[sums] if finish else [],
        ),
        out_shape=[jax.ShapeDtypeStruct(shape, jnp.bfloat16)] * groups if finish else sums,
        compiler_params=PARAMS,
        cost_estimate=cost(0, 1024),
        name="group_grads",
    )(rel, halves, *lows, *rows, *earlier)


def total_kernel(groups, slots_ref, *rest):
    blocks, out_ref, acc = rest[:groups], rest[groups], rest[groups + 1]
    acc[...] = jnp.zeros_like(acc)
    for d in range(groups):
        acc[slots_ref[d]] += blocks[d][...].astype(jnp.float32)
    out_ref[...] = acc[...].astype(out_ref.dtype)


def slot_totals(slots, blocks, owned):
    groups = len(blocks)
    shape = blocks[0].shape
    return pl.pallas_call(
        functools.partial(total_kernel, groups),
        grid_spec=pltpu.PrefetchScalarGridSpec(
            num_scalar_prefetch=1,
            grid=(1,),
            in_specs=[HELD] * groups,
            out_specs=pl.BlockSpec((owned, *shape), lambda i, *_: (0, 0, 0)),
            scratch_shapes=[pltpu.VMEM((owned, *shape), jnp.float32)],
        ),
        out_shape=jax.ShapeDtypeStruct((owned, *shape), jnp.bfloat16),
        compiler_params=PARAMS,
        cost_estimate=cost(groups * blocks[0].size, 2 * (groups + owned) * blocks[0].size),
        name="slot_totals",
    )(slots, *blocks)


def apart(valid, work, *args):
    out = jax.eval_shape(work, *args)
    zeros = lambda *_: jax.tree.map(lambda leaf: jnp.zeros(leaf.shape, leaf.dtype), out)
    return lax.cond(valid, work, zeros, *args)


def body(groups, parts, inputs, cotangent, factor_a, factor_b, adapter_slot, seg_adapter):
    owned = factor_a.shape[0]
    to, back = peers(groups)
    me = lax.axis_index("grp")
    matches = seg_adapter[:, :, None] == jnp.arange(adapter_slot.shape[0], dtype=jnp.int32)
    slot_all = jnp.sum(jnp.where(matches, adapter_slot, 0), axis=2)
    owner_all, local_all = slot_all // owned, slot_all % owned
    my_slots = jnp.max(jnp.where(owner_all == me, local_all, 0), axis=1)
    order = jnp.arange(groups, dtype=jnp.int32)
    slots = jnp.sum(
        jnp.where(to(me, order)[:, None] == order[None, :], my_slots[None, :], 0), axis=1
    )
    my_owners = lax.dynamic_index_in_dim(owner_all, me, 0, keepdims=False)
    rel = jnp.sum(
        jnp.where(my_owners[:, None] == back(me, order)[None, :], order[None, :], 0), axis=1
    )

    valid = me >= 0

    def send(block, d, where):
        return lax.ppermute(block, "grp", [(i, where(i, d)) for i in range(groups)])

    def send_all(blocks, where):
        return [send(block, d, where) for d, block in enumerate(blocks, 1)]

    core = lax.axis_index("tp") % 2
    halves = jnp.stack([1 - core, core])
    steps = chip_steps(parts)
    sent = jnp.bfloat16 if len(steps) <= 2 else jnp.float32
    own_factor_b, *picked_b = pick_factors(slots, factor_b, groups)
    got_b = send_all(picked_b, to)
    own_factor_a, *picked_a = pick_factors(slots, factor_a, groups)
    near_a = send(picked_a[-1], groups - 1, to)
    picked_a, got_b = lax.optimization_barrier((picked_a[:-1], got_b))
    far_a = send_all(picked_a, to)

    def first_grad_sums(rel, halves, cotangent, *blocks):
        give, held, rows = give_rows(rel, halves, cotangent, blocks, True)
        got = from_other_core(parts, give)
        sums, out = chip_sums(keep_rows(rel, halves, rows, held, True), got, sent)
        for step in steps[:-1]:
            sums, out = add_parts(sums, cross(parts, out, step), sent)
        return sums, out

    sums, out = apart(valid, first_grad_sums, rel, halves, cotangent, own_factor_b, *got_b)
    later_halves, out = lax.optimization_barrier((halves, out))
    tok = hold(later_halves, inputs)
    crossed = cross(parts, out, steps[-1])
    tok, far_a, near_a = lax.optimization_barrier((tok, far_a, near_a))
    blocks_a = [own_factor_a, *far_a, near_a]
    give, held = give_held_rows(rel, halves, tok[0], blocks_a, False)
    crossed, give = lax.optimization_barrier((crossed, give))
    got = from_other_core(parts, give)
    low = join_parts(sums, crossed)
    other_low = from_other_core(parts, low)
    kept = keep_rows(rel, halves, tok[1], held, False)
    low, other_low, kept = lax.optimization_barrier((low, other_low, kept))
    own_a, *grads_a = group_grads(rel, halves, (1, 0), [low, other_low], tok[::-1], groups, True)
    back_a = send_all(grads_a, back)
    kept, own_a = lax.optimization_barrier((kept, own_a))

    def input_grads(rel, halves, cotangent, kept, got):
        sums, out = chip_sums(kept, got, sent)
        crossed = cross(parts, out, steps[0])
        crossed, rows = lax.optimization_barrier((crossed, hold(halves, cotangent)))
        for step in steps[1:]:
            sums, out = add_parts(sums, crossed, sent)
            crossed = cross(parts, out, step)
        low = join_parts(sums, crossed)
        other_low = from_other_core(parts, low)
        first = group_grads(rel, halves, (1,), [low], rows[1:], groups, finish=False)
        return group_grads(rel, halves, (0,), [other_low], rows[:1], groups, so_far=first)

    own_b, *grads_b = apart(valid, input_grads, rel, halves, cotangent, kept, got)
    grads_b, back_a = lax.optimization_barrier((grads_b, back_a))
    back_b = send_all(grads_b, back)
    grad_a = slot_totals(slots, [own_a, *back_a], owned)
    grad_b = slot_totals(slots, [own_b, *back_b], owned)
    return grad_a, grad_b


def solution(mesh):
    return jax.shard_map(
        functools.partial(body, mesh.shape["grp"], mesh.shape["tp"]),
        mesh=mesh,
        in_specs=(
            P("grp", "tp"),
            P("grp", "tp"),
            P("grp", "tp", None),
            P("grp", None, "tp"),
            P(),
            P(),
        ),
        out_specs=(P("grp", "tp", None), P("grp", None, "tp")),
        check_vma=False,
    )
```

```python
import functools

import jax
import jax.numpy as jnp
from jax import lax
from jax.experimental import pallas as pl
from jax.experimental.pallas import tpu as pltpu
from jax.sharding import PartitionSpec as P

VMEM_LIMIT = 24 * 1024 * 1024
TOGETHER = 2
ANY = pl.BlockSpec(memory_space=pl.ANY)
HELD = pl.BlockSpec(memory_space=pltpu.VMEM)
PARAMS = pltpu.CompilerParams(vmem_limit_bytes=VMEM_LIMIT)


def cost(flops, moved):
    return pl.CostEstimate(flops=flops, bytes_accessed=moved, transcendentals=0)


def peers(groups):
    if groups & (groups - 1) == 0:
        across = lambda i, d: i ^ ((groups - d) % groups)
        return across, across
    return (lambda i, d: (i + d) % groups), (lambda i, d: (i + groups - d) % groups)


def whole(shape):
    return pl.BlockSpec(shape, lambda i, *_: (0,) * len(shape))


def pick_kernel(groups, slots_ref, *rest):
    for source, out in zip(rest[:groups], rest[groups:]):
        out[...] = source[0]


def pick_factors(slots, factor, groups):
    block = factor.shape[1:]
    return pl.pallas_call(
        functools.partial(pick_kernel, groups),
        grid_spec=pltpu.PrefetchScalarGridSpec(
            num_scalar_prefetch=1,
            grid=(1,),
            in_specs=[
                pl.BlockSpec((1, *block), lambda i, slots, d=d: (slots[d], 0, 0))
                for d in range(groups)
            ],
            out_specs=[whole(block)] * groups,
        ),
        out_shape=[jax.ShapeDtypeStruct(block, factor.dtype)] * groups,
        compiler_params=PARAMS,
        cost_estimate=cost(0, 4 * groups * block[0] * block[1]),
        name="pick_factors",
    )(slots, *[pltpu.with_memory_space_constraint(factor, pltpu.HBM)] * groups)


def spans_of(bounds_ref, half, groups, d):
    first, last = bounds_ref[half * (groups + 1) + d], bounds_ref[half * (groups + 1) + d + 1]
    return first, last, lax.div(last - first + (TOGETHER - 1), TOGETHER)


def step_rows(first, last, step, seg_rows, places):
    own = first + step * TOGETHER
    start = jnp.minimum(own, places - TOGETHER)
    row = lax.broadcasted_iota(jnp.int32, (TOGETHER * seg_rows, 1), 0)
    mask = (row >= (own - start) * seg_rows) & (row < (last - start) * seg_rows)
    return pl.ds(pl.multiple_of(start * seg_rows, seg_rows), TOGETHER * seg_rows), mask


def times_factors(seg_rows, flip, half, bounds_ref, rows, held, out_ref):
    contract = (((1,), (1 if flip else 0,)), ((), ()))
    groups, places = held.shape[0], rows.shape[0] // seg_rows
    for d in range(groups):
        first, last, steps = spans_of(bounds_ref, half, groups, d)

        def multiply(step, carry, d=d, first=first, last=last):
            at, mask = step_rows(first, last, step, seg_rows, places)
            product = lax.dot_general(
                rows[at, :], held[d], contract, preferred_element_type=jnp.float32
            )
            earlier = out_ref[at, :].astype(jnp.float32)
            out_ref[at, :] = jnp.where(mask, product, earlier).astype(out_ref.dtype)
            return carry

        lax.fori_loop(0, steps, multiply, 0)


def segment_copies(seg_rows, half, place_ref, rows_ref, out, sems, first_sem):
    places = out.shape[0] // seg_rows

    def copy(n):
        seg = half * places + n
        return pltpu.make_async_copy(
            rows_ref.at[pl.ds(pl.multiple_of(seg * seg_rows, seg_rows), seg_rows)],
            out.at[pl.ds(pl.multiple_of(place_ref[seg] * seg_rows, seg_rows), seg_rows)],
            sems.at[first_sem + n],
        )

    return [copy(n) for n in range(places)]


def give_kernel(seg_rows, flip, place_ref, bounds_ref, halves_ref, rows_ref, *rest):
    groups = len(rest) - 5
    blocks, (out_ref, held, second, first, sems) = rest[:groups], rest[groups:]
    places = first.shape[0] // seg_rows
    fetches = [pltpu.make_async_copy(blocks[d], held.at[d], sems.at[d]) for d in range(groups)]
    fetches += segment_copies(seg_rows, halves_ref[0], place_ref, rows_ref, first, sems, groups)
    later = segment_copies(
        seg_rows, halves_ref[1], place_ref, rows_ref, second, sems, groups + places
    )
    for copy in fetches + later:
        copy.start()
    for copy in fetches:
        copy.wait()
    times_factors(seg_rows, flip, halves_ref[0], bounds_ref, first, held, out_ref)
    for copy in later:
        copy.wait()


def give_rows(tables, halves, rows, blocks, flip):
    groups, seg_count = len(blocks), tables[0].shape[0]
    seg_rows = rows.shape[0] // seg_count
    half = pltpu.VMEM((rows.shape[0] // 2, rows.shape[1]), rows.dtype)
    shape = (rows.shape[0] // 2, blocks[0].shape[0 if flip else 1])
    return pl.pallas_call(
        functools.partial(give_kernel, seg_rows, flip),
        grid_spec=pltpu.PrefetchScalarGridSpec(
            num_scalar_prefetch=3,
            grid=(1,),
            in_specs=[ANY] * (groups + 1),
            out_specs=[whole(shape), HELD, HELD],
            scratch_shapes=[half, pltpu.SemaphoreType.DMA((groups + seg_count,))],
        ),
        out_shape=[
            jax.ShapeDtypeStruct(shape, jnp.bfloat16),
            pltpu.VMEM((groups, *blocks[0].shape), rows.dtype),
            half,
        ],
        compiler_params=PARAMS,
        cost_estimate=cost(rows.size * shape[1], 2 * rows.size),
        name="give_rows",
    )(*tables, halves, pltpu.with_memory_space_constraint(rows, pltpu.HBM), *blocks)


def give_held_kernel(seg_rows, flip, bounds_ref, halves_ref, rows, *rest):
    blocks, (out_ref, held, sems) = rest[:-3], rest[-3:]
    fetches = [pltpu.make_async_copy(block, held.at[d], sems.at[d]) for d, block in enumerate(blocks)]
    for copy in fetches:
        copy.start()
    for copy in fetches:
        copy.wait()
    times_factors(seg_rows, flip, halves_ref[0], bounds_ref, rows, held, out_ref)


def give_held_rows(tables, halves, rows, blocks, flip):
    groups = len(blocks)
    shape = (rows.shape[0], blocks[0].shape[0 if flip else 1])
    return pl.pallas_call(
        functools.partial(give_held_kernel, 2 * rows.shape[0] // tables[0].shape[0], flip),
        grid_spec=pltpu.PrefetchScalarGridSpec(
            num_scalar_prefetch=2,
            grid=(1,),
            in_specs=[HELD] + [ANY] * groups,
            out_specs=[whole(shape), HELD],
            scratch_shapes=[pltpu.SemaphoreType.DMA((groups,))],
        ),
        out_shape=[
            jax.ShapeDtypeStruct(shape, jnp.bfloat16),
            pltpu.VMEM((groups, *blocks[0].shape), rows.dtype),
        ],
        compiler_params=PARAMS,
        cost_estimate=cost(2 * rows.size * shape[1], 2 * rows.size),
        name="give_held_rows",
    )(tables[1], halves, rows, *blocks)


def keep_kernel(seg_rows, flip, bounds_ref, halves_ref, rows, held, out_ref):
    times_factors(seg_rows, flip, halves_ref[1], bounds_ref, rows, held, out_ref)


def keep_rows(tables, halves, rows, held, flip):
    count, rank = rows.shape[0], held.shape[1 if flip else 2]
    return pl.pallas_call(
        functools.partial(keep_kernel, 2 * count // tables[0].shape[0], flip),
        grid_spec=pltpu.PrefetchScalarGridSpec(
            num_scalar_prefetch=2,
            grid=(1,),
            in_specs=[HELD, HELD],
            out_specs=whole((count, rank)),
        ),
        out_shape=jax.ShapeDtypeStruct((count, rank), jnp.float32),
        compiler_params=PARAMS,
        cost_estimate=cost(2 * rows.size * rank, 2 * rows.size),
        name="keep_rows",
    )(tables[1], halves, rows, held)


def hold_kernel(seg_rows, place_ref, halves_ref, rows_ref, *rest):
    outs, sems = rest[:-1], rest[-1]
    copies = []
    for k, out in enumerate(outs):
        copies += segment_copies(
            seg_rows, halves_ref[k], place_ref, rows_ref, out, sems, len(copies)
        )
    for copy in copies:
        copy.start()
    for copy in copies:
        copy.wait()


def hold(tables, halves, rows):
    seg_count = tables[0].shape[0]
    half = pltpu.VMEM((rows.shape[0] // 2, rows.shape[1]), rows.dtype)
    return pl.pallas_call(
        functools.partial(hold_kernel, rows.shape[0] // seg_count),
        grid_spec=pltpu.PrefetchScalarGridSpec(
            num_scalar_prefetch=2,
            grid=(1,),
            in_specs=[ANY],
            out_specs=[HELD] * 2,
            scratch_shapes=[pltpu.SemaphoreType.DMA((seg_count,))],
        ),
        out_shape=[half] * 2,
        compiler_params=PARAMS,
        cost_estimate=cost(0, 4 * rows.size),
        name="hold_rows",
    )(tables[0], halves, pltpu.with_memory_space_constraint(rows, pltpu.HBM))


def from_other_core(parts, block):
    return lax.ppermute(block, "tp", [(i, i ^ 1) for i in range(parts)])


def chip_kernel(sent, kept_ref, got_ref, *outs):
    start = 0
    for n in range(2):
        at = pl.ds(start, outs[n].shape[0])
        start += outs[n].shape[0]
        total = kept_ref[at, :] + got_ref[at, :].astype(jnp.float32)
        outs[n][...] = total
        outs[2 + n][...] = total.astype(sent)


def chip_sums(kept, got, sent):
    shape = (kept.shape[0] // 2, kept.shape[1])
    outs = pl.pallas_call(
        functools.partial(chip_kernel, sent),
        out_shape=[jax.ShapeDtypeStruct(shape, t) for t in (jnp.float32,) * 2 + (sent,) * 2],
        compiler_params=PARAMS,
        cost_estimate=cost(0, 1024),
        name="chip_sums",
    )(kept, got)
    return outs[:2], outs[2:]


def add_kernel(sent, *refs):
    for n in range(2):
        total = refs[n][...] + refs[2 + n][...].astype(jnp.float32)
        refs[4 + n][...] = total
        refs[6 + n][...] = total.astype(sent)


def add_parts(sums, crossed, sent):
    outs = pl.pallas_call(
        functools.partial(add_kernel, sent),
        out_shape=[jax.ShapeDtypeStruct(sums[0].shape, t) for t in (jnp.float32,) * 2 + (sent,) * 2],
        compiler_params=PARAMS,
        cost_estimate=cost(0, 1024),
        name="add_parts",
    )(*sums, *crossed)
    return outs[:2], outs[2:]


def join_kernel(*refs):
    rows = refs[0].shape[0]
    for n in range(2):
        total = refs[n][...] + refs[2 + n][...].astype(jnp.float32)
        refs[4][pl.ds(n * rows, rows), :] = total.astype(refs[4].dtype)


def join_parts(sums, crossed):
    rows, rank = sums[0].shape
    return pl.pallas_call(
        join_kernel,
        out_shape=jax.ShapeDtypeStruct((2 * rows, rank), jnp.bfloat16),
        compiler_params=PARAMS,
        cost_estimate=cost(0, 1024),
        name="join_parts",
    )(*sums, *crossed)


def chip_steps(parts):
    bits = (parts // 2).bit_length() - 1
    return [[(step + part * (bits // 2)) % bits for part in range(2)] for step in range(bits)]


def cross(parts, blocks, step):
    return [
        lax.ppermute(block, "tp", [(i, i ^ (2 << bit)) for i in range(parts)])
        for block, bit in zip(blocks, step)
    ]


def grad_kernel(order, resume, finish, seg_rows, flip, bounds_ref, halves_ref, *refs):
    lows, rows, refs = refs[: len(order)], refs[len(order) : 2 * len(order)], refs[2 * len(order) :]
    if resume:
        so_far, refs = refs[0], refs[1:]
    outs, acc = (refs[:-1], refs[-1]) if finish else ((), refs[0])
    acc[...] = so_far[...] if resume else jnp.zeros_like(acc)
    groups, places = acc.shape[0], rows[0].shape[0] // seg_rows
    for d in range(groups):
        for half, low, tokens in zip(order, lows, rows):
            first, last, steps = spans_of(bounds_ref, halves_ref[half], groups, d)

            def add_step(step, carry, d=d, first=first, last=last, low=low, tokens=tokens):
                at, mask = step_rows(first, last, step, seg_rows, places)
                own = jnp.where(mask, low[at, :].astype(jnp.float32), 0.0).astype(jnp.bfloat16)
                acc[d] += lax.dot_general(
                    own,
                    tokens[at, :],
                    (((0,), (0,)), ((), ())),
                    preferred_element_type=jnp.float32,
                )
                return carry

            lax.fori_loop(0, steps, add_step, 0)
        if finish:
            total = acc[d].astype(jnp.bfloat16)
            outs[d][...] = total.T if flip else total


def group_grads(tables, halves, order, lows, rows, groups, flip=False, so_far=None, finish=True):
    seg_count = tables[0].shape[0]
    count, features = rows[0].shape
    rank = lows[0].shape[1]
    shape = (features, rank) if flip else (rank, features)
    sums = pltpu.VMEM((groups, rank, features), jnp.float32)
    earlier = [] if so_far is None else [so_far]
    return pl.pallas_call(
        functools.partial(
            grad_kernel, order, bool(earlier), finish, 2 * count // seg_count, flip
        ),
        grid_spec=pltpu.PrefetchScalarGridSpec(
            num_scalar_prefetch=2,
            grid=(1,),
            in_specs=[HELD] * (2 * len(order) + len(earlier)),
            out_specs=[whole(shape)] * groups if finish else HELD,
            scratch_shapes=[sums] if finish else [],
        ),
        out_shape=[jax.ShapeDtypeStruct(shape, jnp.bfloat16)] * groups if finish else sums,
        compiler_params=PARAMS,
        cost_estimate=cost(0, 1024),
        name="group_grads",
    )(tables[1], halves, *lows, *rows, *earlier)


def total_kernel(groups, slots_ref, *rest):
    blocks, out_ref, acc = rest[:groups], rest[groups], rest[groups + 1]
    acc[...] = jnp.zeros_like(acc)
    for d in range(groups):
        acc[slots_ref[d]] += blocks[d][...].astype(jnp.float32)
    out_ref[...] = acc[...].astype(out_ref.dtype)


def slot_totals(slots, blocks, owned):
    groups = len(blocks)
    shape = blocks[0].shape
    return pl.pallas_call(
        functools.partial(total_kernel, groups),
        grid_spec=pltpu.PrefetchScalarGridSpec(
            num_scalar_prefetch=1,
            grid=(1,),
            in_specs=[HELD] * groups,
            out_specs=pl.BlockSpec((owned, *shape), lambda i, *_: (0, 0, 0)),
            scratch_shapes=[pltpu.VMEM((owned, *shape), jnp.float32)],
        ),
        out_shape=jax.ShapeDtypeStruct((owned, *shape), jnp.bfloat16),
        compiler_params=PARAMS,
        cost_estimate=cost(groups * blocks[0].size, 2 * (groups + owned) * blocks[0].size),
        name="slot_totals",
    )(slots, *blocks)


def early_kernel(late, slots_ref, *rest):
    blocks, (out_ref, partial_ref, acc) = rest[:-3], rest[-3:]
    acc[...] = jnp.zeros_like(acc)
    for d, block in blocks_but(late, blocks):
        acc[slots_ref[d]] += block[...].astype(jnp.float32)
    out_ref[...] = acc[...].astype(out_ref.dtype)
    partial_ref[...] = acc[slots_ref[late]]


def blocks_but(late, blocks):
    return [(d + (d >= late), block) for d, block in enumerate(blocks)]


def early_totals(slots, blocks, late, owned):
    shape = blocks[0].shape
    return pl.pallas_call(
        functools.partial(early_kernel, late),
        grid_spec=pltpu.PrefetchScalarGridSpec(
            num_scalar_prefetch=1,
            grid=(1,),
            in_specs=[HELD] * len(blocks),
            out_specs=[whole((owned, *shape)), HELD],
            scratch_shapes=[pltpu.VMEM((owned, *shape), jnp.float32)],
        ),
        out_shape=[
            jax.ShapeDtypeStruct((owned, *shape), jnp.bfloat16),
            pltpu.VMEM(shape, jnp.float32),
        ],
        compiler_params=PARAMS,
        cost_estimate=cost(0, 1024),
        name="early_totals",
    )(slots, *blocks)


def late_kernel(late, slots_ref, totals_ref, partial_ref, block_ref, out_ref, total, sem):
    total[...] = (partial_ref[...] + block_ref[...].astype(jnp.float32)).astype(total.dtype)
    copy = pltpu.make_async_copy(total, out_ref.at[slots_ref[late]], sem)
    copy.start()
    copy.wait()


def late_totals(slots, totals, partial, block, late):
    return pl.pallas_call(
        functools.partial(late_kernel, late),
        grid_spec=pltpu.PrefetchScalarGridSpec(
            num_scalar_prefetch=1,
            grid=(1,),
            in_specs=[ANY, HELD, HELD],
            out_specs=ANY,
            scratch_shapes=[pltpu.VMEM(block.shape, totals.dtype), pltpu.SemaphoreType.DMA],
        ),
        out_shape=jax.ShapeDtypeStruct(totals.shape, totals.dtype),
        input_output_aliases={1: 0},
        compiler_params=PARAMS,
        cost_estimate=cost(0, 1024),
        name="late_totals",
    )(slots, totals, partial, block)


def apart(valid, work, *args):
    out = jax.eval_shape(work, *args)
    zeros = lambda *_: jax.tree.map(lambda leaf: jnp.zeros(leaf.shape, leaf.dtype), out)
    return lax.cond(valid, work, zeros, *args)


def body(groups, parts, inputs, cotangent, factor_a, factor_b, adapter_slot, seg_adapter):
    owned = factor_a.shape[0]
    to, back = peers(groups)
    me = lax.axis_index("grp")
    matches = seg_adapter[:, :, None] == jnp.arange(adapter_slot.shape[0], dtype=jnp.int32)
    slot_all = jnp.sum(jnp.where(matches, adapter_slot, 0), axis=2)
    owner_all, local_all = slot_all // owned, slot_all % owned
    my_slots = jnp.max(jnp.where(owner_all == me, local_all, 0), axis=1)
    order = jnp.arange(groups, dtype=jnp.int32)
    slots = jnp.sum(
        jnp.where(to(me, order)[:, None] == order[None, :], my_slots[None, :], 0), axis=1
    )
    my_owners = lax.dynamic_index_in_dim(owner_all, me, 0, keepdims=False)
    rel = jnp.sum(
        jnp.where(my_owners[:, None] == back(me, order)[None, :], order[None, :], 0), axis=1
    )

    in_half = rel.reshape(2, -1)
    place = jnp.arange(in_half.shape[1], dtype=jnp.int32)
    before = (in_half[:, None, :] < in_half[:, :, None]) | (
        (in_half[:, None, :] == in_half[:, :, None]) & (place[None, :] < place[:, None])
    )
    bounds = in_half[:, None, :] < jnp.arange(groups + 1, dtype=jnp.int32)[:, None]
    tables = [jnp.sum(table, axis=2, dtype=jnp.int32).reshape(-1) for table in (before, bounds)]

    valid = me >= 0

    def send(block, d, where):
        return lax.ppermute(block, "grp", [(i, where(i, d)) for i in range(groups)])

    def send_all(blocks, where):
        return [send(block, d, where) for d, block in enumerate(blocks, 1)]

    core = lax.axis_index("tp") % 2
    halves = jnp.stack([1 - core, core])
    steps = chip_steps(parts)
    sent = jnp.bfloat16 if len(steps) <= 2 else jnp.float32
    own_factor_b, *picked_b = pick_factors(slots, factor_b, groups)
    got_b = send_all(picked_b, to)
    own_factor_a, *picked_a = pick_factors(slots, factor_a, groups)
    near_a = send(picked_a[-1], groups - 1, to)
    picked_a, got_b = lax.optimization_barrier((picked_a[:-1], got_b))
    far_a = send_all(picked_a, to)

    def first_grad_sums(tables, halves, cotangent, *blocks):
        give, held, rows = give_rows(tables, halves, cotangent, blocks, True)
        got = from_other_core(parts, give)
        sums, out = chip_sums(keep_rows(tables, halves, rows, held, True), got, sent)
        for step in steps[:-1]:
            sums, out = add_parts(sums, cross(parts, out, step), sent)
        return sums, out

    sums, out = apart(valid, first_grad_sums, tables, halves, cotangent, own_factor_b, *got_b)
    later_halves, out = lax.optimization_barrier((halves, out))
    tok = hold(tables, later_halves, inputs)
    crossed = cross(parts, out, steps[-1])
    tok, far_a, near_a = lax.optimization_barrier((tok, far_a, near_a))
    give, held = give_held_rows(tables, halves, tok[0], [own_factor_a, *far_a, near_a], False)
    crossed, give = lax.optimization_barrier((crossed, give))
    got = from_other_core(parts, give)
    low = join_parts(sums, crossed)
    other_low = from_other_core(parts, low)
    kept = keep_rows(tables, halves, tok[1], held, False)
    low, other_low, kept = lax.optimization_barrier((low, other_low, kept))
    own_a, *grads_a = group_grads(
        tables, halves, (1, 0), [low, other_low], tok[::-1], groups, True
    )
    back_a = send_all(grads_a[:-1], back)
    kept, own_a = lax.optimization_barrier((kept, own_a))

    def input_grads(tables, halves, cotangent, kept, got, near):
        sums, out = chip_sums(kept, got, sent)
        crossed = cross(parts, out, steps[0])
        crossed, rows = lax.optimization_barrier((crossed, hold(tables, halves, cotangent)))
        for step in steps[1:]:
            sums, out = add_parts(sums, crossed, sent)
            crossed = cross(parts, out, step)
        low = join_parts(sums, crossed)
        other_low = from_other_core(parts, low)
        first = group_grads(tables, halves, (1,), [low], rows[1:], groups, finish=False)
        grads = group_grads(tables, halves, (0,), [other_low], rows[:1], groups, so_far=first)
        return grads, send(near, groups - 1, back)

    (own_b, *grads_b), near_back = apart(
        valid, input_grads, tables, halves, cotangent, kept, got, grads_a[-1]
    )
    grads_b, back_a = lax.optimization_barrier((grads_b, back_a))
    back_b = send_all(grads_b, back)
    back_a = [*back_a, near_back]
    grad_a = slot_totals(slots, [own_a, *back_a], owned)
    late = min(2, groups - 1)
    early = [own_b, *back_b[: late - 1], *back_b[late:]]
    totals, partial = early_totals(slots, early, late, owned)
    grad_b = late_totals(slots, totals, partial, back_b[late - 1], late)
    return grad_a, grad_b


def solution(mesh):
    return jax.shard_map(
        functools.partial(body, mesh.shape["grp"], mesh.shape["tp"]),
        mesh=mesh,
        in_specs=(
            P("grp", "tp"),
            P("grp", "tp"),
            P("grp", "tp", None),
            P("grp", None, "tp"),
            P(),
            P(),
        ),
        out_specs=(P("grp", "tp", None), P("grp", None, "tp")),
        check_vma=False,
    )
```

```python
import functools

import jax
import jax.numpy as jnp
from jax import lax
from jax.experimental import pallas as pl
from jax.experimental.pallas import tpu as pltpu
from jax.sharding import PartitionSpec as P

VMEM_LIMIT = 24 * 1024 * 1024
ANY = pl.BlockSpec(memory_space=pl.ANY)
HELD = pl.BlockSpec(memory_space=pltpu.VMEM)
PARAMS = pltpu.CompilerParams(vmem_limit_bytes=VMEM_LIMIT)


def cost(flops, moved):
    return pl.CostEstimate(flops=flops, bytes_accessed=moved, transcendentals=0)


def peers(groups):
    if groups & (groups - 1) == 0:
        across = lambda i, d: i ^ ((groups - d) % groups)
        return across, across
    return (lambda i, d: (i + d) % groups), (lambda i, d: (i + groups - d) % groups)


def step_segments(seg_count, most):
    return max(n for n in range(1, most + 1) if seg_count % n == 0)


def whole(shape):
    return pl.BlockSpec(shape, lambda i, *_: (0,) * len(shape))


def pick_kernel(groups, slots_ref, *rest):
    for source, out in zip(rest[:groups], rest[groups:]):
        out[...] = source[0]


def pick_factors(slots, factor, groups):
    block = factor.shape[1:]
    return pl.pallas_call(
        functools.partial(pick_kernel, groups),
        grid_spec=pltpu.PrefetchScalarGridSpec(
            num_scalar_prefetch=1,
            grid=(1,),
            in_specs=[
                pl.BlockSpec((1, *block), lambda i, slots, d=d: (slots[d], 0, 0))
                for d in range(groups)
            ],
            out_specs=[whole(block)] * groups,
        ),
        out_shape=[jax.ShapeDtypeStruct(block, factor.dtype)] * groups,
        compiler_params=PARAMS,
        cost_estimate=cost(0, 4 * groups * block[0] * block[1]),
        name="pick_factors",
    )(slots, *[pltpu.with_memory_space_constraint(factor, pltpu.HBM)] * groups)


def times_factors(seg_rows, flip, base, spans, rel_ref, rows, held, out_ref):
    contract = (((1,), (1 if flip else 0,)), ((), ()))
    for arrived, segs in spans:
        arrived()
        for n in segs:
            at = pl.ds(n * seg_rows, seg_rows)
            out_ref[at, :] = lax.dot_general(
                rows[at, :], held[rel_ref[base + n]], contract, preferred_element_type=jnp.float32
            ).astype(out_ref.dtype)


def give_kernel(seg_rows, pieces, flip, rel_ref, halves_ref, rows_ref, *rest):
    groups = len(rest) - 5
    blocks, (out_ref, held, second, first, sems) = rest[:groups], rest[groups:]
    count = first.shape[0]
    piece = count // pieces
    fetches = [pltpu.make_async_copy(blocks[d], held.at[d], sems.at[d]) for d in range(groups)]
    arrivals = [
        pltpu.make_async_copy(
            rows_ref.at[pl.ds(pl.multiple_of(halves_ref[h] * count + k * piece, seg_rows), piece)],
            half.at[pl.ds(k * piece, piece)],
            sems.at[groups + h * pieces + k],
        )
        for h, half in enumerate((first, second))
        for k in range(pieces)
    ]
    for copy in fetches + arrivals:
        copy.start()
    for copy in fetches:
        copy.wait()
    segs = piece // seg_rows
    spans = [(arrivals[k].wait, range(k * segs, (k + 1) * segs)) for k in range(pieces)]
    base = halves_ref[0] * segs * pieces
    times_factors(seg_rows, flip, base, spans, rel_ref, first, held, out_ref)
    for copy in arrivals[pieces:]:
        copy.wait()


def give_rows(rel, halves, rows, blocks, flip):
    groups = len(blocks)
    seg_count = rel.shape[0]
    seg_rows = rows.shape[0] // seg_count
    pieces = seg_count // 2 // step_segments(seg_count // 2, 3)
    half = pltpu.VMEM((rows.shape[0] // 2, rows.shape[1]), rows.dtype)
    shape = (rows.shape[0] // 2, blocks[0].shape[0 if flip else 1])
    return pl.pallas_call(
        functools.partial(give_kernel, seg_rows, pieces, flip),
        grid_spec=pltpu.PrefetchScalarGridSpec(
            num_scalar_prefetch=2,
            grid=(1,),
            in_specs=[ANY] * (groups + 1),
            out_specs=[whole(shape), HELD, HELD],
            scratch_shapes=[half, pltpu.SemaphoreType.DMA((groups + 2 * pieces,))],
        ),
        out_shape=[
            jax.ShapeDtypeStruct(shape, jnp.bfloat16),
            pltpu.VMEM((groups, *blocks[0].shape), rows.dtype),
            half,
        ],
        compiler_params=PARAMS,
        cost_estimate=cost(rows.size * shape[1], 2 * rows.size),
        name="give_rows",
    )(rel, halves, pltpu.with_memory_space_constraint(rows, pltpu.HBM), *blocks)


def give_held_kernel(seg_rows, flip, rel_ref, halves_ref, rows, *rest):
    blocks, (out_ref, held, sems) = rest[:-3], rest[-3:]
    fetches = [pltpu.make_async_copy(block, held.at[d], sems.at[d]) for d, block in enumerate(blocks)]
    for copy in fetches:
        copy.start()
    for copy in fetches:
        copy.wait()
    segs = rows.shape[0] // seg_rows
    spans = [(lambda: None, range(segs))]
    times_factors(seg_rows, flip, halves_ref[0] * segs, spans, rel_ref, rows, held, out_ref)


def give_held_rows(rel, halves, rows, blocks, flip):
    groups = len(blocks)
    shape = (rows.shape[0], blocks[0].shape[0 if flip else 1])
    return pl.pallas_call(
        functools.partial(give_held_kernel, 2 * rows.shape[0] // rel.shape[0], flip),
        grid_spec=pltpu.PrefetchScalarGridSpec(
            num_scalar_prefetch=2,
            grid=(1,),
            in_specs=[HELD] + [ANY] * groups,
            out_specs=[whole(shape), HELD],
            scratch_shapes=[pltpu.SemaphoreType.DMA((groups,))],
        ),
        out_shape=[
            jax.ShapeDtypeStruct(shape, jnp.bfloat16),
            pltpu.VMEM((groups, *blocks[0].shape), rows.dtype),
        ],
        compiler_params=PARAMS,
        cost_estimate=cost(2 * rows.size * shape[1], 2 * rows.size),
        name="give_held_rows",
    )(rel, halves, rows, *blocks)


def keep_kernel(seg_rows, flip, rel_ref, halves_ref, rows, held, out_ref):
    segs = rows.shape[0] // seg_rows
    spans = [(lambda: None, range(segs))]
    times_factors(seg_rows, flip, halves_ref[1] * segs, spans, rel_ref, rows, held, out_ref)


def keep_rows(rel, halves, rows, held, flip):
    count, rank = rows.shape[0], held.shape[1 if flip else 2]
    return pl.pallas_call(
        functools.partial(keep_kernel, 2 * count // rel.shape[0], flip),
        grid_spec=pltpu.PrefetchScalarGridSpec(
            num_scalar_prefetch=2,
            grid=(1,),
            in_specs=[HELD, HELD],
            out_specs=whole((count, rank)),
        ),
        out_shape=jax.ShapeDtypeStruct((count, rank), jnp.float32),
        compiler_params=PARAMS,
        cost_estimate=cost(2 * rows.size * rank, 2 * rows.size),
        name="keep_rows",
    )(rel, halves, rows, held)


def hold_kernel(halves_ref, rows_ref, *rest):
    outs, sems = rest[:-1], rest[-1]
    count = outs[0].shape[0]
    copies = [
        pltpu.make_async_copy(
            rows_ref.at[pl.ds(pl.multiple_of(halves_ref[k] * count, 16), count)], out, sems.at[k]
        )
        for k, out in enumerate(outs)
    ]
    for copy in copies:
        copy.start()
    for copy in copies:
        copy.wait()


def hold(halves, rows):
    shape = (rows.shape[0] // 2, rows.shape[1])
    return pl.pallas_call(
        hold_kernel,
        grid_spec=pltpu.PrefetchScalarGridSpec(
            num_scalar_prefetch=1,
            grid=(1,),
            in_specs=[ANY],
            out_specs=[HELD] * 2,
            scratch_shapes=[pltpu.SemaphoreType.DMA((2,))],
        ),
        out_shape=[pltpu.VMEM(shape, rows.dtype)] * 2,
        compiler_params=PARAMS,
        cost_estimate=cost(0, 4 * rows.size),
        name="hold_rows",
    )(halves, pltpu.with_memory_space_constraint(rows, pltpu.HBM))


def from_other_core(parts, block):
    return lax.ppermute(block, "tp", [(i, i ^ 1) for i in range(parts)])


def chip_kernel(sent, kept_ref, got_ref, *outs):
    start = 0
    for n in range(2):
        at = pl.ds(start, outs[n].shape[0])
        start += outs[n].shape[0]
        total = kept_ref[at, :] + got_ref[at, :].astype(jnp.float32)
        outs[n][...] = total
        outs[2 + n][...] = total.astype(sent)


def chip_sums(kept, got, sent):
    shape = (kept.shape[0] // 2, kept.shape[1])
    outs = pl.pallas_call(
        functools.partial(chip_kernel, sent),
        out_shape=[jax.ShapeDtypeStruct(shape, t) for t in (jnp.float32,) * 2 + (sent,) * 2],
        compiler_params=PARAMS,
        cost_estimate=cost(0, 1024),
        name="chip_sums",
    )(kept, got)
    return outs[:2], outs[2:]


def add_kernel(sent, *refs):
    for n in range(2):
        total = refs[n][...] + refs[2 + n][...].astype(jnp.float32)
        refs[4 + n][...] = total
        refs[6 + n][...] = total.astype(sent)


def add_parts(sums, crossed, sent):
    outs = pl.pallas_call(
        functools.partial(add_kernel, sent),
        out_shape=[jax.ShapeDtypeStruct(sums[0].shape, t) for t in (jnp.float32,) * 2 + (sent,) * 2],
        compiler_params=PARAMS,
        cost_estimate=cost(0, 1024),
        name="add_parts",
    )(*sums, *crossed)
    return outs[:2], outs[2:]


def join_kernel(*refs):
    rows = refs[0].shape[0]
    for n in range(2):
        total = refs[n][...] + refs[2 + n][...].astype(jnp.float32)
        refs[4][pl.ds(n * rows, rows), :] = total.astype(refs[4].dtype)


def join_parts(sums, crossed):
    rows, rank = sums[0].shape
    return pl.pallas_call(
        join_kernel,
        out_shape=jax.ShapeDtypeStruct((2 * rows, rank), jnp.bfloat16),
        compiler_params=PARAMS,
        cost_estimate=cost(0, 1024),
        name="join_parts",
    )(*sums, *crossed)


def chip_steps(parts):
    bits = (parts // 2).bit_length() - 1
    return [[(step + part * (bits // 2)) % bits for part in range(2)] for step in range(bits)]


def cross(parts, blocks, step):
    return [
        lax.ppermute(block, "tp", [(i, i ^ (2 << bit)) for i in range(parts)])
        for block, bit in zip(blocks, step)
    ]


def grad_kernel(order, resume, finish, seg_rows, flip, rel_ref, halves_ref, *refs):
    lows, rows, refs = refs[: len(order)], refs[len(order) : 2 * len(order)], refs[2 * len(order) :]
    if resume:
        so_far, refs = refs[0], refs[1:]
    outs, acc = (refs[:-1], refs[-1]) if finish else ((), refs[0])
    acc[...] = so_far[...] if resume else jnp.zeros_like(acc)
    segs = rows[0].shape[0] // seg_rows
    unroll = step_segments(segs, 15)
    for half, low, tokens in zip(order, lows, rows):

        def add_segments(step, carry, half=half, low=low, tokens=tokens):
            for n in range(unroll):
                seg = step * unroll + n
                at = pl.ds(pl.multiple_of(seg * seg_rows, seg_rows), seg_rows)
                acc[rel_ref[halves_ref[half] * segs + seg]] += lax.dot_general(
                    low[at, :],
                    tokens[at, :],
                    (((0,), (0,)), ((), ())),
                    preferred_element_type=jnp.float32,
                )
            return carry

        lax.fori_loop(0, segs // unroll, add_segments, 0)
    for d, out in enumerate(outs):
        total = acc[d].astype(jnp.bfloat16)
        out[...] = total.T if flip else total


def group_grads(rel, halves, order, lows, rows, groups, flip=False, so_far=None, finish=True):
    seg_count = rel.shape[0]
    count, features = rows[0].shape
    rank = lows[0].shape[1]
    shape = (features, rank) if flip else (rank, features)
    sums = pltpu.VMEM((groups, rank, features), jnp.float32)
    earlier = [] if so_far is None else [so_far]
    return pl.pallas_call(
        functools.partial(
            grad_kernel, order, bool(earlier), finish, 2 * count // seg_count, flip
        ),
        grid_spec=pltpu.PrefetchScalarGridSpec(
            num_scalar_prefetch=2,
            grid=(1,),
            in_specs=[HELD] * (2 * len(order) + len(earlier)),
            out_specs=[whole(shape)] * groups if finish else HELD,
            scratch_shapes=[sums] if finish else [],
        ),
        out_shape=[jax.ShapeDtypeStruct(shape, jnp.bfloat16)] * groups if finish else sums,
        compiler_params=PARAMS,
        cost_estimate=cost(0, 1024),
        name="group_grads",
    )(rel, halves, *lows, *rows, *earlier)


def total_kernel(groups, slots_ref, *rest):
    blocks, out_ref, acc = rest[:groups], rest[groups], rest[groups + 1]
    acc[...] = jnp.zeros_like(acc)
    for d in range(groups):
        acc[slots_ref[d]] += blocks[d][...].astype(jnp.float32)
    out_ref[...] = acc[...].astype(out_ref.dtype)


def slot_totals(slots, blocks, owned):
    groups = len(blocks)
    shape = blocks[0].shape
    return pl.pallas_call(
        functools.partial(total_kernel, groups),
        grid_spec=pltpu.PrefetchScalarGridSpec(
            num_scalar_prefetch=1,
            grid=(1,),
            in_specs=[HELD] * groups,
            out_specs=pl.BlockSpec((owned, *shape), lambda i, *_: (0, 0, 0)),
            scratch_shapes=[pltpu.VMEM((owned, *shape), jnp.float32)],
        ),
        out_shape=jax.ShapeDtypeStruct((owned, *shape), jnp.bfloat16),
        compiler_params=PARAMS,
        cost_estimate=cost(groups * blocks[0].size, 2 * (groups + owned) * blocks[0].size),
        name="slot_totals",
    )(slots, *blocks)


def early_kernel(late, slots_ref, *rest):
    blocks, (out_ref, partial_ref, acc) = rest[:-3], rest[-3:]
    acc[...] = jnp.zeros_like(acc)
    for d, block in blocks_but(late, blocks):
        acc[slots_ref[d]] += block[...].astype(jnp.float32)
    out_ref[...] = acc[...].astype(out_ref.dtype)
    partial_ref[...] = acc[slots_ref[late]]


def blocks_but(late, blocks):
    return [(d + (d >= late), block) for d, block in enumerate(blocks)]


def early_totals(slots, blocks, late, owned):
    shape = blocks[0].shape
    return pl.pallas_call(
        functools.partial(early_kernel, late),
        grid_spec=pltpu.PrefetchScalarGridSpec(
            num_scalar_prefetch=1,
            grid=(1,),
            in_specs=[HELD] * len(blocks),
            out_specs=[whole((owned, *shape)), HELD],
            scratch_shapes=[pltpu.VMEM((owned, *shape), jnp.float32)],
        ),
        out_shape=[
            jax.ShapeDtypeStruct((owned, *shape), jnp.bfloat16),
            pltpu.VMEM(shape, jnp.float32),
        ],
        compiler_params=PARAMS,
        cost_estimate=cost(0, 1024),
        name="early_totals",
    )(slots, *blocks)


def late_kernel(late, slots_ref, totals_ref, partial_ref, block_ref, out_ref, total, sem):
    total[...] = (partial_ref[...] + block_ref[...].astype(jnp.float32)).astype(total.dtype)
    copy = pltpu.make_async_copy(total, out_ref.at[slots_ref[late]], sem)
    copy.start()
    copy.wait()


def late_totals(slots, totals, partial, block, late):
    return pl.pallas_call(
        functools.partial(late_kernel, late),
        grid_spec=pltpu.PrefetchScalarGridSpec(
            num_scalar_prefetch=1,
            grid=(1,),
            in_specs=[ANY, HELD, HELD],
            out_specs=ANY,
            scratch_shapes=[pltpu.VMEM(block.shape, totals.dtype), pltpu.SemaphoreType.DMA],
        ),
        out_shape=jax.ShapeDtypeStruct(totals.shape, totals.dtype),
        input_output_aliases={1: 0},
        compiler_params=PARAMS,
        cost_estimate=cost(0, 1024),
        name="late_totals",
    )(slots, totals, partial, block)


def apart(valid, work, *args):
    out = jax.eval_shape(work, *args)
    zeros = lambda *_: jax.tree.map(lambda leaf: jnp.zeros(leaf.shape, leaf.dtype), out)
    return lax.cond(valid, work, zeros, *args)


def body(groups, parts, inputs, cotangent, factor_a, factor_b, adapter_slot, seg_adapter):
    owned = factor_a.shape[0]
    to, back = peers(groups)
    me = lax.axis_index("grp")
    matches = seg_adapter[:, :, None] == jnp.arange(adapter_slot.shape[0], dtype=jnp.int32)
    slot_all = jnp.sum(jnp.where(matches, adapter_slot, 0), axis=2)
    owner_all, local_all = slot_all // owned, slot_all % owned
    my_slots = jnp.max(jnp.where(owner_all == me, local_all, 0), axis=1)
    order = jnp.arange(groups, dtype=jnp.int32)
    slots = jnp.sum(
        jnp.where(to(me, order)[:, None] == order[None, :], my_slots[None, :], 0), axis=1
    )
    my_owners = lax.dynamic_index_in_dim(owner_all, me, 0, keepdims=False)
    rel = jnp.sum(
        jnp.where(my_owners[:, None] == back(me, order)[None, :], order[None, :], 0), axis=1
    )

    valid = me >= 0

    def send(block, d, where):
        return lax.ppermute(block, "grp", [(i, where(i, d)) for i in range(groups)])

    def send_all(blocks, where):
        return [send(block, d, where) for d, block in enumerate(blocks, 1)]

    core = lax.axis_index("tp") % 2
    halves = jnp.stack([1 - core, core])
    steps = chip_steps(parts)
    sent = jnp.bfloat16 if len(steps) <= 2 else jnp.float32
    own_factor_b, *picked_b = pick_factors(slots, factor_b, groups)
    got_b = send_all(picked_b, to)
    own_factor_a, *picked_a = pick_factors(slots, factor_a, groups)
    near_a = send(picked_a[-1], groups - 1, to)
    picked_a, got_b = lax.optimization_barrier((picked_a[:-1], got_b))
    far_a = send_all(picked_a, to)

    def first_grad_sums(rel, halves, cotangent, inputs, *blocks):
        give, held, rows = give_rows(rel, halves, cotangent, blocks, True)
        got = from_other_core(parts, give)
        sums, out = chip_sums(keep_rows(rel, halves, rows, held, True), got, sent)
        tok = None
        for step in steps[:-1]:
            crossed = cross(parts, out, step)
            if tok is None:
                crossed, tok = lax.optimization_barrier((crossed, hold(halves, inputs)))
            sums, out = add_parts(sums, crossed, sent)
        return sums, out, tok

    sums, out, tok = apart(
        valid, first_grad_sums, rel, halves, cotangent, inputs, own_factor_b, *got_b
    )
    crossed = cross(parts, out, steps[-1])
    give, held = give_held_rows(rel, halves, tok[0], [own_factor_a, *far_a, near_a], False)
    got = from_other_core(parts, give)
    kept = keep_rows(rel, halves, tok[1], held, False)
    crossed, kept = lax.optimization_barrier((crossed, kept))
    low = join_parts(sums, crossed)
    other_low = from_other_core(parts, low)
    first = group_grads(rel, halves, (1,), [low], tok[1:], groups, finish=False)
    own_a, *grads_a = group_grads(
        rel, halves, (0,), [other_low], tok[:1], groups, True, so_far=first
    )
    back_a = send_all(grads_a, back)
    kept, own_a = lax.optimization_barrier((kept, own_a))

    def input_grads(rel, halves, cotangent, kept, got):
        sums, out = chip_sums(kept, got, sent)
        crossed = cross(parts, out, steps[0])
        crossed, rows = lax.optimization_barrier((crossed, hold(halves, cotangent)))
        for step in steps[1:]:
            sums, out = add_parts(sums, crossed, sent)
            crossed = cross(parts, out, step)
        low = join_parts(sums, crossed)
        other_low = from_other_core(parts, low)
        first = group_grads(rel, halves, (1,), [low], rows[1:], groups, finish=False)
        return group_grads(rel, halves, (0,), [other_low], rows[:1], groups, so_far=first)

    own_b, *grads_b = apart(valid, input_grads, rel, halves, cotangent, kept, got)
    grads_b, back_a = lax.optimization_barrier((grads_b, back_a))
    back_b = send_all(grads_b, back)
    grad_a = slot_totals(slots, [own_a, *back_a], owned)
    late = min(2, groups - 1)
    early = [own_b, *back_b[: late - 1], *back_b[late:]]
    totals, partial = early_totals(slots, early, late, owned)
    grad_b = late_totals(slots, totals, partial, back_b[late - 1], late)
    return grad_a, grad_b


def solution(mesh):
    return jax.shard_map(
        functools.partial(body, mesh.shape["grp"], mesh.shape["tp"]),
        mesh=mesh,
        in_specs=(
            P("grp", "tp"),
            P("grp", "tp"),
            P("grp", "tp", None),
            P("grp", None, "tp"),
            P(),
            P(),
        ),
        out_specs=(P("grp", "tp", None), P("grp", None, "tp")),
        check_vma=False,
    )
```

```python
import functools

import jax
import jax.numpy as jnp
from jax import lax
from jax.experimental import pallas as pl
from jax.experimental.pallas import tpu as pltpu
from jax.sharding import PartitionSpec as P

VMEM_LIMIT = 24 * 1024 * 1024
ANY = pl.BlockSpec(memory_space=pl.ANY)
HELD = pl.BlockSpec(memory_space=pltpu.VMEM)
PARAMS = pltpu.CompilerParams(vmem_limit_bytes=VMEM_LIMIT)


def cost(flops, moved):
    return pl.CostEstimate(flops=flops, bytes_accessed=moved, transcendentals=0)


def peers(groups):
    if groups & (groups - 1) == 0:
        across = lambda i, d: i ^ ((groups - d) % groups)
        return across, across
    return (lambda i, d: (i + d) % groups), (lambda i, d: (i + groups - d) % groups)


def step_segments(seg_count, most):
    return max(n for n in range(1, most + 1) if seg_count % n == 0)


def whole(shape):
    return pl.BlockSpec(shape, lambda i, *_: (0,) * len(shape))


def pick_kernel(groups, slots_ref, *rest):
    for source, out in zip(rest[:groups], rest[groups:]):
        out[...] = source[0]


def pick_factors(slots, factor, groups):
    block = factor.shape[1:]
    return pl.pallas_call(
        functools.partial(pick_kernel, groups),
        grid_spec=pltpu.PrefetchScalarGridSpec(
            num_scalar_prefetch=1,
            grid=(1,),
            in_specs=[
                pl.BlockSpec((1, *block), lambda i, slots, d=d: (slots[d], 0, 0))
                for d in range(groups)
            ],
            out_specs=[whole(block)] * groups,
        ),
        out_shape=[jax.ShapeDtypeStruct(block, factor.dtype)] * groups,
        compiler_params=PARAMS,
        cost_estimate=cost(0, 4 * groups * block[0] * block[1]),
        name="pick_factors",
    )(slots, *[pltpu.with_memory_space_constraint(factor, pltpu.HBM)] * groups)


def times_factors(seg_rows, flip, base, spans, rel_ref, rows, held, out_ref):
    contract = (((1,), (1 if flip else 0,)), ((), ()))
    for arrived, segs in spans:
        arrived()
        for n in segs:
            at = pl.ds(n * seg_rows, seg_rows)
            out_ref[at, :] = lax.dot_general(
                rows[at, :], held[rel_ref[base + n]], contract, preferred_element_type=jnp.float32
            ).astype(out_ref.dtype)


def give_kernel(seg_rows, flip, rel_ref, halves_ref, rows, *rest):
    blocks, (out_ref, held, sems) = rest[:-3], rest[-3:]
    fetches = [pltpu.make_async_copy(block, held.at[d], sems.at[d]) for d, block in enumerate(blocks)]
    for copy in fetches:
        copy.start()
    for copy in fetches:
        copy.wait()
    segs = rows.shape[0] // seg_rows
    spans = [(lambda: None, range(segs))]
    times_factors(seg_rows, flip, halves_ref[0] * segs, spans, rel_ref, rows, held, out_ref)


def give_rows(rel, halves, rows, blocks, flip):
    groups = len(blocks)
    shape = (rows.shape[0], blocks[0].shape[0 if flip else 1])
    return pl.pallas_call(
        functools.partial(give_kernel, 2 * rows.shape[0] // rel.shape[0], flip),
        grid_spec=pltpu.PrefetchScalarGridSpec(
            num_scalar_prefetch=2,
            grid=(1,),
            in_specs=[HELD] + [ANY] * groups,
            out_specs=[whole(shape), HELD],
            scratch_shapes=[pltpu.SemaphoreType.DMA((groups,))],
        ),
        out_shape=[
            jax.ShapeDtypeStruct(shape, jnp.bfloat16),
            pltpu.VMEM((groups, *blocks[0].shape), rows.dtype),
        ],
        compiler_params=PARAMS,
        cost_estimate=cost(2 * rows.size * shape[1], 2 * rows.size),
        name="give_rows",
    )(rel, halves, rows, *blocks)


def keep_kernel(seg_rows, flip, rel_ref, halves_ref, rows, held, out_ref):
    segs = rows.shape[0] // seg_rows
    spans = [(lambda: None, range(segs))]
    times_factors(seg_rows, flip, halves_ref[1] * segs, spans, rel_ref, rows, held, out_ref)


def keep_rows(rel, halves, rows, held, flip):
    count, rank = rows.shape[0], held.shape[1 if flip else 2]
    return pl.pallas_call(
        functools.partial(keep_kernel, 2 * count // rel.shape[0], flip),
        grid_spec=pltpu.PrefetchScalarGridSpec(
            num_scalar_prefetch=2,
            grid=(1,),
            in_specs=[HELD, HELD],
            out_specs=whole((count, rank)),
        ),
        out_shape=jax.ShapeDtypeStruct((count, rank), jnp.float32),
        compiler_params=PARAMS,
        cost_estimate=cost(2 * rows.size * rank, 2 * rows.size),
        name="keep_rows",
    )(rel, halves, rows, held)


def hold_kernel(halves_ref, rows_ref, *rest):
    outs, sems = rest[:-1], rest[-1]
    count = outs[0].shape[0]
    copies = [
        pltpu.make_async_copy(
            rows_ref.at[pl.ds(pl.multiple_of(halves_ref[k] * count, 16), count)], out, sems.at[k]
        )
        for k, out in enumerate(outs)
    ]
    for copy in copies:
        copy.start()
    for copy in copies:
        copy.wait()


def hold(halves, rows):
    shape = (rows.shape[0] // 2, rows.shape[1])
    return pl.pallas_call(
        hold_kernel,
        grid_spec=pltpu.PrefetchScalarGridSpec(
            num_scalar_prefetch=1,
            grid=(1,),
            in_specs=[ANY],
            out_specs=[HELD] * 2,
            scratch_shapes=[pltpu.SemaphoreType.DMA((2,))],
        ),
        out_shape=[pltpu.VMEM(shape, rows.dtype)] * 2,
        compiler_params=PARAMS,
        cost_estimate=cost(0, 4 * rows.size),
        name="hold_rows",
    )(halves, pltpu.with_memory_space_constraint(rows, pltpu.HBM))


def from_other_core(parts, block):
    return lax.ppermute(block, "tp", [(i, i ^ 1) for i in range(parts)])


def chip_kernel(sent, kept_ref, got_ref, *outs):
    start = 0
    for n in range(2):
        at = pl.ds(start, outs[n].shape[0])
        start += outs[n].shape[0]
        total = kept_ref[at, :] + got_ref[at, :].astype(jnp.float32)
        outs[n][...] = total
        outs[2 + n][...] = total.astype(sent)


def chip_sums(kept, got, sent):
    shape = (kept.shape[0] // 2, kept.shape[1])
    outs = pl.pallas_call(
        functools.partial(chip_kernel, sent),
        out_specs=[HELD] * 4,
        out_shape=[pltpu.VMEM(shape, t) for t in (jnp.float32,) * 2 + (sent,) * 2],
        compiler_params=PARAMS,
        cost_estimate=cost(0, 1024),
        name="chip_sums",
    )(kept, got)
    return outs[:2], outs[2:]


def add_kernel(sent, *refs):
    for n in range(2):
        total = refs[n][...] + refs[2 + n][...].astype(jnp.float32)
        refs[4 + n][...] = total
        refs[6 + n][...] = total.astype(sent)


def add_parts(sums, crossed, sent):
    outs = pl.pallas_call(
        functools.partial(add_kernel, sent),
        out_specs=[HELD] * 4,
        out_shape=[pltpu.VMEM(sums[0].shape, t) for t in (jnp.float32,) * 2 + (sent,) * 2],
        compiler_params=PARAMS,
        cost_estimate=cost(0, 1024),
        name="add_parts",
    )(*sums, *crossed)
    return outs[:2], outs[2:]


def join_kernel(*refs):
    rows = refs[0].shape[0]
    for n in range(2):
        total = refs[n][...] + refs[2 + n][...].astype(jnp.float32)
        refs[4][pl.ds(n * rows, rows), :] = total.astype(refs[4].dtype)


def join_parts(sums, crossed):
    rows, rank = sums[0].shape
    return pl.pallas_call(
        join_kernel,
        out_shape=jax.ShapeDtypeStruct((2 * rows, rank), jnp.bfloat16),
        compiler_params=PARAMS,
        cost_estimate=cost(0, 1024),
        name="join_parts",
    )(*sums, *crossed)


def chip_steps(parts):
    bits = (parts // 2).bit_length() - 1
    return [[(step + part * (bits // 2)) % bits for part in range(2)] for step in range(bits)]


def cross(parts, blocks, step):
    return [
        lax.ppermute(block, "tp", [(i, i ^ (2 << bit)) for i in range(parts)])
        for block, bit in zip(blocks, step)
    ]


def grad_kernel(order, resume, finish, seg_rows, flip, rel_ref, halves_ref, *refs):
    lows, rows, refs = refs[: len(order)], refs[len(order) : 2 * len(order)], refs[2 * len(order) :]
    if resume:
        so_far, refs = refs[0], refs[1:]
    outs, acc = (refs[:-1], refs[-1]) if finish else ((), refs[0])
    acc[...] = so_far[...] if resume else jnp.zeros_like(acc)
    segs = rows[0].shape[0] // seg_rows
    unroll = step_segments(segs, 15)
    for half, low, tokens in zip(order, lows, rows):

        def add_segments(step, carry, half=half, low=low, tokens=tokens):
            for n in range(unroll):
                seg = step * unroll + n
                at = pl.ds(pl.multiple_of(seg * seg_rows, seg_rows), seg_rows)
                acc[rel_ref[halves_ref[half] * segs + seg]] += lax.dot_general(
                    low[at, :],
                    tokens[at, :],
                    (((0,), (0,)), ((), ())),
                    preferred_element_type=jnp.float32,
                )
            return carry

        lax.fori_loop(0, segs // unroll, add_segments, 0)
    for d, out in enumerate(outs):
        total = acc[d].astype(jnp.bfloat16)
        out[...] = total.T if flip else total


def group_grads(rel, halves, order, lows, rows, groups, flip=False, so_far=None, finish=True):
    seg_count = rel.shape[0]
    count, features = rows[0].shape
    rank = lows[0].shape[1]
    shape = (features, rank) if flip else (rank, features)
    sums = pltpu.VMEM((groups, rank, features), jnp.float32)
    earlier = [] if so_far is None else [so_far]
    return pl.pallas_call(
        functools.partial(
            grad_kernel, order, bool(earlier), finish, 2 * count // seg_count, flip
        ),
        grid_spec=pltpu.PrefetchScalarGridSpec(
            num_scalar_prefetch=2,
            grid=(1,),
            in_specs=[HELD] * (2 * len(order) + len(earlier)),
            out_specs=[HELD] * groups if finish else HELD,
            scratch_shapes=[sums] if finish else [],
        ),
        out_shape=[pltpu.VMEM(shape, jnp.bfloat16)] * groups if finish else sums,
        compiler_params=PARAMS,
        cost_estimate=cost(0, 1024),
        name="group_grads",
    )(rel, halves, *lows, *rows, *earlier)


def total_kernel(groups, slots_ref, *rest):
    blocks, out_ref, acc = rest[:groups], rest[groups], rest[groups + 1]
    acc[...] = jnp.zeros_like(acc)
    for d in range(groups):
        acc[slots_ref[d]] += blocks[d][...].astype(jnp.float32)
    out_ref[...] = acc[...].astype(out_ref.dtype)


def slot_totals(slots, blocks, owned):
    groups = len(blocks)
    shape = blocks[0].shape
    return pl.pallas_call(
        functools.partial(total_kernel, groups),
        grid_spec=pltpu.PrefetchScalarGridSpec(
            num_scalar_prefetch=1,
            grid=(1,),
            in_specs=[HELD] * groups,
            out_specs=pl.BlockSpec((owned, *shape), lambda i, *_: (0, 0, 0)),
            scratch_shapes=[pltpu.VMEM((owned, *shape), jnp.float32)],
        ),
        out_shape=jax.ShapeDtypeStruct((owned, *shape), jnp.bfloat16),
        compiler_params=PARAMS,
        cost_estimate=cost(groups * blocks[0].size, 2 * (groups + owned) * blocks[0].size),
        name="slot_totals",
    )(slots, *blocks)


def early_kernel(late, slots_ref, *rest):
    blocks, (out_ref, partial_ref, acc) = rest[:-3], rest[-3:]
    acc[...] = jnp.zeros_like(acc)
    for d, block in blocks_but(late, blocks):
        acc[slots_ref[d]] += block[...].astype(jnp.float32)
    out_ref[...] = acc[...].astype(out_ref.dtype)
    partial_ref[...] = acc[slots_ref[late]]


def blocks_but(late, blocks):
    return [(d + (d >= late), block) for d, block in enumerate(blocks)]


def early_totals(slots, blocks, late, owned):
    shape = blocks[0].shape
    return pl.pallas_call(
        functools.partial(early_kernel, late),
        grid_spec=pltpu.PrefetchScalarGridSpec(
            num_scalar_prefetch=1,
            grid=(1,),
            in_specs=[HELD] * len(blocks),
            out_specs=[whole((owned, *shape)), HELD],
            scratch_shapes=[pltpu.VMEM((owned, *shape), jnp.float32)],
        ),
        out_shape=[
            jax.ShapeDtypeStruct((owned, *shape), jnp.bfloat16),
            pltpu.VMEM(shape, jnp.float32),
        ],
        compiler_params=PARAMS,
        cost_estimate=cost(0, 1024),
        name="early_totals",
    )(slots, *blocks)


def late_kernel(late, slots_ref, totals_ref, partial_ref, block_ref, out_ref, total, sem):
    total[...] = (partial_ref[...] + block_ref[...].astype(jnp.float32)).astype(total.dtype)
    copy = pltpu.make_async_copy(total, out_ref.at[slots_ref[late]], sem)
    copy.start()
    copy.wait()


def late_totals(slots, totals, partial, block, late):
    return pl.pallas_call(
        functools.partial(late_kernel, late),
        grid_spec=pltpu.PrefetchScalarGridSpec(
            num_scalar_prefetch=1,
            grid=(1,),
            in_specs=[ANY, HELD, HELD],
            out_specs=ANY,
            scratch_shapes=[pltpu.VMEM(block.shape, totals.dtype), pltpu.SemaphoreType.DMA],
        ),
        out_shape=jax.ShapeDtypeStruct(totals.shape, totals.dtype),
        input_output_aliases={1: 0},
        compiler_params=PARAMS,
        cost_estimate=cost(0, 1024),
        name="late_totals",
    )(slots, totals, partial, block)


def apart(valid, work, *args):
    out = jax.eval_shape(work, *args)
    zeros = lambda *_: jax.tree.map(lambda leaf: jnp.zeros(leaf.shape, leaf.dtype), out)
    return lax.cond(valid, work, zeros, *args)


def body(groups, parts, inputs, cotangent, factor_a, factor_b, adapter_slot, seg_adapter):
    owned = factor_a.shape[0]
    to, back = peers(groups)
    me = lax.axis_index("grp")
    matches = seg_adapter[:, :, None] == jnp.arange(adapter_slot.shape[0], dtype=jnp.int32)
    slot_all = jnp.sum(jnp.where(matches, adapter_slot, 0), axis=2)
    owner_all, local_all = slot_all // owned, slot_all % owned
    my_slots = jnp.max(jnp.where(owner_all == me, local_all, 0), axis=1)
    order = jnp.arange(groups, dtype=jnp.int32)
    slots = jnp.sum(
        jnp.where(to(me, order)[:, None] == order[None, :], my_slots[None, :], 0), axis=1
    )
    my_owners = lax.dynamic_index_in_dim(owner_all, me, 0, keepdims=False)
    rel = jnp.sum(
        jnp.where(my_owners[:, None] == back(me, order)[None, :], order[None, :], 0), axis=1
    )

    valid = me >= 0

    def send(block, d, where):
        return lax.ppermute(block, "grp", [(i, where(i, d)) for i in range(groups)])

    def send_all(blocks, where):
        return [send(block, d, where) for d, block in enumerate(blocks, 1)]

    core = lax.axis_index("tp") % 2
    halves = jnp.stack([1 - core, core])
    steps = chip_steps(parts)
    sent = jnp.bfloat16 if len(steps) <= 2 else jnp.float32
    own_factor_b, *picked_b = pick_factors(slots, factor_b, groups)
    got_b = send_all(picked_b, to)
    own_factor_a, *picked_a = pick_factors(slots, factor_a, groups)
    near_a = send(picked_a[-1], groups - 1, to)
    cot = hold(halves, cotangent)
    picked_a, got_b, cot = lax.optimization_barrier((picked_a[:-1], got_b, cot))
    far_a = send_all(picked_a, to)

    def grad_sums(rel, halves, cot, inputs, *blocks):
        give, held = give_rows(rel, halves, cot[0], blocks, True)
        got = from_other_core(parts, give)
        sums, out = chip_sums(keep_rows(rel, halves, cot[1], held, True), got, sent)
        tok = None
        for step in steps[:-1]:
            crossed = cross(parts, out, step)
            if tok is None:
                crossed, tok = lax.optimization_barrier((crossed, hold(halves, inputs)))
            sums, out = add_parts(sums, crossed, sent)
        return sums, out, tok

    sums, out, tok = apart(valid, grad_sums, rel, halves, cot, inputs, own_factor_b, *got_b)
    crossed = cross(parts, out, steps[-1])
    give, held = give_rows(rel, halves, tok[0], [own_factor_a, *far_a, near_a], False)
    got = from_other_core(parts, give)
    crossed, give = lax.optimization_barrier((crossed, give))
    low = join_parts(sums, crossed)
    other_low = from_other_core(parts, low)
    first = group_grads(rel, halves, (1,), [low], tok[1:], groups, finish=False)
    own_a, *grads_a = group_grads(
        rel, halves, (0,), [other_low], tok[:1], groups, True, so_far=first
    )
    back_a = send_all(grads_a, back)
    got, own_a = lax.optimization_barrier((got, own_a))

    def input_grads(rel, halves, cotangent, rows, held, got):
        sums, out = chip_sums(keep_rows(rel, halves, rows, held, False), got, sent)
        crossed = cross(parts, out, steps[0])
        crossed, rows = lax.optimization_barrier((crossed, hold(halves, cotangent)))
        for step in steps[1:]:
            sums, out = add_parts(sums, crossed, sent)
            crossed = cross(parts, out, step)
        low = join_parts(sums, crossed)
        other_low = from_other_core(parts, low)
        first = group_grads(rel, halves, (1,), [low], rows[1:], groups, finish=False)
        return group_grads(rel, halves, (0,), [other_low], rows[:1], groups, so_far=first)

    own_b, *grads_b = apart(valid, input_grads, rel, halves, cotangent, tok[1], held, got)
    grads_b, back_a = lax.optimization_barrier((grads_b, back_a))
    back_b = send_all(grads_b, back)
    grad_a = slot_totals(slots, [own_a, *back_a], owned)
    late = min(2, groups - 1)
    early = [own_b, *back_b[: late - 1], *back_b[late:]]
    totals, partial = early_totals(slots, early, late, owned)
    grad_b = late_totals(slots, totals, partial, back_b[late - 1], late)
    return grad_a, grad_b


def solution(mesh):
    return jax.shard_map(
        functools.partial(body, mesh.shape["grp"], mesh.shape["tp"]),
        mesh=mesh,
        in_specs=(
            P("grp", "tp"),
            P("grp", "tp"),
            P("grp", "tp", None),
            P("grp", None, "tp"),
            P(),
            P(),
        ),
        out_specs=(P("grp", "tp", None), P("grp", None, "tp")),
        check_vma=False,
    )
```

```python
import functools

import jax
import jax.numpy as jnp
from jax import lax
from jax.experimental import pallas as pl
from jax.experimental.pallas import tpu as pltpu
from jax.sharding import PartitionSpec as P

VMEM_LIMIT = 12 * 1024 * 1024
ANY = pl.BlockSpec(memory_space=pl.ANY)
HELD = pl.BlockSpec(memory_space=pltpu.VMEM)
PARAMS = pltpu.CompilerParams(vmem_limit_bytes=VMEM_LIMIT)


def cost(flops, moved):
    return pl.CostEstimate(flops=flops, bytes_accessed=moved, transcendentals=0)


def peers(groups):
    if groups & (groups - 1) == 0:
        across = lambda i, d: i ^ ((groups - d) % groups)
        return across, across
    return (lambda i, d: (i + d) % groups), (lambda i, d: (i + groups - d) % groups)


def step_segments(seg_count, most):
    return max(n for n in range(1, most + 1) if seg_count % n == 0)


def whole(shape):
    return pl.BlockSpec(shape, lambda i, *_: (0,) * len(shape))


def pick_kernel(count, slots_ref, *rest):
    for source, out in zip(rest[:count], rest[count:]):
        out[...] = source[0]


def pick_factors(slots, factor, groups):
    block, count = factor.shape[1:], groups - 1
    return pl.pallas_call(
        functools.partial(pick_kernel, count),
        grid_spec=pltpu.PrefetchScalarGridSpec(
            num_scalar_prefetch=1,
            grid=(1,),
            in_specs=[
                pl.BlockSpec((1, *block), lambda i, slots, d=d: (slots[d], 0, 0))
                for d in range(1, groups)
            ],
            out_specs=[whole(block)] * count,
        ),
        out_shape=[jax.ShapeDtypeStruct(block, factor.dtype)] * count,
        compiler_params=PARAMS,
        cost_estimate=cost(0, 4 * count * block[0] * block[1]),
        name="pick_factors",
    )(slots, *[pltpu.with_memory_space_constraint(factor, pltpu.HBM)] * count)


def times_factors(seg_rows, flip, base, spans, rel_ref, rows, held, out_ref):
    contract = (((1,), (1 if flip else 0,)), ((), ()))
    for arrived, segs in spans:
        arrived()
        for n in segs:
            at = pl.ds(n * seg_rows, seg_rows)
            out_ref[at, :] = lax.dot_general(
                rows[at, :], held[rel_ref[base + n]], contract, preferred_element_type=jnp.float32
            ).astype(out_ref.dtype)


def give_kernel(seg_rows, flip, rel_ref, halves_ref, slots_ref, rows, store_ref, *rest):
    blocks, (out_ref, held, sems) = rest[:-3], rest[-3:]
    sources = [store_ref.at[slots_ref[0]], *blocks]
    fetches = [pltpu.make_async_copy(s, held.at[d], sems.at[d]) for d, s in enumerate(sources)]
    for copy in fetches:
        copy.start()
    for copy in fetches:
        copy.wait()
    segs = rows.shape[0] // seg_rows
    spans = [(lambda: None, range(segs))]
    times_factors(seg_rows, flip, halves_ref[0] * segs, spans, rel_ref, rows, held, out_ref)


def give_rows(rel, halves, slots, rows, store, blocks, flip):
    groups = len(blocks) + 1
    shape = (rows.shape[0], blocks[0].shape[0 if flip else 1])
    return pl.pallas_call(
        functools.partial(give_kernel, 2 * rows.shape[0] // rel.shape[0], flip),
        grid_spec=pltpu.PrefetchScalarGridSpec(
            num_scalar_prefetch=3,
            grid=(1,),
            in_specs=[HELD] + [ANY] * groups,
            out_specs=[whole(shape), HELD],
            scratch_shapes=[pltpu.SemaphoreType.DMA((groups,))],
        ),
        out_shape=[
            jax.ShapeDtypeStruct(shape, jnp.bfloat16),
            pltpu.VMEM((groups, *blocks[0].shape), rows.dtype),
        ],
        compiler_params=PARAMS,
        cost_estimate=cost(2 * rows.size * shape[1], 2 * rows.size),
        name="give_rows",
    )(rel, halves, slots, rows, pltpu.with_memory_space_constraint(store, pltpu.HBM), *blocks)


def keep_kernel(seg_rows, flip, rel_ref, halves_ref, rows, held, out_ref):
    segs = rows.shape[0] // seg_rows
    spans = [(lambda: None, range(segs))]
    times_factors(seg_rows, flip, halves_ref[1] * segs, spans, rel_ref, rows, held, out_ref)


def keep_rows(rel, halves, rows, held, flip):
    count, rank = rows.shape[0], held.shape[1 if flip else 2]
    return pl.pallas_call(
        functools.partial(keep_kernel, 2 * count // rel.shape[0], flip),
        grid_spec=pltpu.PrefetchScalarGridSpec(
            num_scalar_prefetch=2,
            grid=(1,),
            in_specs=[HELD, HELD],
            out_specs=whole((count, rank)),
        ),
        out_shape=jax.ShapeDtypeStruct((count, rank), jnp.float32),
        compiler_params=PARAMS,
        cost_estimate=cost(2 * rows.size * rank, 2 * rows.size),
        name="keep_rows",
    )(rel, halves, rows, held)


def hold_kernel(halves_ref, rows_ref, *rest):
    outs, sems = rest[:-1], rest[-1]
    count = outs[0].shape[0]
    copies = [
        pltpu.make_async_copy(
            rows_ref.at[pl.ds(pl.multiple_of(halves_ref[k] * count, 16), count)], out, sems.at[k]
        )
        for k, out in enumerate(outs)
    ]
    for copy in copies:
        copy.start()
    for copy in copies:
        copy.wait()


def hold(halves, rows):
    shape = (rows.shape[0] // 2, rows.shape[1])
    return pl.pallas_call(
        hold_kernel,
        grid_spec=pltpu.PrefetchScalarGridSpec(
            num_scalar_prefetch=1,
            grid=(1,),
            in_specs=[ANY],
            out_specs=[HELD] * 2,
            scratch_shapes=[pltpu.SemaphoreType.DMA((2,))],
        ),
        out_shape=[pltpu.VMEM(shape, rows.dtype)] * 2,
        compiler_params=PARAMS,
        cost_estimate=cost(0, 4 * rows.size),
        name="hold_rows",
    )(halves, pltpu.with_memory_space_constraint(rows, pltpu.HBM))


def from_other_core(parts, block):
    return lax.ppermute(block, "tp", [(i, i ^ 1) for i in range(parts)])


def split_sums(total, sent, outs):
    rows = outs[0].shape[0]
    for n in range(2):
        part = total(pl.ds(n * rows, rows))
        outs[n][...] = part
        outs[2 + n][...] = part.astype(sent)


def chip_kernel(sent, kept_ref, got_ref, *outs):
    split_sums(lambda at: kept_ref[at, :] + got_ref[at, :].astype(jnp.float32), sent, outs)


def keep_sums_kernel(seg_rows, flip, sent, rel_ref, halves_ref, rows, held, got_ref, *rest):
    outs, (kept, got, sem) = rest[:4], rest[4:]
    copy = pltpu.make_async_copy(got_ref, got, sem)
    copy.start()
    keep_kernel(seg_rows, flip, rel_ref, halves_ref, rows, held, kept)
    copy.wait()
    chip_kernel(sent, kept, got, *outs)


def keep_sums(rel, halves, rows, held, got, sent, flip):
    count, rank = got.shape
    part = (count // 2, rank)
    outs = pl.pallas_call(
        functools.partial(keep_sums_kernel, 2 * count // rel.shape[0], flip, sent),
        grid_spec=pltpu.PrefetchScalarGridSpec(
            num_scalar_prefetch=2,
            grid=(1,),
            in_specs=[HELD, HELD, ANY],
            out_specs=[HELD] * 4,
            scratch_shapes=[
                pltpu.VMEM((count, rank), jnp.float32),
                pltpu.VMEM((count, rank), got.dtype),
                pltpu.SemaphoreType.DMA,
            ],
        ),
        out_shape=[pltpu.VMEM(part, t) for t in (jnp.float32,) * 2 + (sent,) * 2],
        compiler_params=PARAMS,
        cost_estimate=cost(2 * rows.size * rank, 2 * rows.size),
        name="keep_sums",
    )(rel, halves, rows, held, got)
    return outs[:2], outs[2:]


def chip_sums(kept, got, sent):
    shape = (kept.shape[0] // 2, kept.shape[1])
    outs = pl.pallas_call(
        functools.partial(chip_kernel, sent),
        out_specs=[HELD] * 4,
        out_shape=[pltpu.VMEM(shape, t) for t in (jnp.float32,) * 2 + (sent,) * 2],
        compiler_params=PARAMS,
        cost_estimate=cost(0, 1024),
        name="chip_sums",
    )(kept, got)
    return outs[:2], outs[2:]


def add_kernel(sent, *refs):
    for n in range(2):
        total = refs[n][...] + refs[2 + n][...].astype(jnp.float32)
        refs[4 + n][...] = total
        refs[6 + n][...] = total.astype(sent)


def add_parts(sums, crossed, sent):
    outs = pl.pallas_call(
        functools.partial(add_kernel, sent),
        out_specs=[HELD] * 4,
        out_shape=[pltpu.VMEM(sums[0].shape, t) for t in (jnp.float32,) * 2 + (sent,) * 2],
        compiler_params=PARAMS,
        cost_estimate=cost(0, 1024),
        name="add_parts",
    )(*sums, *crossed)
    return outs[:2], outs[2:]


def join_kernel(*refs):
    rows = refs[0].shape[0]
    for n in range(2):
        total = refs[n][...] + refs[2 + n][...].astype(jnp.float32)
        refs[4][pl.ds(n * rows, rows), :] = total.astype(refs[4].dtype)


def join_parts(sums, crossed):
    rows, rank = sums[0].shape
    return pl.pallas_call(
        join_kernel,
        out_shape=jax.ShapeDtypeStruct((2 * rows, rank), jnp.bfloat16),
        compiler_params=PARAMS,
        cost_estimate=cost(0, 1024),
        name="join_parts",
    )(*sums, *crossed)


def chip_steps(parts):
    bits = (parts // 2).bit_length() - 1
    return [[(step + part * (bits // 2)) % bits for part in range(2)] for step in range(bits)]


def cross(parts, blocks, step):
    return [
        lax.ppermute(block, "tp", [(i, i ^ (2 << bit)) for i in range(parts)])
        for block, bit in zip(blocks, step)
    ]


def grad_kernel(order, resume, finish, seg_rows, flip, rel_ref, halves_ref, *refs):
    lows, rows, refs = refs[: len(order)], refs[len(order) : 2 * len(order)], refs[2 * len(order) :]
    if resume:
        so_far, refs = refs[0], refs[1:]
    outs, acc = (refs[:-1], refs[-1]) if finish else ((), refs[0])
    acc[...] = so_far[...] if resume else jnp.zeros_like(acc)
    segs = rows[0].shape[0] // seg_rows
    unroll = step_segments(segs, 15)
    for half, low, tokens in zip(order, lows, rows):

        def add_segments(step, carry, half=half, low=low, tokens=tokens):
            for n in range(unroll):
                seg = step * unroll + n
                at = pl.ds(pl.multiple_of(seg * seg_rows, seg_rows), seg_rows)
                acc[rel_ref[halves_ref[half] * segs + seg]] += lax.dot_general(
                    low[at, :],
                    tokens[at, :],
                    (((0,), (0,)), ((), ())),
                    preferred_element_type=jnp.float32,
                )
            return carry

        lax.fori_loop(0, segs // unroll, add_segments, 0)
    for d, out in enumerate(outs):
        total = acc[d].astype(jnp.bfloat16)
        out[...] = total.T if flip else total


def group_grads(
    rel, halves, order, lows, rows, groups, flip=False, so_far=None, finish=True, stay=False
):
    seg_count = rel.shape[0]
    count, features = rows[0].shape
    rank = lows[0].shape[1]
    shape = (features, rank) if flip else (rank, features)
    sums = pltpu.VMEM((groups, rank, features), jnp.float32)
    gradient = (pltpu.VMEM if stay else jax.ShapeDtypeStruct)(shape, jnp.bfloat16)
    earlier = [] if so_far is None else [so_far]
    return pl.pallas_call(
        functools.partial(
            grad_kernel, order, bool(earlier), finish, 2 * count // seg_count, flip
        ),
        grid_spec=pltpu.PrefetchScalarGridSpec(
            num_scalar_prefetch=2,
            grid=(1,),
            in_specs=[HELD] * (2 * len(order) + len(earlier)),
            out_specs=[HELD if stay else whole(shape)] * groups if finish else HELD,
            scratch_shapes=[sums] if finish else [],
        ),
        out_shape=[gradient] * groups if finish else sums,
        compiler_params=PARAMS,
        cost_estimate=cost(0, 1024),
        name="group_grads",
    )(rel, halves, *lows, *rows, *earlier)


def total_kernel(groups, slots_ref, *rest):
    blocks, out_ref, acc = rest[:groups], rest[groups], rest[groups + 1]
    acc[...] = jnp.zeros_like(acc)
    for d in range(groups):
        acc[slots_ref[d]] += blocks[d][...].astype(jnp.float32)
    out_ref[...] = acc[...].astype(out_ref.dtype)


def slot_totals(slots, blocks, owned):
    groups = len(blocks)
    shape = blocks[0].shape
    return pl.pallas_call(
        functools.partial(total_kernel, groups),
        grid_spec=pltpu.PrefetchScalarGridSpec(
            num_scalar_prefetch=1,
            grid=(1,),
            in_specs=[HELD] * groups,
            out_specs=pl.BlockSpec((owned, *shape), lambda i, *_: (0, 0, 0)),
            scratch_shapes=[pltpu.VMEM((owned, *shape), jnp.float32)],
        ),
        out_shape=jax.ShapeDtypeStruct((owned, *shape), jnp.bfloat16),
        compiler_params=PARAMS,
        cost_estimate=cost(groups * blocks[0].size, 2 * (groups + owned) * blocks[0].size),
        name="slot_totals",
    )(slots, *blocks)


def early_kernel(late, slots_ref, *rest):
    blocks, (out_ref, partial_ref, acc) = rest[:-3], rest[-3:]
    acc[...] = jnp.zeros_like(acc)
    for d, block in blocks_but(late, blocks):
        acc[slots_ref[d]] += block[...].astype(jnp.float32)
    out_ref[...] = acc[...].astype(out_ref.dtype)
    partial_ref[...] = acc[slots_ref[late]]


def blocks_but(late, blocks):
    return [(d + (d >= late), block) for d, block in enumerate(blocks)]


def early_totals(slots, blocks, late, owned):
    shape = blocks[0].shape
    return pl.pallas_call(
        functools.partial(early_kernel, late),
        grid_spec=pltpu.PrefetchScalarGridSpec(
            num_scalar_prefetch=1,
            grid=(1,),
            in_specs=[HELD] * len(blocks),
            out_specs=[whole((owned, *shape)), HELD],
            scratch_shapes=[pltpu.VMEM((owned, *shape), jnp.float32)],
        ),
        out_shape=[
            jax.ShapeDtypeStruct((owned, *shape), jnp.bfloat16),
            pltpu.VMEM(shape, jnp.float32),
        ],
        compiler_params=PARAMS,
        cost_estimate=cost(0, 1024),
        name="early_totals",
    )(slots, *blocks)


def late_kernel(late, slots_ref, totals_ref, partial_ref, block_ref, out_ref, total, sem):
    total[...] = (partial_ref[...] + block_ref[...].astype(jnp.float32)).astype(total.dtype)
    copy = pltpu.make_async_copy(total, out_ref.at[slots_ref[late]], sem)
    copy.start()
    copy.wait()


def late_totals(slots, totals, partial, block, late):
    return pl.pallas_call(
        functools.partial(late_kernel, late),
        grid_spec=pltpu.PrefetchScalarGridSpec(
            num_scalar_prefetch=1,
            grid=(1,),
            in_specs=[ANY, HELD, HELD],
            out_specs=ANY,
            scratch_shapes=[pltpu.VMEM(block.shape, totals.dtype), pltpu.SemaphoreType.DMA],
        ),
        out_shape=jax.ShapeDtypeStruct(totals.shape, totals.dtype),
        input_output_aliases={1: 0},
        compiler_params=PARAMS,
        cost_estimate=cost(0, 1024),
        name="late_totals",
    )(slots, totals, partial, block)


def apart(valid, work, *args):
    out = jax.eval_shape(work, *args)
    zeros = lambda *_: jax.tree.map(lambda leaf: jnp.zeros(leaf.shape, leaf.dtype), out)
    return lax.cond(valid, work, zeros, *args)


def body(groups, parts, inputs, cotangent, factor_a, factor_b, adapter_slot, seg_adapter):
    owned = factor_a.shape[0]
    to, back = peers(groups)
    me = lax.axis_index("grp")
    matches = seg_adapter[:, :, None] == jnp.arange(adapter_slot.shape[0], dtype=jnp.int32)
    slot_all = jnp.sum(jnp.where(matches, adapter_slot, 0), axis=2)
    owner_all, local_all = slot_all // owned, slot_all % owned
    my_slots = jnp.max(jnp.where(owner_all == me, local_all, 0), axis=1)
    order = jnp.arange(groups, dtype=jnp.int32)
    slots = jnp.sum(
        jnp.where(to(me, order)[:, None] == order[None, :], my_slots[None, :], 0), axis=1
    )
    my_owners = lax.dynamic_index_in_dim(owner_all, me, 0, keepdims=False)
    rel = jnp.sum(
        jnp.where(my_owners[:, None] == back(me, order)[None, :], order[None, :], 0), axis=1
    )

    valid = me >= 0

    def send(block, d, where):
        return lax.ppermute(block, "grp", [(i, where(i, d)) for i in range(groups)])

    def send_all(blocks, where):
        return [send(block, d, where) for d, block in enumerate(blocks, 1)]

    core = lax.axis_index("tp") % 2
    halves = jnp.stack([1 - core, core])
    steps = chip_steps(parts)
    sent = jnp.bfloat16 if len(steps) <= 2 else jnp.float32
    picked_b = pick_factors(slots, factor_b, groups)
    got_b = send_all(picked_b, to)
    picked_a = pick_factors(slots, factor_a, groups)
    near_a = send(picked_a[-1], groups - 1, to)
    cot = hold(halves, cotangent)
    picked_a, got_b, cot = lax.optimization_barrier((picked_a[:-1], got_b, cot))
    far_a = send_all(picked_a, to)

    def grad_sums(rel, halves, slots, cot, inputs, store, *blocks):
        give, held = give_rows(rel, halves, slots, cot[0], store, blocks, True)
        got = from_other_core(parts, give)
        sums, out = chip_sums(keep_rows(rel, halves, cot[1], held, True), got, sent)
        tok = None
        for step in steps[:-1]:
            crossed = cross(parts, out, step)
            if tok is None:
                crossed, tok = lax.optimization_barrier((crossed, hold(halves, inputs)))
            sums, out = add_parts(sums, crossed, sent)
        return sums, out, tok

    sums, out, tok = apart(valid, grad_sums, rel, halves, slots, cot, inputs, factor_b, *got_b)
    crossed = cross(parts, out, steps[-1])
    give, held = give_rows(rel, halves, slots, tok[0], factor_a, [*far_a, near_a], False)
    got = from_other_core(parts, give)
    crossed, give = lax.optimization_barrier((crossed, give))
    low = join_parts(sums, crossed)
    other_low = from_other_core(parts, low)
    first = group_grads(rel, halves, (1,), [low], tok[1:], groups, finish=False)
    own_a, *grads_a = group_grads(
        rel, halves, (0,), [other_low], tok[:1], groups, True, so_far=first
    )
    back_a = send_all(grads_a, back)
    got, own_a = lax.optimization_barrier((got, own_a))

    def input_grads(rel, halves, cotangent, rows, held, got):
        sums, out = keep_sums(rel, halves, rows, held, got, sent, False)
        crossed = cross(parts, out, steps[0])
        crossed, rows = lax.optimization_barrier((crossed, hold(halves, cotangent)))
        for step in steps[1:]:
            sums, out = add_parts(sums, crossed, sent)
            crossed = cross(parts, out, step)
        low = join_parts(sums, crossed)
        other_low = from_other_core(parts, low)
        first = group_grads(rel, halves, (1,), [low], rows[1:], groups, finish=False)
        return group_grads(
            rel, halves, (0,), [other_low], rows[:1], groups, so_far=first, stay=True
        )

    own_b, *grads_b = apart(valid, input_grads, rel, halves, cotangent, tok[1], held, got)
    grads_b, back_a = lax.optimization_barrier((grads_b, back_a))
    back_b = send_all(grads_b, back)
    grad_a = slot_totals(slots, [own_a, *back_a], owned)
    late = min(2, groups - 1)
    early = [own_b, *back_b[: late - 1], *back_b[late:]]
    totals, partial = early_totals(slots, early, late, owned)
    grad_b = late_totals(slots, totals, partial, back_b[late - 1], late)
    return grad_a, grad_b


def solution(mesh):
    return jax.shard_map(
        functools.partial(body, mesh.shape["grp"], mesh.shape["tp"]),
        mesh=mesh,
        in_specs=(
            P("grp", "tp"),
            P("grp", "tp"),
            P("grp", "tp", None),
            P("grp", None, "tp"),
            P(),
            P(),
        ),
        out_specs=(P("grp", "tp", None), P("grp", None, "tp")),
        check_vma=False,
    )
```

```python
import functools

import jax
import jax.numpy as jnp
from jax import lax
from jax.experimental import pallas as pl
from jax.experimental.pallas import tpu as pltpu
from jax.sharding import PartitionSpec as P

VMEM_LIMIT = 14 * 1024 * 1024
ANY = pl.BlockSpec(memory_space=pl.ANY)
HELD = pl.BlockSpec(memory_space=pltpu.VMEM)
PARAMS = pltpu.CompilerParams(vmem_limit_bytes=VMEM_LIMIT)


def cost(flops, moved):
    return pl.CostEstimate(flops=flops, bytes_accessed=moved, transcendentals=0)


def peers(groups):
    if groups & (groups - 1) == 0:
        across = lambda i, d: i ^ ((groups - d) % groups)
        return across, across
    return (lambda i, d: (i + d) % groups), (lambda i, d: (i + groups - d) % groups)


def step_segments(seg_count, most):
    return max(n for n in range(1, most + 1) if seg_count % n == 0)


def whole(shape):
    return pl.BlockSpec(shape, lambda i, *_: (0,) * len(shape))


def pick_kernel(count, slots_ref, *rest):
    for source, out in zip(rest[:count], rest[count:]):
        out[...] = source[0]


def pick_factors(slots, factor, indices):
    block, count = factor.shape[1:], len(indices)
    return pl.pallas_call(
        functools.partial(pick_kernel, count),
        grid_spec=pltpu.PrefetchScalarGridSpec(
            num_scalar_prefetch=1,
            grid=(1,),
            in_specs=[
                pl.BlockSpec((1, *block), lambda i, slots, d=d: (slots[d], 0, 0)) for d in indices
            ],
            out_specs=[whole(block)] * count,
        ),
        out_shape=[jax.ShapeDtypeStruct(block, factor.dtype)] * count,
        compiler_params=PARAMS,
        cost_estimate=cost(0, 4 * count * block[0] * block[1]),
        name="pick_factors",
    )(slots, *[pltpu.with_memory_space_constraint(factor, pltpu.HBM)] * count)


def times_factors(seg_rows, flip, base, spans, rel_ref, rows, held, out_ref):
    contract = (((1,), (1 if flip else 0,)), ((), ()))
    for arrived, segs in spans:
        arrived()
        for n in segs:
            at = pl.ds(n * seg_rows, seg_rows)
            out_ref[at, :] = lax.dot_general(
                rows[at, :], held[rel_ref[base + n]], contract, preferred_element_type=jnp.float32
            ).astype(out_ref.dtype)


def give_kernel(seg_rows, flip, rel_ref, halves_ref, rows, *rest):
    blocks, (out_ref, held, sems) = rest[:-3], rest[-3:]
    fetches = [pltpu.make_async_copy(block, held.at[d], sems.at[d]) for d, block in enumerate(blocks)]
    for copy in fetches:
        copy.start()
    for copy in fetches:
        copy.wait()
    segs = rows.shape[0] // seg_rows
    spans = [(lambda: None, range(segs))]
    times_factors(seg_rows, flip, halves_ref[0] * segs, spans, rel_ref, rows, held, out_ref)


def give_rows(rel, halves, rows, blocks, flip):
    groups = len(blocks)
    shape = (rows.shape[0], blocks[0].shape[0 if flip else 1])
    return pl.pallas_call(
        functools.partial(give_kernel, 2 * rows.shape[0] // rel.shape[0], flip),
        grid_spec=pltpu.PrefetchScalarGridSpec(
            num_scalar_prefetch=2,
            grid=(1,),
            in_specs=[HELD] + [ANY] * groups,
            out_specs=[whole(shape), HELD],
            scratch_shapes=[pltpu.SemaphoreType.DMA((groups,))],
        ),
        out_shape=[
            jax.ShapeDtypeStruct(shape, jnp.bfloat16),
            pltpu.VMEM((groups, *blocks[0].shape), rows.dtype),
        ],
        compiler_params=PARAMS,
        cost_estimate=cost(2 * rows.size * shape[1], 2 * rows.size),
        name="give_rows",
    )(rel, halves, rows, *blocks)


def keep_kernel(seg_rows, flip, rel_ref, halves_ref, rows, held, out_ref):
    segs = rows.shape[0] // seg_rows
    spans = [(lambda: None, range(segs))]
    times_factors(seg_rows, flip, halves_ref[1] * segs, spans, rel_ref, rows, held, out_ref)


def keep_rows(rel, halves, rows, held, flip):
    count, rank = rows.shape[0], held.shape[1 if flip else 2]
    return pl.pallas_call(
        functools.partial(keep_kernel, 2 * count // rel.shape[0], flip),
        grid_spec=pltpu.PrefetchScalarGridSpec(
            num_scalar_prefetch=2,
            grid=(1,),
            in_specs=[HELD, HELD],
            out_specs=whole((count, rank)),
        ),
        out_shape=jax.ShapeDtypeStruct((count, rank), jnp.float32),
        compiler_params=PARAMS,
        cost_estimate=cost(2 * rows.size * rank, 2 * rows.size),
        name="keep_rows",
    )(rel, halves, rows, held)


def hold_kernel(own, halves_ref, *refs):
    if own:
        slots_ref, store_ref, refs = refs[0], refs[2], (refs[1], *refs[3:])
    rows_ref, outs, sems = refs[0], refs[1:-1], refs[-1]
    count = outs[0].shape[0]
    sources = [
        rows_ref.at[pl.ds(pl.multiple_of(halves_ref[k] * count, 16), count)] for k in range(2)
    ]
    if own:
        sources.append(store_ref.at[slots_ref[0]])
    copies = [
        pltpu.make_async_copy(source, out, sems.at[k])
        for k, (source, out) in enumerate(zip(sources, outs))
    ]
    for copy in copies:
        copy.start()
    for copy in copies:
        copy.wait()


def hold(halves, rows, slots=None, store=None):
    own = store is not None
    outs = [pltpu.VMEM((rows.shape[0] // 2, rows.shape[1]), rows.dtype)] * 2
    if own:
        outs.append(pltpu.VMEM(store.shape[1:], store.dtype))
    hbm = [pltpu.with_memory_space_constraint(x, pltpu.HBM) for x in ([rows, store] if own else [rows])]
    return pl.pallas_call(
        functools.partial(hold_kernel, own),
        grid_spec=pltpu.PrefetchScalarGridSpec(
            num_scalar_prefetch=2 if own else 1,
            grid=(1,),
            in_specs=[ANY] * len(hbm),
            out_specs=[HELD] * len(outs),
            scratch_shapes=[pltpu.SemaphoreType.DMA((len(outs),))],
        ),
        out_shape=outs,
        compiler_params=PARAMS,
        cost_estimate=cost(0, 4 * rows.size),
        name="hold_rows",
    )(*([halves, slots] if own else [halves]), *hbm)


def from_other_core(parts, block):
    return lax.ppermute(block, "tp", [(i, i ^ 1) for i in range(parts)])


def chip_kernel(sent, kept_ref, got_ref, *outs):
    start = 0
    for n in range(2):
        at = pl.ds(start, outs[n].shape[0])
        start += outs[n].shape[0]
        total = kept_ref[at, :] + got_ref[at, :].astype(jnp.float32)
        outs[n][...] = total
        outs[2 + n][...] = total.astype(sent)


def chip_sums(kept, got, sent):
    shape = (kept.shape[0] // 2, kept.shape[1])
    outs = pl.pallas_call(
        functools.partial(chip_kernel, sent),
        out_specs=[HELD] * 4,
        out_shape=[pltpu.VMEM(shape, t) for t in (jnp.float32,) * 2 + (sent,) * 2],
        compiler_params=PARAMS,
        cost_estimate=cost(0, 1024),
        name="chip_sums",
    )(kept, got)
    return outs[:2], outs[2:]


def add_kernel(sent, *refs):
    for n in range(2):
        total = refs[n][...] + refs[2 + n][...].astype(jnp.float32)
        refs[4 + n][...] = total
        refs[6 + n][...] = total.astype(sent)


def add_parts(sums, crossed, sent):
    outs = pl.pallas_call(
        functools.partial(add_kernel, sent),
        out_specs=[HELD] * 4,
        out_shape=[pltpu.VMEM(sums[0].shape, t) for t in (jnp.float32,) * 2 + (sent,) * 2],
        compiler_params=PARAMS,
        cost_estimate=cost(0, 1024),
        name="add_parts",
    )(*sums, *crossed)
    return outs[:2], outs[2:]


def join_kernel(*refs):
    rows = refs[0].shape[0]
    for n in range(2):
        total = refs[n][...] + refs[2 + n][...].astype(jnp.float32)
        refs[4][pl.ds(n * rows, rows), :] = total.astype(refs[4].dtype)


def join_parts(sums, crossed):
    rows, rank = sums[0].shape
    return pl.pallas_call(
        join_kernel,
        out_shape=jax.ShapeDtypeStruct((2 * rows, rank), jnp.bfloat16),
        compiler_params=PARAMS,
        cost_estimate=cost(0, 1024),
        name="join_parts",
    )(*sums, *crossed)


def chip_steps(parts):
    bits = (parts // 2).bit_length() - 1
    return [[(step + part * (bits // 2)) % bits for part in range(2)] for step in range(bits)]


def cross(parts, blocks, step):
    return [
        lax.ppermute(block, "tp", [(i, i ^ (2 << bit)) for i in range(parts)])
        for block, bit in zip(blocks, step)
    ]


def grad_kernel(order, resume, finish, seg_rows, flip, rel_ref, halves_ref, *refs):
    lows, rows, refs = refs[: len(order)], refs[len(order) : 2 * len(order)], refs[2 * len(order) :]
    if resume:
        so_far, refs = refs[0], refs[1:]
    outs, acc = (refs[:-1], refs[-1]) if finish else ((), refs[0])
    acc[...] = so_far[...] if resume else jnp.zeros_like(acc)
    segs = rows[0].shape[0] // seg_rows
    unroll = step_segments(segs, 15)
    for half, low, tokens in zip(order, lows, rows):

        def add_segments(step, carry, half=half, low=low, tokens=tokens):
            for n in range(unroll):
                seg = step * unroll + n
                at = pl.ds(pl.multiple_of(seg * seg_rows, seg_rows), seg_rows)
                acc[rel_ref[halves_ref[half] * segs + seg]] += lax.dot_general(
                    low[at, :],
                    tokens[at, :],
                    (((0,), (0,)), ((), ())),
                    preferred_element_type=jnp.float32,
                )
            return carry

        lax.fori_loop(0, segs // unroll, add_segments, 0)
    for d, out in enumerate(outs):
        total = acc[d].astype(jnp.bfloat16)
        out[...] = total.T if flip else total


def group_grads(rel, halves, order, lows, rows, groups, flip=False, so_far=None, finish=True):
    seg_count = rel.shape[0]
    count, features = rows[0].shape
    rank = lows[0].shape[1]
    shape = (features, rank) if flip else (rank, features)
    sums = pltpu.VMEM((groups, rank, features), jnp.float32)
    earlier = [] if so_far is None else [so_far]
    return pl.pallas_call(
        functools.partial(
            grad_kernel, order, bool(earlier), finish, 2 * count // seg_count, flip
        ),
        grid_spec=pltpu.PrefetchScalarGridSpec(
            num_scalar_prefetch=2,
            grid=(1,),
            in_specs=[HELD] * (2 * len(order) + len(earlier)),
            out_specs=[whole(shape)] * groups if finish else HELD,
            scratch_shapes=[sums] if finish else [],
        ),
        out_shape=[jax.ShapeDtypeStruct(shape, jnp.bfloat16)] * groups if finish else sums,
        compiler_params=PARAMS,
        cost_estimate=cost(0, 1024),
        name="group_grads",
    )(rel, halves, *lows, *rows, *earlier)


def total_kernel(groups, slots_ref, *rest):
    blocks, out_ref, acc = rest[:groups], rest[groups], rest[groups + 1]
    acc[...] = jnp.zeros_like(acc)
    for d in range(groups):
        acc[slots_ref[d]] += blocks[d][...].astype(jnp.float32)
    out_ref[...] = acc[...].astype(out_ref.dtype)


def slot_totals(slots, blocks, owned):
    groups = len(blocks)
    shape = blocks[0].shape
    return pl.pallas_call(
        functools.partial(total_kernel, groups),
        grid_spec=pltpu.PrefetchScalarGridSpec(
            num_scalar_prefetch=1,
            grid=(1,),
            in_specs=[HELD] * groups,
            out_specs=pl.BlockSpec((owned, *shape), lambda i, *_: (0, 0, 0)),
            scratch_shapes=[pltpu.VMEM((owned, *shape), jnp.float32)],
        ),
        out_shape=jax.ShapeDtypeStruct((owned, *shape), jnp.bfloat16),
        compiler_params=PARAMS,
        cost_estimate=cost(groups * blocks[0].size, 2 * (groups + owned) * blocks[0].size),
        name="slot_totals",
    )(slots, *blocks)


def early_kernel(late, slots_ref, *rest):
    blocks, (out_ref, partial_ref, acc) = rest[:-3], rest[-3:]
    acc[...] = jnp.zeros_like(acc)
    for d, block in blocks_but(late, blocks):
        acc[slots_ref[d]] += block[...].astype(jnp.float32)
    out_ref[...] = acc[...].astype(out_ref.dtype)
    partial_ref[...] = acc[slots_ref[late]]


def blocks_but(late, blocks):
    return [(d + (d >= late), block) for d, block in enumerate(blocks)]


def early_totals(slots, blocks, late, owned):
    shape = blocks[0].shape
    return pl.pallas_call(
        functools.partial(early_kernel, late),
        grid_spec=pltpu.PrefetchScalarGridSpec(
            num_scalar_prefetch=1,
            grid=(1,),
            in_specs=[HELD] * len(blocks),
            out_specs=[whole((owned, *shape)), HELD],
            scratch_shapes=[pltpu.VMEM((owned, *shape), jnp.float32)],
        ),
        out_shape=[
            jax.ShapeDtypeStruct((owned, *shape), jnp.bfloat16),
            pltpu.VMEM(shape, jnp.float32),
        ],
        compiler_params=PARAMS,
        cost_estimate=cost(0, 1024),
        name="early_totals",
    )(slots, *blocks)


def late_kernel(late, slots_ref, totals_ref, partial_ref, block_ref, out_ref, total, sem):
    total[...] = (partial_ref[...] + block_ref[...].astype(jnp.float32)).astype(total.dtype)
    copy = pltpu.make_async_copy(total, out_ref.at[slots_ref[late]], sem)
    copy.start()
    copy.wait()


def late_totals(slots, totals, partial, block, late):
    return pl.pallas_call(
        functools.partial(late_kernel, late),
        grid_spec=pltpu.PrefetchScalarGridSpec(
            num_scalar_prefetch=1,
            grid=(1,),
            in_specs=[ANY, HELD, HELD],
            out_specs=ANY,
            scratch_shapes=[pltpu.VMEM(block.shape, totals.dtype), pltpu.SemaphoreType.DMA],
        ),
        out_shape=jax.ShapeDtypeStruct(totals.shape, totals.dtype),
        input_output_aliases={1: 0},
        compiler_params=PARAMS,
        cost_estimate=cost(0, 1024),
        name="late_totals",
    )(slots, totals, partial, block)


def apart(valid, work, *args):
    out = jax.eval_shape(work, *args)
    zeros = lambda *_: jax.tree.map(lambda leaf: jnp.zeros(leaf.shape, leaf.dtype), out)
    return lax.cond(valid, work, zeros, *args)


def body(groups, parts, inputs, cotangent, factor_a, factor_b, adapter_slot, seg_adapter):
    owned = factor_a.shape[0]
    to, back = peers(groups)
    me = lax.axis_index("grp")
    matches = seg_adapter[:, :, None] == jnp.arange(adapter_slot.shape[0], dtype=jnp.int32)
    slot_all = jnp.sum(jnp.where(matches, adapter_slot, 0), axis=2)
    owner_all, local_all = slot_all // owned, slot_all % owned
    my_slots = jnp.max(jnp.where(owner_all == me, local_all, 0), axis=1)
    order = jnp.arange(groups, dtype=jnp.int32)
    slots = jnp.sum(
        jnp.where(to(me, order)[:, None] == order[None, :], my_slots[None, :], 0), axis=1
    )
    my_owners = lax.dynamic_index_in_dim(owner_all, me, 0, keepdims=False)
    rel = jnp.sum(
        jnp.where(my_owners[:, None] == back(me, order)[None, :], order[None, :], 0), axis=1
    )

    valid = me >= 0

    def send(block, d, where):
        return lax.ppermute(block, "grp", [(i, where(i, d)) for i in range(groups)])

    def send_all(blocks, where):
        return [send(block, d, where) for d, block in enumerate(blocks, 1)]

    core = lax.axis_index("tp") % 2
    halves = jnp.stack([1 - core, core])
    steps = chip_steps(parts)
    sent = jnp.bfloat16 if len(steps) <= 2 else jnp.float32
    picked_b = pick_factors(slots, factor_b, range(1, groups))
    got_b = send_all(picked_b, to)
    own_factor_a, *picked_a = pick_factors(slots, factor_a, range(groups))
    near_a = send(picked_a[-1], groups - 1, to)
    *cot, own_factor_b = hold(halves, cotangent, slots, factor_b)
    picked_a, got_b, cot = lax.optimization_barrier((picked_a[:-1], got_b, cot))
    far_a = send_all(picked_a, to)

    def first_grad_sums(rel, halves, cot, inputs, *blocks):
        give, held = give_rows(rel, halves, cot[0], blocks, True)
        got = from_other_core(parts, give)
        sums, out = chip_sums(keep_rows(rel, halves, cot[1], held, True), got, sent)
        tok = None
        for step in steps[:-1]:
            crossed = cross(parts, out, step)
            if tok is None:
                crossed, tok = lax.optimization_barrier((crossed, hold(halves, inputs)))
            sums, out = add_parts(sums, crossed, sent)
        return sums, out, tok

    sums, out, tok = apart(
        valid, first_grad_sums, rel, halves, cot, inputs, own_factor_b, *got_b
    )
    crossed = cross(parts, out, steps[-1])
    give, held = give_rows(rel, halves, tok[0], [own_factor_a, *far_a, near_a], False)
    got = from_other_core(parts, give)
    kept = keep_rows(rel, halves, tok[1], held, False)
    crossed, kept = lax.optimization_barrier((crossed, kept))
    low = join_parts(sums, crossed)
    other_low = from_other_core(parts, low)
    first = group_grads(rel, halves, (1,), [low], tok[1:], groups, finish=False)
    own_a, *grads_a = group_grads(
        rel, halves, (0,), [other_low], tok[:1], groups, True, so_far=first
    )
    back_a = send_all(grads_a, back)
    sums, out = chip_sums(kept, got, sent)
    sums, out, own_a = lax.optimization_barrier((sums, out, own_a))

    def input_grads(rel, halves, cotangent, sums, out):
        crossed = cross(parts, out, steps[0])
        crossed, rows = lax.optimization_barrier((crossed, hold(halves, cotangent)))
        for step in steps[1:]:
            sums, out = add_parts(sums, crossed, sent)
            crossed = cross(parts, out, step)
        low = join_parts(sums, crossed)
        other_low = from_other_core(parts, low)
        first = group_grads(rel, halves, (1,), [low], rows[1:], groups, finish=False)
        return group_grads(rel, halves, (0,), [other_low], rows[:1], groups, so_far=first)

    own_b, *grads_b = apart(valid, input_grads, rel, halves, cotangent, sums, out)
    grads_b, back_a = lax.optimization_barrier((grads_b, back_a))
    back_b = send_all(grads_b, back)
    grad_a = slot_totals(slots, [own_a, *back_a], owned)
    late = min(2, groups - 1)
    early = [own_b, *back_b[: late - 1], *back_b[late:]]
    totals, partial = early_totals(slots, early, late, owned)
    grad_b = late_totals(slots, totals, partial, back_b[late - 1], late)
    return grad_a, grad_b


def solution(mesh):
    return jax.shard_map(
        functools.partial(body, mesh.shape["grp"], mesh.shape["tp"]),
        mesh=mesh,
        in_specs=(
            P("grp", "tp"),
            P("grp", "tp"),
            P("grp", "tp", None),
            P("grp", None, "tp"),
            P(),
            P(),
        ),
        out_specs=(P("grp", "tp", None), P("grp", None, "tp")),
        check_vma=False,
    )
```
